128 devices in a mesh: tm: 32 (over x, y, core), seq: 4 (over z).
Axes of the slice: x: 4, y: 4, z: 4, core: 2. Of those that a mesh axis runs over, the one named last changes fastest.
Arguments:
- latents: bfloat16 [128, 16, 2048], P('tm', None, 'seq'), may hold values from -6 to 6
- hidden: bfloat16 [65536, 3072], P(('tm', 'seq')), may hold values from -6 to 6
- grad_out: bfloat16 [128, 512, 2048], P('tm', None, 'seq'), may hold values from -6 to 6
- conv_in_w: bfloat16 [3, 512, 16], replicated, may hold values from -0.875 to 0.875
- conv_in_b: float32 [512], replicated, may hold values from -4 to 4
- conv_w: bfloat16 [3, 512, 512], replicated, may hold values from -0.15625 to 0.15625
- final_w: bfloat16 [3072, 64], replicated, may hold values from -0.109375 to 0.109375
- modulation: float32 [2, 3072], replicated, may hold values from -3 to 3
- clip_start: int32 [128], replicated, may hold values from 0 to 127, as said below
Outputs:
- hidden_input_gradient: bfloat16 [65536, 3072], P(('tm', 'seq'))
- convolution_weight_gradient: float32 [512, 3, 512], P(('tm', 'seq'))
- input_convolution_gradient: float32 [3, 512, 16], replicated
- input_bias_gradient: float32 [512], replicated
- final_grad: float32 [3072, 64], replicated
- modulation_grad: float32 [2, 3072], replicated
The draws below stay inside these ranges and needn't reach their ends.
Inputs may be any that keep to these rules, and one draw needn't show every extreme that they name: Clips are consecutive runs of frames: clip_start never falls, clip_start[t] <= t, clip_start[t] == t at each clip's first frame; every clip has 9 to 33 frames except the last two, which are cut by the bin's end; the bin's last frame begins a clip of its own.
All inputs are finite; a program needn't handle non-finite values.
Results may differ from the reference program's by a relative error of at most 0.012.
Values may be sent and summed in bfloat16 or wider, within the bound.
No kernel may reach another device: no remote copies, remote signals or barrier semaphores. Data moves between devices by JAX's collectives and lax.ppermute only.
A program may use at most 128 MiB of HBM per device.

```python
import jax
import jax.numpy as jnp
from jax import lax

C = 512
CL = 16
D = 3072
PATCH_EDGE = 4
TAPS = 3
CLIP_MIN = 9
CLIP_MAX = 33
PIX = 2048
FRAMES = 128
TOKENS = 65536
N_TM = 32
N_SEQ = 4


def draw_clip_start(key, part):
    clip_count = FRAMES // CLIP_MIN + 1
    lengths = jax.random.randint(jax.random.fold_in(key, 17), (clip_count,), CLIP_MIN, CLIP_MAX + 1).astype(jnp.int32)
    clip_ends = jnp.cumsum(lengths).astype(jnp.int32)
    clip_first = clip_ends - lengths
    frame_order = jnp.arange(FRAMES, dtype=jnp.int32)
    owner_clip = jnp.sum((clip_ends[None, :] <= frame_order[:, None]).astype(jnp.int32), axis=1)
    clip_index = jnp.arange(clip_count, dtype=jnp.int32)
    picked = jnp.where(clip_index[None, :] == owner_clip[:, None], clip_first[None, :], 0)
    starts = jnp.sum(picked, axis=1).astype(jnp.int32)
    return jnp.where(frame_order == FRAMES - 1, frame_order, starts).astype(jnp.int32)


def strengthened(drawn, rng, source, target, shards_of, factor):
    owner, partner = [(jnp.arange(drawn.shape[dim]) // (drawn.shape[dim] // shards_of)).reshape([-1 if axis == dim else 1 for axis in range(drawn.ndim)]) for dim in (source, target)]
    chosen = jax.random.permutation(rng, shards_of)[partner]
    strong = (owner == chosen) | (owner == (partner + shards_of // 2) % shards_of)
    return jnp.where(strong, factor * drawn, drawn)


def shard_levels(own_key, extent, split, low, high):
    level = 1.0
    for dim, shards_of in split:
        heights = jax.random.uniform(jax.random.fold_in(jax.random.fold_in(own_key, 6), dim), (shards_of,), jnp.float32, low / len(split), high / len(split))
        level = level * jnp.repeat(jnp.exp(heights), extent[dim] // shards_of).reshape((-1,) + (1,) * (len(extent) - 1 - dim))
    return level


def scatter_about(own_key, shape, width, reach, pieces=(), held_as=jnp.bfloat16):
    values = jax.random.normal(own_key, shape, jnp.float32) * width
    if len(pieces) > 0:
        values = shard_levels(own_key, shape, pieces, -0.22, 0.18) * values
    return jnp.clip(values, min=-reach, max=reach).astype(held_as)


def noise_with(stream_key, dims, scale, most, pieces, heavy, kind=jnp.bfloat16):
    values = scale * jax.random.normal(stream_key, dims, jnp.float32)
    if pieces:
        values = values * shard_levels(stream_key, dims, pieces, -0.22, 0.18)
    return jnp.clip(strengthened(values, jax.random.fold_in(stream_key, 3), *heavy), -most, most).astype(kind)


def setup_inputs(seed: int = 0) -> dict:
    keys = jax.random.split(jax.random.key(seed), 10)
    latents = scatter_about(keys[0], (FRAMES, CL, PIX), 1.0, 6.0, ((0, 32), (2, 4)))
    hidden = scatter_about(keys[1], (TOKENS, D), 1.0, 6.0, ((0, 128),))
    grad_out = noise_with(keys[2], (FRAMES, C, PIX), 1.0, 6.0, ((0, 32), (2, 4)), (0, 1, 32, 2.75))
    conv_in_w = scatter_about(keys[3], (TAPS, C, CL), (TAPS * CL) ** -0.5, 0.875)
    conv_in_b = scatter_about(keys[4], (C,), 1.0, 4.0, (), jnp.float32)
    conv_w = scatter_about(keys[5], (TAPS, C, C), (TAPS * C) ** -0.5, 0.15625)
    final_w = scatter_about(keys[6], (D, CL * PATCH_EDGE), D ** -0.5, 0.109375)
    modulation = scatter_about(keys[7], (2, D), 0.5, 3.0, (), jnp.float32)
    clip_start = draw_clip_start(jax.random.fold_in(keys[9], 71), 0)
    return dict(latents=latents, hidden=hidden, grad_out=grad_out, conv_in_w=conv_in_w, conv_in_b=conv_in_b, conv_w=conv_w, final_w=final_w, modulation=modulation, clip_start=clip_start)


def silu_parts(pre_act):
    sigmoid_v = jax.nn.sigmoid(pre_act)
    return (pre_act * sigmoid_v, sigmoid_v * (1.0 + pre_act * (1.0 - sigmoid_v)))

def reference(latents, hidden, grad_out, conv_in_w, conv_in_b, conv_w, final_w, modulation, clip_start):
    frames = latents.shape[0]
    chans = grad_out.shape[1]
    latent_channels = latents.shape[1]
    frame_order = jnp.arange(frames, dtype=jnp.int32)
    source = [jnp.maximum(frame_order - offset, clip_start).astype(jnp.int32) for offset in range(TAPS)]
    blocks = N_SEQ
    block_width = PIX // blocks

    def to_blocks(array):
        return array.reshape(array.shape[0], array.shape[1], blocks, block_width).transpose(2, 0, 1, 3)
    w_in = conv_in_w.astype(jnp.float32)
    w_mid = conv_w.astype(jnp.float32)

    def decode_block(running_totals, piece_list):
        lat_block, grad_block = piece_list
        lat_f = lat_block.astype(jnp.float32)
        grad_f = grad_block.astype(jnp.float32)
        pre_act = conv_in_b[None, :, None] + sum((jnp.einsum('oc,tcp->top', w_in[offset], lat_f[source[offset]]) for offset in range(TAPS)))
        activation, silu_slope = silu_parts(pre_act)
        act_low = lax.optimization_barrier(activation.astype(jnp.bfloat16))
        act_f = act_low.astype(jnp.float32)
        grad_act = sum((jnp.zeros((frames, chans, block_width), jnp.float32).at[source[offset]].add(jnp.einsum('oi,top->tip', w_mid[offset], grad_f)) for offset in range(TAPS)))
        grad_pre = lax.optimization_barrier((grad_act * silu_slope).astype(jnp.bfloat16))
        pre_f = grad_pre.astype(jnp.float32)
        lat_grad = sum((jnp.zeros((frames, latent_channels, block_width), jnp.float32).at[source[offset]].add(jnp.einsum('oc,top->tcp', w_in[offset], pre_f)) for offset in range(TAPS)))
        conv_term = jnp.stack([jnp.einsum('top,tip->oi', grad_f, act_f[source[offset]]) for offset in range(TAPS)], axis=1)
        in_term = jnp.stack([jnp.einsum('top,tcp->oc', pre_f, lat_f[source[offset]]) for offset in range(TAPS)], axis=0)
        bias_term = lax.optimization_barrier(jnp.sum(pre_f, axis=(0, 2)))
        new_totals = (running_totals[0] + conv_term, running_totals[1] + in_term, running_totals[2] + bias_term)
        return (new_totals, lat_grad.astype(jnp.bfloat16))
    start_totals = (jnp.zeros((chans, TAPS, chans), jnp.float32), jnp.zeros((TAPS, chans, latent_channels), jnp.float32), jnp.zeros((chans,), jnp.float32))
    running_totals, grad_blocks = lax.scan(decode_block, start_totals, (to_blocks(latents), to_blocks(grad_out)))
    convolution_weight_gradient, input_convolution_gradient, input_bias_gradient = running_totals
    latent_grad = grad_blocks.transpose(1, 2, 0, 3).reshape(frames, latent_channels, PIX)
    token_gradient = latent_grad.reshape(frames, latent_channels, PIX // PATCH_EDGE, PATCH_EDGE).transpose(0, 2, 1, 3).reshape(frames * (PIX // PATCH_EDGE), latent_channels * PATCH_EDGE)
    group_list = N_TM * N_SEQ
    rows_per_block = hidden.shape[0] // group_list
    shift_vec = modulation[0]
    scale_vec = modulation[1]

    def transformer_block(running_totals, piece_list):
        hid_block, grad_block = piece_list
        hid_f = hid_block.astype(jnp.float32)
        center = hid_f - lax.optimization_barrier(jnp.mean(hid_f, axis=1, keepdims=True))
        variance = lax.optimization_barrier(jnp.mean(center * center, axis=1, keepdims=True))
        inv_std = lax.rsqrt(variance + 1e-06)
        normed = center * inv_std
        modulated = (normed * (1.0 + scale_vec) + shift_vec).astype(jnp.bfloat16)
        final_term = jnp.dot(modulated.T, grad_block, preferred_element_type=jnp.float32)
        mod_in = jnp.dot(grad_block, final_w.T, preferred_element_type=jnp.float32)
        mod_term = jnp.stack([lax.optimization_barrier(jnp.sum(mod_in, axis=0)), lax.optimization_barrier(jnp.sum(mod_in * normed, axis=0))])
        norm_grad = mod_in * (1.0 + scale_vec)
        hid_grad = inv_std * (norm_grad - lax.optimization_barrier(jnp.mean(norm_grad, axis=1, keepdims=True)) - normed * lax.optimization_barrier(jnp.mean(norm_grad * normed, axis=1, keepdims=True)))
        return ((running_totals[0] + final_term, running_totals[1] + mod_term), hid_grad.astype(jnp.bfloat16))
    transformer_start = (jnp.zeros((hidden.shape[1], latent_channels * PATCH_EDGE), jnp.float32), jnp.zeros((2, hidden.shape[1]), jnp.float32))
    transformer_totals, hidden_blocks = lax.scan(transformer_block, transformer_start, (hidden.reshape(group_list, rows_per_block, hidden.shape[1]), token_gradient.reshape(group_list, rows_per_block, latent_channels * PATCH_EDGE)))
    hidden_input_gradient = hidden_blocks.reshape(hidden.shape[0], hidden.shape[1])
    return (hidden_input_gradient, convolution_weight_gradient, input_convolution_gradient, input_bias_gradient, transformer_totals[0], transformer_totals[1])
```

```python
import jax
import jax.numpy as jnp
from jax import lax
from jax.experimental import pallas as pl
from jax.experimental.pallas import tpu as pltpu
from jax.sharding import PartitionSpec as P

BF = jnp.bfloat16
F32 = jnp.float32
VMEM = pl.BlockSpec(memory_space=pltpu.VMEM)
SMEM = pl.BlockSpec(memory_space=pltpu.SMEM)
EDGE = 4
TAPS = 3
SLAB = 4
CL = 16
C = 512
PX = 512
D = 3072
E = 64
NTOK = 512
FRAMES = 128
BOTH = ("tm", "seq")


def params(mib):
    return pltpu.CompilerParams(vmem_limit_bytes=mib * 1024 * 1024)


def cost(flops, nbytes, trans=0):
    return pl.CostEstimate(flops=flops, bytes_accessed=nbytes, transcendentals=trans)


def mm(a, b, ca, cb):
    return lax.dot_general(a, b, (((ca,), (cb,)), ((), ())), preferred_element_type=F32)


def clip_rel(clip_ref, first, frame):
    whole = first + frame
    start = clip_ref[jnp.clip(whole, 0, FRAMES - 1)]
    return jnp.where(whole >= FRAMES, frame, start - first)


def source(clip_ref, first, frame, tap):
    return jnp.maximum(frame - tap, clip_rel(clip_ref, first, frame))


def k_prep(hidden_ref, conv_w_ref, normed_ref, conv_t_ref):
    gain = 1.0 / D

    def rows(i, _):
        at = pl.ds(pl.multiple_of(i * 64, 64), 64)
        h = hidden_ref[at, :].astype(F32)
        center = h - jnp.sum(h, axis=1, keepdims=True) * gain
        var = jnp.sum(center * center, axis=1, keepdims=True) * gain
        normed_ref[at, :] = (center * lax.rsqrt(var + 1e-06)).astype(BF)
        return 0

    lax.fori_loop(0, NTOK // 64, rows, 0)
    for k in range(TAPS):
        conv_t_ref[k] = conv_w_ref[k].T


def load_taps(clip_ref, first, lat_ref, z_ref, slot, frame, base):
    for k in range(TAPS):
        src = jnp.clip(source(clip_ref, first, frame, k) + base, 0, lat_ref.shape[0] - 1)
        z_ref[slot, k * CL : (k + 1) * CL, :] = lat_ref[src]


def k_first(
    clip_ref, prev_ref, lat_ref, win_ref, bias_ref, grad_ref, conv_t_ref,
    act_ref, slope_ref, acc_out_ref, part_ref, halo_ref, icg_ref,
    all_ref, z_ref, wcat_ref, acc_ref, sl_ref, lacc_ref, icg_acc,
):
    first = lax.axis_index("tm") * SLAB
    all_ref[:SLAB] = prev_ref[...]
    all_ref[SLAB:] = lat_ref[...]
    for k in range(TAPS):
        wcat_ref[k * CL : (k + 1) * CL, :] = win_ref[k]
    bias = bias_ref[...]
    high = bias.astype(BF)
    rest = bias - high.astype(F32)
    mid = rest.astype(BF)
    low = (rest - mid.astype(F32)).astype(BF)
    row = lax.broadcasted_iota(jnp.int32, (CL, C), 0)
    tail = jnp.where(row == 0, high.astype(F32), 0.0)
    tail = jnp.where(row == 1, mid.astype(F32), tail)
    tail = jnp.where(row == 2, low.astype(F32), tail)
    wcat_ref[TAPS * CL :, :] = tail.astype(BF)
    wcol = wcat_ref[...].T
    acc_ref[...] = jnp.zeros_like(acc_ref)
    lacc_ref[...] = jnp.zeros_like(lacc_ref)
    icg_acc[...] = jnp.zeros_like(icg_acc)

    def pre_step(j, _):
        load_taps(clip_ref, first, all_ref, z_ref, j, j - 2, SLAB)
        z_ref[j, TAPS * CL :, :] = jnp.ones((CL, PX), BF)
        pre = mm(wcol, z_ref[j], 1, 0)
        sig = 0.5 * jnp.tanh(0.5 * pre) + 0.5
        act_ref[j] = (pre * sig).astype(BF)
        sl_ref[j] = sig * (1.0 + pre * (1.0 - sig))
        return 0

    lax.fori_loop(0, SLAB + 2, pre_step, 0)

    def act_step(t, _):
        for k in range(TAPS):
            src = source(clip_ref, first, t, k)
            src = jnp.where(src < 0, SLAB, src)
            acc_ref[src] += mm(conv_t_ref[k], grad_ref[t], 1, 0)
        return 0

    lax.fori_loop(0, SLAB, act_step, 0)

    def pre_grad(t, _):
        gp = (acc_ref[t] * sl_ref[t + 2]).astype(BF)
        back = mm(wcat_ref[...], gp, 1, 0)
        for k in range(TAPS):
            src = source(clip_ref, first, t, k) + 2
            lacc_ref[src] += back[k * CL : (k + 1) * CL]
        icg_acc[...] += mm(z_ref[t + 2], gp, 1, 1)
        return 0

    lax.fori_loop(0, 2, pre_grad, 0)
    halo_ref[...] = lacc_ref[:2]
    part_ref[...] = lacc_ref[2:]
    icg_ref[...] = icg_acc[...]
    slope_ref[...] = sl_ref[SLAB:]
    acc_out_ref[...] = acc_ref[2:SLAB]


def k_weight(clip_ref, grad_ref, act_ref, out_ref, acc_ref):
    first = lax.axis_index("tm") * SLAB
    acc_ref[...] = jnp.zeros_like(acc_ref)

    def step(t, _):
        for k in range(TAPS):
            src = jnp.maximum(source(clip_ref, first, t, k), -2) + 2
            acc_ref[:, k * C : (k + 1) * C] += mm(grad_ref[t], act_ref[src], 1, 1)
        return 0

    lax.fori_loop(0, SLAB, step, 0)
    upper = lax.broadcasted_iota(jnp.int32, (64, 8, 128), 1) < 4
    for jj in range(0, TAPS * C // 128, 4):
        even, odd = [], []
        for h in range(2):
            at = (jj + 2 * h) * 128
            a = acc_ref[:, at : at + 128].reshape(64, 8, 128)
            b = acc_ref[:, at + 128 : at + 256].reshape(64, 8, 128)
            even.append(jnp.where(upper, a, pltpu.roll(b, 4, 1)))
            odd.append(jnp.where(upper, pltpu.roll(a, 4, 1), b))
        out_ref[:, 0, jj * 4 : jj * 4 + 16, :] = jnp.concatenate(even, axis=1).astype(BF)
        out_ref[:, 1, jj * 4 : jj * 4 + 16, :] = jnp.concatenate(odd, axis=1).astype(BF)


def k_second(
    clip_ref, next_ref, lat_ref, win_ref, conv_t_ref, acc_in_ref, slope_ref, part_ref, halo_ref, icg_in_ref,
    tok_ref, icg_ref, acc_ref, z_ref, wcat_ref, lacc_ref, icg_acc, low_ref,
):
    first = lax.axis_index("tm") * SLAB
    acc_ref[:2] = acc_in_ref[...]
    for k in range(TAPS):
        wcat_ref[k * CL : (k + 1) * CL, :] = win_ref[k]
    for t, k in ((0, 1), (0, 2), (1, 2)):
        src = source(clip_ref, first, SLAB + t, k) - 2
        acc_ref[jnp.minimum(src, 2)] += mm(conv_t_ref[k], next_ref[t], 1, 0)
    lacc_ref[...] = jnp.zeros_like(lacc_ref)
    lacc_ref[:SLAB] = part_ref[...]
    lacc_ref[2:SLAB] += halo_ref[...]
    icg = icg_in_ref[...]
    for t in range(2):
        gp = (acc_ref[t] * slope_ref[t]).astype(BF)
        load_taps(clip_ref, first, lat_ref, z_ref, t, t + 2, 0)
        z_ref[t, TAPS * CL :, :] = jnp.ones((CL, PX), BF)
        back = mm(wcat_ref[...], gp, 1, 0)
        for k in range(TAPS):
            src = source(clip_ref, first, t + 2, k)
            lacc_ref[src] += back[k * CL : (k + 1) * CL]
        icg = icg + mm(z_ref[t], gp, 1, 1)
    icg_acc[...] = icg
    for f in range(SLAB):
        low_ref[f * CL : (f + 1) * CL, :] = lacc_ref[f].astype(BF)
    r = lax.broadcasted_iota(jnp.int32, (PX, PX), 0)
    c = lax.broadcasted_iota(jnp.int32, (PX, PX), 1)
    pick = (((r & 3) << 7) + (r >> 2) == c).astype(F32).astype(BF)
    tok_ref[...] = mm(low_ref[...], pick, 1, 0).astype(BF)
    for rb in range(4):
        for lb in range(4):
            icg_ref[rb * 4 + lb] = icg_acc[rb * 16 : (rb + 1) * 16, lb * 128 : (lb + 1) * 128].astype(BF)


def k_grad(recv_ref, normed_ref, icg_ref, pack_ref, tok_ref, raw_ref, g_ref):
    for s in range(4):
        for q in range(EDGE):
            raw_ref[q * CL : (q + 1) * CL, s * 128 : (s + 1) * 128] = recv_ref[
                s, :, q * 128 : (q + 1) * 128
            ]
    r = lax.broadcasted_iota(jnp.int32, (E, E), 0)
    c = lax.broadcasted_iota(jnp.int32, (E, E), 1)
    order = (((r & 3) << 4) + (r >> 2) == c).astype(F32).astype(BF)
    tok = mm(order, raw_ref[...], 1, 0)
    tok_ref[...] = tok.astype(BF)
    total = jnp.broadcast_to(jnp.sum(tok, axis=1, keepdims=True), (E, 128)).astype(BF)
    for lb in range(D // 512):
        g = mm(tok_ref[...], normed_ref[:, lb * 512 : (lb + 1) * 512], 1, 0).astype(BF)
        for u in range(4):
            for rb in range(4):
                pack_ref[rb * 24 + lb * 4 + u] = g[rb * 16 : (rb + 1) * 16, u * 128 : (u + 1) * 128]
    pack_ref[96:112] = icg_ref[...]
    for rb in range(4):
        pack_ref[112 + rb] = total[rb * 16 : (rb + 1) * 16]
    pack_ref[116:] = jnp.zeros((12, 16, 128), BF)


def k_hidden(tok_ref, hidden_ref, wt_ref, mod_ref, out_ref):
    gain = 1.0 / D
    h = hidden_ref[...].astype(F32)
    center = h - jnp.sum(h, axis=1, keepdims=True) * gain
    var = jnp.sum(center * center, axis=1, keepdims=True) * gain
    inv = lax.rsqrt(var + 1e-06)
    normed = center * inv
    mod_in = mm(tok_ref[...].T, wt_ref[...], 1, 0)
    ng = mod_in * (1.0 + mod_ref[1:2, :])
    m1 = jnp.sum(ng, axis=1, keepdims=True) * gain
    m2 = jnp.sum(ng * normed, axis=1, keepdims=True) * gain
    out_ref[...] = (inv * (ng - m1 - normed * m2)).astype(BF)


def k_sum(recv_ref, out_ref):
    total = jnp.sum(recv_ref[...].astype(F32), axis=0).astype(BF)
    out_ref[...] = jnp.broadcast_to(total[None], out_ref.shape)


def k_last(all_ref, wt_ref, mod_ref, final_ref, modg_ref, icg_ref, bias_ref):
    tot = [all_ref[112 + rb].astype(F32) for rb in range(4)]
    for lb in range(D // 128):
        at = slice(lb * 128, (lb + 1) * 128)
        scale = 1.0 + mod_ref[1:2, at]
        shift = mod_ref[0:1, at]
        s0 = jnp.zeros((1, 128), F32)
        s1 = jnp.zeros((1, 128), F32)
        for rb in range(4):
            rows = slice(rb * 16, (rb + 1) * 16)
            g = all_ref[rb * 24 + lb].astype(F32)
            w = wt_ref[rows, at].astype(F32)
            final_ref[rows, at] = g * scale + shift * tot[rb]
            s0 = s0 + jnp.sum(w * tot[rb], axis=0, keepdims=True)
            s1 = s1 + jnp.sum(w * g, axis=0, keepdims=True)
        modg_ref[0:1, at] = s0
        modg_ref[1:2, at] = s1
    for rb in range(3):
        for lb in range(4):
            icg_ref[rb * 16 : (rb + 1) * 16, lb * 128 : (lb + 1) * 128] = all_ref[96 + rb * 4 + lb].astype(F32)
    for lb in range(4):
        bias_ref[:, lb * 128 : (lb + 1) * 128] = all_ref[96 + 12 + lb].astype(F32)[0:1]


def k_weight_sum(recv_ref, out_ref):
    total = jnp.sum(recv_ref[...].astype(F32), axis=0)
    for k in range(TAPS):
        for u in range(4):
            j = k * 4 + u
            out_ref[k, :, u * 128 : (u + 1) * 128] = total[j * 4 : (j + 1) * 4]


def call(fn, outs, specs, scratch=(), mib=40, est=None, name=None):
    return pl.pallas_call(
        fn,
        out_shape=outs,
        in_specs=specs,
        out_specs=jax.tree.map(lambda _: VMEM, outs),
        scratch_shapes=list(scratch),
        compiler_params=params(mib),
        cost_estimate=est,
        name=name,
    )


def sds(shape, dtype):
    return jax.ShapeDtypeStruct(shape, dtype)


def shifted(block, distance):
    n = lax.axis_size("tm")
    route = [(i - distance, i) for i in range(n) if 0 <= i - distance < n]
    return lax.ppermute(block, "tm", route)


def exchange(block, axes):
    return lax.all_to_all(block, axes, split_axis=0, concat_axis=0, tiled=True)


def local(latents, hidden, grad_out, conv_in_w, conv_in_b, conv_w, final_w, modulation, clip_start):
    win = conv_in_w.transpose(0, 2, 1)
    wt = final_w.T
    bias = conv_in_b.reshape(1, C)
    grad_next = shifted(grad_out[:2], -1)
    lat_prev = shifted(latents, 1)
    unit = 2 * C * C * PX
    normed, conv_t = call(
        k_prep, (sds((NTOK, D), BF), sds((TAPS, C, C), BF)), [VMEM] * 2,
        est=cost(10 * NTOK * D, 10 << 20), name="prep",
    )(hidden, conv_w)
    act, slope, acc, part, halo, icg_part = call(
        k_first,
        (
            sds((SLAB + 2, C, PX), BF), sds((2, C, PX), F32), sds((2, C, PX), F32),
            sds((SLAB, CL, PX), F32), sds((2, CL, PX), F32), sds((E, C), F32),
        ),
        [SMEM] + [VMEM] * 6,
        [
            pltpu.VMEM((2 * SLAB, CL, PX), BF), pltpu.VMEM((SLAB + 2, E, PX), BF), pltpu.VMEM((E, C), BF),
            pltpu.VMEM((SLAB + 1, C, PX), F32), pltpu.VMEM((SLAB + 2, C, PX), F32),
            pltpu.VMEM((SLAB + 2, CL, PX), F32), pltpu.VMEM((E, C), F32),
        ],
        est=cost(16 * unit, 10 << 20), name="first",
    )(clip_start, lat_prev, latents, win, bias, grad_out, conv_t)
    halo_recv = shifted(halo, -1)
    weight_pack = call(
        k_weight, sds((64, 2, 48, 128), BF), [SMEM] + [VMEM] * 2,
        [pltpu.VMEM((C, TAPS * C), F32)], est=cost(12 * unit, 7 << 20), name="weight",
    )(clip_start, grad_out, act)
    tok_part, icg_blocks = call(
        k_second, (sds((SLAB * CL, PX), BF), sds((16, 16, 128), BF)), [SMEM] + [VMEM] * 9,
        [
            pltpu.VMEM((3, C, PX), F32), pltpu.VMEM((2, E, PX), BF), pltpu.VMEM((TAPS * CL, C), BF),
            pltpu.VMEM((SLAB, CL, PX), F32), pltpu.VMEM((E, C), F32), pltpu.VMEM((SLAB * CL, PX), BF),
        ],
        est=cost(6 * unit, 8 << 20), name="second",
    )(clip_start, grad_next, latents, win, conv_t, acc, slope, part, halo_recv, icg_part)
    tok_recv = exchange(tok_part, "seq").reshape(4, CL, PX)
    pack, tok = call(
        k_grad, (sds((128, 16, 128), BF), sds((E, NTOK), BF)), [VMEM] * 3,
        [pltpu.VMEM((E, NTOK), BF), pltpu.VMEM((E, D), F32)],
        est=cost(2 * NTOK * D * E, 5 << 20), name="grad",
    )(tok_recv, normed, icg_blocks)
    recv = exchange(pack, BOTH)
    hidden_grad = pl.pallas_call(
        k_hidden,
        grid=(4,),
        out_shape=sds((NTOK, D), BF),
        in_specs=[
            pl.BlockSpec((E, 128), lambda i: (0, i)),
            pl.BlockSpec((128, D), lambda i: (i, 0)),
            pl.BlockSpec((E, D), lambda i: (0, 0)),
            pl.BlockSpec((2, D), lambda i: (0, 0)),
        ],
        out_specs=pl.BlockSpec((128, D), lambda i: (i, 0)),
        compiler_params=params(40),
        cost_estimate=cost(2 * NTOK * D * E, 6 << 20),
        name="hidden",
    )(tok, hidden, wt, modulation)
    weight_recv = exchange(weight_pack.reshape(128, 48, 128), BOTH)
    copies = call(k_sum, sds((128, 16, 128), BF), [VMEM], est=cost(1 << 18, 1 << 20), name="sum")(recv)
    everything = exchange(copies, BOTH)
    weight_grad = call(
        k_weight_sum, sds((TAPS, 4, C), F32), [VMEM], est=cost(1 << 20, 1536 << 10), name="weight_sum"
    )(weight_recv)
    final_t, mod_grad, icg, bias_grad = call(
        k_last, (sds((E, D), F32), sds((2, D), F32), sds((TAPS * CL, C), F32), sds((1, C), F32)), [VMEM] * 3,
        est=cost(1 << 20, 2 << 20), name="last",
    )(everything, wt, modulation)
    return (
        hidden_grad,
        weight_grad.transpose(1, 0, 2),
        icg.reshape(TAPS, CL, C).transpose(0, 2, 1),
        bias_grad.reshape(C),
        final_t.T,
        mod_grad,
    )


def solution(mesh):
    return jax.shard_map(
        local,
        mesh=mesh,
        in_specs=(
            P("tm", None, "seq"),
            P(("tm", "seq"), None),
            P("tm", None, "seq"),
            P(), P(), P(), P(), P(), P(),
        ),
        out_specs=(P(("tm", "seq"), None), P(("tm", "seq"), None, None), P(), P(), P(), P()),
        check_vma=False,
    )
```

```python
import jax
import jax.numpy as jnp
from jax import lax
from jax.experimental import pallas as pl
from jax.experimental.pallas import tpu as pltpu
from jax.sharding import PartitionSpec as P

BF = jnp.bfloat16
F32 = jnp.float32
VMEM = pl.BlockSpec(memory_space=pltpu.VMEM)
SMEM = pl.BlockSpec(memory_space=pltpu.SMEM)
HERE = pl.BlockSpec(memory_space=pl.ANY)
EDGE = 4
TAPS = 3
SLAB = 4
CL = 16
C = 512
PX = 512
D = 3072
E = 64
NTOK = 512
FRAMES = 128
BOTH = ("tm", "seq")


def params(mib):
    return pltpu.CompilerParams(vmem_limit_bytes=mib * 1024 * 1024)


def cost(flops, nbytes, trans=0):
    return pl.CostEstimate(flops=flops, bytes_accessed=nbytes, transcendentals=trans)


def mm(a, b, ca, cb):
    return lax.dot_general(a, b, (((ca,), (cb,)), ((), ())), preferred_element_type=F32)


def clip_rel(clip_ref, first, frame):
    whole = first + frame
    start = clip_ref[jnp.clip(whole, 0, FRAMES - 1)]
    return jnp.where(whole >= FRAMES, frame, start - first)


def source(clip_ref, first, frame, tap):
    return jnp.maximum(frame - tap, clip_rel(clip_ref, first, frame))


def k_prep(hidden_ref, after_ref, normed_ref):
    gain = 1.0 / D

    def rows(i, _):
        at = pl.ds(pl.multiple_of(i * 64, 64), 64)
        h = hidden_ref[at, :].astype(F32)
        center = h - jnp.sum(h, axis=1, keepdims=True) * gain
        var = jnp.sum(center * center, axis=1, keepdims=True) * gain
        normed_ref[at, :] = (center * lax.rsqrt(var + 1e-06)).astype(BF)
        return 0

    lax.fori_loop(0, NTOK // 64, rows, 0)


def only(keep, value):
    return jnp.where(keep, value, jnp.zeros_like(value))


def k_back(clip_ref, grad_ref, conv_ref, acc_ref):
    first = lax.axis_index("tm") * SLAB
    start = [clip_rel(clip_ref, first, t) for t in range(SLAB)]
    for s in range(SLAB):
        total = mm(conv_ref[0], grad_ref[s], 0, 0)
        for k in range(1, min(TAPS, SLAB - s)):
            total = total + mm(conv_ref[k], only(start[s + k] <= s, grad_ref[s + k]), 0, 0)
        acc_ref[s] = total

    def opens(s, _):
        @pl.when(clip_rel(clip_ref, first, s) == s)
        def _():
            later = jnp.minimum(s + 1, SLAB - 1)
            keep = (s + 1 < SLAB) & (clip_rel(clip_ref, first, s + 1) <= s)
            acc_ref[s] += (
                mm(conv_ref[1], grad_ref[s], 0, 0)
                + mm(conv_ref[2], grad_ref[s], 0, 0)
                + mm(conv_ref[2], only(keep, grad_ref[later]), 0, 0)
            )

        return 0

    lax.fori_loop(0, SLAB, opens, 0)


def load_taps(clip_ref, first, lat_ref, z_ref, slot, frame, base):
    for k in range(TAPS):
        src = jnp.clip(source(clip_ref, first, frame, k) + base, 0, lat_ref.shape[0] - 1)
        z_ref[slot, k * CL : (k + 1) * CL, :] = lat_ref[src]


def k_first(
    clip_ref, prev_ref, lat_ref, win_ref, bias_ref, acc_ref,
    act_ref, slope_ref, part_ref, halo_ref, icg_ref,
    all_ref, z_ref, wcat_ref, sl_ref, lacc_ref,
):
    first = lax.axis_index("tm") * SLAB
    all_ref[:SLAB] = prev_ref[...]
    all_ref[SLAB:] = lat_ref[...]
    for k in range(TAPS):
        wcat_ref[k * CL : (k + 1) * CL, :] = win_ref[k]
    bias = bias_ref[...]
    high = bias.astype(BF)
    rest = bias - high.astype(F32)
    mid = rest.astype(BF)
    low = (rest - mid.astype(F32)).astype(BF)
    row = lax.broadcasted_iota(jnp.int32, (CL, C), 0)
    tail = jnp.where(row == 0, high.astype(F32), 0.0)
    tail = jnp.where(row == 1, mid.astype(F32), tail)
    tail = jnp.where(row == 2, low.astype(F32), tail)
    wcat_ref[TAPS * CL :, :] = tail.astype(BF)
    wcol = wcat_ref[...].T
    lacc_ref[...] = jnp.zeros_like(lacc_ref)

    def pre_of(j):
        load_taps(clip_ref, first, all_ref, z_ref, j, j - 2, SLAB)
        z_ref[j, TAPS * CL :, :] = jnp.ones((CL, PX), BF)
        pre = mm(wcol, z_ref[j], 1, 0)
        sig = 0.5 * jnp.tanh(0.5 * pre) + 0.5
        act_ref[j] = (pre * sig).astype(BF)
        return pre, sig

    def before(j, _):
        pre_of(j)
        return 0

    def own(j, _):
        pre, sig = pre_of(j)
        sl_ref[j - 2] = sig * (1.0 + pre * (1.0 - sig))
        return 0

    lax.fori_loop(0, 2, before, 0)
    lax.fori_loop(2, SLAB + 2, own, 0)
    icg = jnp.zeros((E, C), F32)
    for t in range(2):
        gp = (acc_ref[t] * sl_ref[t]).astype(BF)
        back = mm(wcat_ref[...], gp, 1, 0)
        for k in range(TAPS):
            src = source(clip_ref, first, t, k) + 2
            lacc_ref[src] += back[k * CL : (k + 1) * CL]
        icg = icg + mm(z_ref[t + 2], gp, 1, 1)
    halo_ref[...] = lacc_ref[:2]
    part_ref[...] = lacc_ref[2:]
    icg_ref[...] = icg
    slope_ref[...] = sl_ref[2:]


def k_weight(clip_ref, grad_ref, act_ref, after_ref, keep_ref, send_ref, acc_ref):
    first = lax.axis_index("tm") * SLAB
    core = lax.axis_index("tm") % 2
    for k in range(TAPS):
        total = None
        for t in range(SLAB):
            src = jnp.maximum(source(clip_ref, first, t, k), -2) + 2
            part = mm(grad_ref[t], act_ref[src], 1, 1)
            total = part if total is None else total + part
        acc_ref[:, :, :, k * C : (k + 1) * C] = total.reshape(16, 2, 16, C)
    upper = lax.broadcasted_iota(jnp.int32, (32, 8, 128), 1) < 4
    for ref, half in ((keep_ref, core), (send_ref, 1 - core)):
        for jj in range(0, TAPS * C // 128, 4):
            even, odd = [], []
            for h in range(2):
                at = (jj + 2 * h) * 128
                a = acc_ref[:, half, :, at : at + 128].reshape(32, 8, 128)
                b = acc_ref[:, half, :, at + 128 : at + 256].reshape(32, 8, 128)
                even.append(jnp.where(upper, a, pltpu.roll(b, 4, 1)))
                odd.append(jnp.where(upper, pltpu.roll(a, 4, 1), b))
            ref[:, 0, jj * 4 : jj * 4 + 16, :] = jnp.concatenate(even, axis=1).astype(BF)
            ref[:, 1, jj * 4 : jj * 4 + 16, :] = jnp.concatenate(odd, axis=1).astype(BF)


def k_second(
    clip_ref, next_ref, lat_ref, win_ref, conv_ref, acc_in_ref, slope_ref, part_ref, halo_ref, icg_in_ref, after_ref,
    tok_ref, icg_ref, acc_ref, z_ref, wcat_ref, lacc_ref, icg_acc, low_ref,
):
    first = lax.axis_index("tm") * SLAB
    start = [clip_rel(clip_ref, first, SLAB + t) for t in range(2)]
    for k in range(TAPS):
        wcat_ref[k * CL : (k + 1) * CL, :] = win_ref[k]
    acc_ref[0] = acc_in_ref[2] + mm(conv_ref[2], only(start[0] <= 2, next_ref[0]), 0, 0)
    acc_ref[1] = (
        acc_in_ref[3]
        + mm(conv_ref[1], only(start[0] <= 3, next_ref[0]), 0, 0)
        + mm(conv_ref[2], only(start[1] <= 3, next_ref[1]), 0, 0)
    )

    @pl.when((clip_rel(clip_ref, first, 3) == 3) & (start[0] <= 3))
    def _():
        acc_ref[1] += mm(conv_ref[2], next_ref[0], 0, 0)

    lacc_ref[:SLAB] = part_ref[...]
    lacc_ref[2:SLAB] += halo_ref[...]
    icg = icg_in_ref[...]
    for t in range(2):
        gp = (acc_ref[t] * slope_ref[t]).astype(BF)
        load_taps(clip_ref, first, lat_ref, z_ref, t, t + 2, 0)
        z_ref[t, TAPS * CL :, :] = jnp.ones((CL, PX), BF)
        back = mm(wcat_ref[...], gp, 1, 0)
        for k in range(TAPS):
            src = source(clip_ref, first, t + 2, k)
            lacc_ref[src] += back[k * CL : (k + 1) * CL]
        icg = icg + mm(z_ref[t], gp, 1, 1)
    icg_acc[...] = icg
    for f in range(SLAB):
        low_ref[f * CL : (f + 1) * CL, :] = lacc_ref[f].astype(BF)
    r = lax.broadcasted_iota(jnp.int32, (PX, PX), 0)
    c = lax.broadcasted_iota(jnp.int32, (PX, PX), 1)
    pick = (((r & 3) << 7) + (r >> 2) == c).astype(F32).astype(BF)
    tok_ref[...] = mm(low_ref[...], pick, 1, 0).astype(BF)
    for rb in range(4):
        for lb in range(4):
            icg_ref[rb * 4 + lb] = icg_acc[rb * 16 : (rb + 1) * 16, lb * 128 : (lb + 1) * 128].astype(BF)


def k_grad(recv_ref, normed_ref, icg_ref, keep_ref, other_ref, pack_ref, tok_ref, raw_ref):
    for s in range(4):
        for q in range(EDGE):
            raw_ref[q * CL : (q + 1) * CL, s * 128 : (s + 1) * 128] = recv_ref[
                s, :, q * 128 : (q + 1) * 128
            ]
    r = lax.broadcasted_iota(jnp.int32, (E, E), 0)
    c = lax.broadcasted_iota(jnp.int32, (E, E), 1)
    order = (((r & 3) << 4) + (r >> 2) == c).astype(F32).astype(BF)
    tok = mm(order, raw_ref[...], 1, 0)
    tok_ref[...] = tok.astype(BF)
    total = jnp.broadcast_to(jnp.sum(tok, axis=1, keepdims=True), (E, 128)).astype(BF)
    for lb in range(D // 512):
        g = mm(tok_ref[...], normed_ref[:, lb * 512 : (lb + 1) * 512], 1, 0).astype(BF)
        for u in range(4):
            for rb in range(4):
                pack_ref[rb * 24 + lb * 4 + u, :16, :] = g[rb * 16 : (rb + 1) * 16, u * 128 : (u + 1) * 128]
    pack_ref[96:112, :16, :] = icg_ref[...]
    for rb in range(4):
        pack_ref[112 + rb, :16, :] = total[rb * 16 : (rb + 1) * 16]
    pack_ref[116:, :16, :] = jnp.zeros((12, 16, 128), BF)
    for xy in range(16):
        for half in range(2):
            at = pl.ds((xy * 2 + half) * 4, 4)
            rows = slice(half * 24, half * 24 + 24)
            both = keep_ref[xy * 4 : xy * 4 + 4].astype(F32) + other_ref[xy * 4 : xy * 4 + 4].astype(F32)
            pack_ref[at, 16:, :] = both[:, rows, :].astype(BF)


def k_hidden(tok_ref, hidden_ref, wt_ref, mod_ref, out_ref):
    gain = 1.0 / D
    h = hidden_ref[...].astype(F32)
    center = h - jnp.sum(h, axis=1, keepdims=True) * gain
    var = jnp.sum(center * center, axis=1, keepdims=True) * gain
    inv = lax.rsqrt(var + 1e-06)
    normed = center * inv
    mod_in = mm(tok_ref[...].T, wt_ref[...], 1, 0)
    ng = mod_in * (1.0 + mod_ref[1:2, :])
    m1 = jnp.sum(ng, axis=1, keepdims=True) * gain
    m2 = jnp.sum(ng * normed, axis=1, keepdims=True) * gain
    out_ref[...] = (inv * (ng - m1 - normed * m2)).astype(BF)


def k_sum(recv_ref, out_ref, keep_ref, send_ref):
    core = lax.axis_index("tm") % 2
    total = jnp.sum(recv_ref[:, :16, :].astype(F32), axis=0).astype(BF)
    out_ref[...] = jnp.broadcast_to(total[None], out_ref.shape)
    sums = [jnp.zeros((24, 128), F32)] * 2
    for d in range(128):
        c = (d // 4) % 2
        sums[c] = sums[c] + recv_ref[d, 16:, :].astype(F32)
    keep_ref[...] = jnp.where(core == 0, sums[0], sums[1])
    send_ref[...] = jnp.where(core == 0, sums[1], sums[0])


def k_last(all_ref, wt_ref, mod_ref, final_ref, modg_ref, icg_ref, bias_ref):
    tot = [all_ref[112 + rb].astype(F32) for rb in range(4)]
    for lb in range(D // 128):
        at = slice(lb * 128, (lb + 1) * 128)
        scale = 1.0 + mod_ref[1:2, at]
        shift = mod_ref[0:1, at]
        s0 = jnp.zeros((1, 128), F32)
        s1 = jnp.zeros((1, 128), F32)
        for rb in range(4):
            rows = slice(rb * 16, (rb + 1) * 16)
            g = all_ref[rb * 24 + lb].astype(F32)
            w = wt_ref[rows, at].astype(F32)
            final_ref[rows, at] = g * scale + shift * tot[rb]
            s0 = s0 + jnp.sum(w * tot[rb], axis=0, keepdims=True)
            s1 = s1 + jnp.sum(w * g, axis=0, keepdims=True)
        modg_ref[0:1, at] = s0
        modg_ref[1:2, at] = s1
    for rb in range(3):
        for lb in range(4):
            icg_ref[rb * 16 : (rb + 1) * 16, lb * 128 : (lb + 1) * 128] = all_ref[96 + rb * 4 + lb].astype(F32)
    for lb in range(4):
        bias_ref[:, lb * 128 : (lb + 1) * 128] = all_ref[96 + 12 + lb].astype(F32)[0:1]


def k_weight_out(keep_ref, other_ref, out_ref):
    core = lax.axis_index("tm") % 2
    mine, other = keep_ref[...], other_ref[...]
    halves = [jnp.where(core == 0, mine, other), jnp.where(core == 0, other, mine)]
    for j in range(12):
        rows = halves[j // 6][(j % 6) * 4 : (j % 6) * 4 + 4]
        out_ref[j // 4, :, (j % 4) * 128 : (j % 4 + 1) * 128] = rows


def call(fn, outs, specs, scratch=(), mib=40, est=None, name=None):
    return pl.pallas_call(
        fn,
        out_shape=outs,
        in_specs=specs,
        out_specs=jax.tree.map(lambda _: VMEM, outs),
        scratch_shapes=list(scratch),
        compiler_params=params(mib),
        cost_estimate=est,
        name=name,
    )


def sds(shape, dtype):
    return jax.ShapeDtypeStruct(shape, dtype)


def shifted(block, distance):
    n = lax.axis_size("tm")
    route = [(i - distance, i) for i in range(n) if 0 <= i - distance < n]
    return lax.ppermute(block, "tm", route)


def swapped(block):
    return lax.ppermute(block, "tm", [(i, i ^ 1) for i in range(lax.axis_size("tm"))])


def exchange(block, axes):
    return lax.all_to_all(block, axes, split_axis=0, concat_axis=0, tiled=True)


def local(latents, hidden, grad_out, conv_in_w, conv_in_b, conv_w, final_w, modulation, clip_start):
    win = conv_in_w.transpose(0, 2, 1)
    wt = final_w.T
    bias = conv_in_b.reshape(1, C)
    grad_next = shifted(grad_out[:2], -1)
    lat_prev = shifted(latents, 1)
    unit = 2 * C * C * PX
    acc = call(
        k_back, sds((SLAB, C, PX), F32), [SMEM, VMEM, VMEM], mib=16, est=cost(9 * unit, 8 << 20), name="back"
    )(clip_start, grad_out, conv_w)
    act, slope, part, halo, icg_part = call(
        k_first,
        (
            sds((SLAB + 2, C, PX), BF), sds((2, C, PX), F32),
            sds((SLAB, CL, PX), F32), sds((2, CL, PX), F32), sds((E, C), F32),
        ),
        [SMEM] + [VMEM] * 5,
        [
            pltpu.VMEM((2 * SLAB, CL, PX), BF), pltpu.VMEM((SLAB + 2, E, PX), BF), pltpu.VMEM((E, C), BF),
            pltpu.VMEM((SLAB, C, PX), F32), pltpu.VMEM((SLAB + 2, CL, PX), F32),
        ],
        mib=24, est=cost(4 * unit, 10 << 20), name="first",
    )(clip_start, lat_prev, latents, win, bias, acc)
    halo_recv = shifted(halo, -1)
    normed = call(
        k_prep, sds((NTOK, D), BF), [VMEM, HERE], mib=16, est=cost(10 * NTOK * D, 6 << 20), name="prep"
    )(hidden, halo)
    tok_part, icg_blocks = call(
        k_second, (sds((SLAB * CL, PX), BF), sds((16, 16, 128), BF)), [SMEM] + [VMEM] * 9 + [HERE],
        [
            pltpu.VMEM((2, C, PX), F32), pltpu.VMEM((2, E, PX), BF), pltpu.VMEM((TAPS * CL, C), BF),
            pltpu.VMEM((SLAB, CL, PX), F32), pltpu.VMEM((E, C), F32), pltpu.VMEM((SLAB * CL, PX), BF),
        ],
        mib=16, est=cost(6 * unit, 8 << 20), name="second",
    )(clip_start, grad_next, latents, win, conv_w, acc, slope, part, halo_recv, icg_part, normed)
    tok_recv = exchange(tok_part, "seq").reshape(4, CL, PX)
    keep, send = call(
        k_weight, (sds((32, 2, 48, 128), BF),) * 2, [SMEM] + [VMEM] * 2 + [HERE],
        [pltpu.VMEM((16, 2, 16, TAPS * C), F32)], mib=16, est=cost(12 * unit, 7 << 20), name="weight",
    )(clip_start, grad_out, act, icg_blocks)
    other = swapped(send)
    pack, tok = call(
        k_grad, (sds((128, 40, 128), BF), sds((E, NTOK), BF)), [VMEM] * 5,
        [pltpu.VMEM((E, NTOK), BF)],
        mib=16, est=cost(2 * NTOK * D * E, 5 << 20), name="grad",
    )(tok_recv, normed, icg_blocks, keep.reshape(64, 48, 128), other.reshape(64, 48, 128))
    recv = exchange(pack, BOTH)
    hidden_grad = pl.pallas_call(
        k_hidden,
        grid=(4,),
        out_shape=sds((NTOK, D), BF),
        in_specs=[
            pl.BlockSpec((E, 128), lambda i: (0, i)),
            pl.BlockSpec((128, D), lambda i: (i, 0)),
            pl.BlockSpec((E, D), lambda i: (0, 0)),
            pl.BlockSpec((2, D), lambda i: (0, 0)),
        ],
        out_specs=pl.BlockSpec((128, D), lambda i: (i, 0)),
        compiler_params=params(16),
        cost_estimate=cost(2 * NTOK * D * E, 6 << 20),
        name="hidden",
    )(tok, hidden, wt, modulation)
    copies, own, away = call(
        k_sum, (sds((128, 16, 128), BF), sds((24, 128), F32), sds((24, 128), F32)), [VMEM],
        mib=16, est=cost(1 << 20, 2 << 20), name="sum",
    )(recv)
    everything = exchange(copies, BOTH)
    weight_grad = call(
        k_weight_out, sds((TAPS, 4, C), F32), [VMEM] * 2, mib=16, est=cost(1 << 12, 1 << 16), name="weight_out"
    )(own, swapped(away))
    final_t, mod_grad, icg, bias_grad = call(
        k_last, (sds((E, D), F32), sds((2, D), F32), sds((TAPS * CL, C), F32), sds((1, C), F32)), [VMEM] * 3,
        mib=16, est=cost(1 << 20, 2 << 20), name="last",
    )(everything, wt, modulation)
    return (
        hidden_grad,
        weight_grad.transpose(1, 0, 2),
        icg.reshape(TAPS, CL, C).transpose(0, 2, 1),
        bias_grad.reshape(C),
        final_t.T,
        mod_grad,
    )


def solution(mesh):
    return jax.shard_map(
        local,
        mesh=mesh,
        in_specs=(
            P("tm", None, "seq"),
            P(("tm", "seq"), None),
            P("tm", None, "seq"),
            P(), P(), P(), P(), P(), P(),
        ),
        out_specs=(P(("tm", "seq"), None), P(("tm", "seq"), None, None), P(), P(), P(), P()),
        check_vma=False,
    )
```

```python
import jax
import jax.numpy as jnp
from jax import lax
from jax.experimental import pallas as pl
from jax.experimental.pallas import tpu as pltpu
from jax.sharding import PartitionSpec as P

BF = jnp.bfloat16
F32 = jnp.float32
VMEM = pl.BlockSpec(memory_space=pltpu.VMEM)
SMEM = pl.BlockSpec(memory_space=pltpu.SMEM)
HERE = pl.BlockSpec(memory_space=pl.ANY)
PIN = pl.BlockSpec(memory_space=pltpu.HBM)
EDGE = 4
TAPS = 3
SLAB = 4
CL = 16
C = 512
PX = 512
D = 3072
E = 64
NTOK = 512
FRAMES = 128
BOTH = ("tm", "seq")


def params(mib):
    return pltpu.CompilerParams(vmem_limit_bytes=mib * 1024 * 1024)


def cost(flops, nbytes, trans=0):
    return pl.CostEstimate(flops=flops, bytes_accessed=nbytes, transcendentals=trans)


def mm(a, b, ca, cb):
    return lax.dot_general(a, b, (((ca,), (cb,)), ((), ())), preferred_element_type=F32)


def clip_rel(clip_ref, first, frame):
    whole = first + frame
    start = clip_ref[jnp.clip(whole, 0, FRAMES - 1)]
    return jnp.where(whole >= FRAMES, frame, start - first)


def source(clip_ref, first, frame, tap):
    return jnp.maximum(frame - tap, clip_rel(clip_ref, first, frame))


def k_prep(hidden_ref, after_ref, normed_ref):
    gain = 1.0 / D

    def rows(i, _):
        at = pl.ds(pl.multiple_of(i * 64, 64), 64)
        h = hidden_ref[at, :].astype(F32)
        center = h - jnp.sum(h, axis=1, keepdims=True) * gain
        var = jnp.sum(center * center, axis=1, keepdims=True) * gain
        normed_ref[at, :] = (center * lax.rsqrt(var + 1e-06)).astype(BF)
        return 0

    lax.fori_loop(0, NTOK // 64, rows, 0)


def only(keep, value):
    return jnp.where(keep, value, jnp.zeros_like(value))


def k_back(clip_hbm, conv_hbm, sent_ref, grad_hbm, acc_ref, clip_ref, conv_ref, grad_ref, sems):
    copies = [
        pltpu.make_async_copy(clip_hbm, clip_ref, sems.at[0]),
        pltpu.make_async_copy(conv_hbm, conv_ref, sems.at[1]),
        pltpu.make_async_copy(grad_hbm.at[pl.ds(2, 2)], grad_ref.at[pl.ds(2, 2)], sems.at[2]),
    ]
    for copy in copies:
        copy.start()
    grad_ref[:2] = sent_ref[...]
    first = lax.axis_index("tm") * SLAB
    for copy in copies:
        copy.wait()
    start = [clip_rel(clip_ref, first, t) for t in range(SLAB)]
    for s in range(SLAB):
        total = mm(conv_ref[0], grad_ref[s], 0, 0)
        for k in range(1, min(TAPS, SLAB - s)):
            total = total + mm(conv_ref[k], only(start[s + k] <= s, grad_ref[s + k]), 0, 0)
        acc_ref[s] = total

    def opens(s, _):
        @pl.when(clip_rel(clip_ref, first, s) == s)
        def _():
            later = jnp.minimum(s + 1, SLAB - 1)
            keep = (s + 1 < SLAB) & (clip_rel(clip_ref, first, s + 1) <= s)
            acc_ref[s] += (
                mm(conv_ref[1], grad_ref[s], 0, 0)
                + mm(conv_ref[2], grad_ref[s], 0, 0)
                + mm(conv_ref[2], only(keep, grad_ref[later]), 0, 0)
            )

        return 0

    lax.fori_loop(0, SLAB, opens, 0)


def load_taps(clip_ref, first, lat_ref, z_ref, slot, frame, base):
    for k in range(TAPS):
        src = jnp.clip(source(clip_ref, first, frame, k) + base, 0, lat_ref.shape[0] - 1)
        z_ref[slot, k * CL : (k + 1) * CL, :] = lat_ref[src]


def set_weights(win_ref, bias_ref, wcat_ref):
    for k in range(TAPS):
        wcat_ref[k * CL : (k + 1) * CL, :] = win_ref[k]
    bias = bias_ref[...]
    high = bias.astype(BF)
    rest = bias - high.astype(F32)
    mid = rest.astype(BF)
    low = (rest - mid.astype(F32)).astype(BF)
    row = lax.broadcasted_iota(jnp.int32, (CL, C), 0)
    tail = jnp.where(row == 0, high.astype(F32), 0.0)
    tail = jnp.where(row == 1, mid.astype(F32), tail)
    tail = jnp.where(row == 2, low.astype(F32), tail)
    wcat_ref[TAPS * CL :, :] = tail.astype(BF)


def pre_of(clip_ref, first, all_ref, z_ref, wcol, slot, frame):
    load_taps(clip_ref, first, all_ref, z_ref, slot, frame, SLAB)
    z_ref[slot, TAPS * CL :, :] = jnp.ones((CL, PX), BF)
    pre = mm(wcol, z_ref[slot], 1, 0)
    return pre, 0.5 * jnp.tanh(0.5 * pre) + 0.5


def k_first(
    clip_ref, prev_ref, lat_ref, win_ref, bias_ref, acc_ref,
    act_ref, part_ref, halo_ref, icg_ref,
    all_ref, z_ref, wcat_ref, lacc_ref,
):
    first = lax.axis_index("tm") * SLAB
    all_ref[:SLAB] = prev_ref[...]
    all_ref[SLAB:] = lat_ref[...]
    set_weights(win_ref, bias_ref, wcat_ref)
    wcol = wcat_ref[...].T
    lacc_ref[...] = jnp.zeros_like(lacc_ref)
    icg = jnp.zeros((E, C), F32)
    for t in range(2):
        pre, sig = pre_of(clip_ref, first, all_ref, z_ref, wcol, t, t)
        act_ref[t] = (pre * sig).astype(BF)
        gp = (acc_ref[t] * (sig * (1.0 + pre * (1.0 - sig)))).astype(BF)
        back = mm(wcat_ref[...], gp, 1, 0)
        for k in range(TAPS):
            src = source(clip_ref, first, t, k) + 2
            lacc_ref[src] += back[k * CL : (k + 1) * CL]
        icg = icg + mm(z_ref[t], gp, 1, 1)
    halo_ref[...] = lacc_ref[:2]
    part_ref[...] = lacc_ref[2:]
    icg_ref[...] = icg


def k_rest(
    clip_ref, prev_ref, lat_ref, win_ref, bias_ref, act01_ref,
    act_ref, slope_ref, all_ref, z_ref, wcat_ref,
):
    first = lax.axis_index("tm") * SLAB
    all_ref[:SLAB] = prev_ref[...]
    all_ref[SLAB:] = lat_ref[...]
    set_weights(win_ref, bias_ref, wcat_ref)
    wcol = wcat_ref[...].T
    act_ref[2:4] = act01_ref[...]

    def before(j, _):
        pre, sig = pre_of(clip_ref, first, all_ref, z_ref, wcol, j, j - 2)
        act_ref[j] = (pre * sig).astype(BF)
        return 0

    def own(j, _):
        pre, sig = pre_of(clip_ref, first, all_ref, z_ref, wcol, j, j)
        act_ref[j + 2] = (pre * sig).astype(BF)
        slope_ref[j - 2] = sig * (1.0 + pre * (1.0 - sig))
        return 0

    lax.fori_loop(0, 2, before, 0)
    lax.fori_loop(2, SLAB, own, 0)


def k_weight(clip_ref, grad_ref, act_ref, keep_ref, send_ref, acc_ref):
    first = lax.axis_index("tm") * SLAB
    core = lax.axis_index("tm") % 2
    for k in range(TAPS):
        total = None
        for t in range(SLAB):
            src = jnp.maximum(source(clip_ref, first, t, k), -2) + 2
            part = mm(grad_ref[t], act_ref[src], 1, 1)
            total = part if total is None else total + part
        acc_ref[:, :, :, k * C : (k + 1) * C] = total.reshape(16, 2, 16, C)
    upper = lax.broadcasted_iota(jnp.int32, (32, 8, 128), 1) < 4
    for ref, half in ((keep_ref, core), (send_ref, 1 - core)):
        for jj in range(0, TAPS * C // 128, 4):
            even, odd = [], []
            for h in range(2):
                at = (jj + 2 * h) * 128
                a = acc_ref[:, half, :, at : at + 128].reshape(32, 8, 128)
                b = acc_ref[:, half, :, at + 128 : at + 256].reshape(32, 8, 128)
                even.append(jnp.where(upper, a, pltpu.roll(b, 4, 1)))
                odd.append(jnp.where(upper, pltpu.roll(a, 4, 1), b))
            ref[:, 0, jj * 4 : jj * 4 + 16, :] = jnp.concatenate(even, axis=1).astype(BF)
            ref[:, 1, jj * 4 : jj * 4 + 16, :] = jnp.concatenate(odd, axis=1).astype(BF)


def k_second(
    clip_ref, next_ref, lat_ref, win_ref, conv_ref, acc_in_ref, slope_ref, part_ref, halo_ref, icg_in_ref, after_ref,
    tok0_ref, tok1_ref, tok2_ref, tok3_ref, icg_ref, passed_ref, acc_ref, z_ref, wcat_ref, lacc_ref, icg_acc, low_ref,
):
    first = lax.axis_index("tm") * SLAB
    start = [clip_rel(clip_ref, first, SLAB + t) for t in range(2)]
    for k in range(TAPS):
        wcat_ref[k * CL : (k + 1) * CL, :] = win_ref[k]
    acc_ref[0] = acc_in_ref[2] + mm(conv_ref[2], only(start[0] <= 2, next_ref[0]), 0, 0)
    acc_ref[1] = (
        acc_in_ref[3]
        + mm(conv_ref[1], only(start[0] <= 3, next_ref[0]), 0, 0)
        + mm(conv_ref[2], only(start[1] <= 3, next_ref[1]), 0, 0)
    )

    @pl.when((clip_rel(clip_ref, first, 3) == 3) & (start[0] <= 3))
    def _():
        acc_ref[1] += mm(conv_ref[2], next_ref[0], 0, 0)

    lacc_ref[:SLAB] = part_ref[...]
    lacc_ref[2:SLAB] += halo_ref[...]
    icg = icg_in_ref[...]
    for t in range(2):
        gp = (acc_ref[t] * slope_ref[t]).astype(BF)
        load_taps(clip_ref, first, lat_ref, z_ref, t, t + 2, 0)
        z_ref[t, TAPS * CL :, :] = jnp.ones((CL, PX), BF)
        back = mm(wcat_ref[...], gp, 1, 0)
        for k in range(TAPS):
            src = source(clip_ref, first, t + 2, k)
            lacc_ref[src] += back[k * CL : (k + 1) * CL]
        icg = icg + mm(z_ref[t], gp, 1, 1)
    icg_acc[...] = icg
    for f in range(SLAB):
        low_ref[f * CL : (f + 1) * CL, :] = lacc_ref[f].astype(BF)
    r = lax.broadcasted_iota(jnp.int32, (PX, PX), 0)
    c = lax.broadcasted_iota(jnp.int32, (PX, PX), 1)
    pick = (((r & 3) << 7) + (r >> 2) == c).astype(F32).astype(BF)
    low_ref[...] = mm(low_ref[...], pick, 1, 0).astype(BF)
    z = lax.axis_index("seq")
    for k, ref in enumerate((tok0_ref, tok1_ref, tok2_ref, tok3_ref)):
        ref[...] = low_ref[pl.ds(pl.multiple_of(lax.rem(z + k, 4) * CL, CL), CL), :]
    for rb in range(4):
        for lb in range(4):
            icg_ref[rb * 4 + lb] = icg_acc[rb * 16 : (rb + 1) * 16, lb * 128 : (lb + 1) * 128].astype(BF)


def k_grad(
    tok0_ref, tok1_ref, tok2_ref, tok3_ref, normed_ref, icg_ref, keep_ref, other_ref,
    pack_ref, tok_hbm, raw_ref, recv_ref, tok_ref, sem,
):
    z = lax.axis_index("seq")
    for k, ref in enumerate((tok0_ref, tok1_ref, tok2_ref, tok3_ref)):
        recv_ref[lax.rem(z + 4 - k, 4)] = ref[...]
    for s in range(4):
        for q in range(EDGE):
            raw_ref[q * CL : (q + 1) * CL, s * 128 : (s + 1) * 128] = recv_ref[
                s, :, q * 128 : (q + 1) * 128
            ]
    r = lax.broadcasted_iota(jnp.int32, (E, E), 0)
    c = lax.broadcasted_iota(jnp.int32, (E, E), 1)
    order = (((r & 3) << 4) + (r >> 2) == c).astype(F32).astype(BF)
    tok = mm(order, raw_ref[...], 1, 0)
    tok_ref[...] = tok.astype(BF)
    copy = pltpu.make_async_copy(tok_ref, tok_hbm, sem)
    copy.start()
    total = jnp.broadcast_to(jnp.sum(tok, axis=1, keepdims=True), (E, 128)).astype(BF)
    for lb in range(D // 512):
        g = mm(tok_ref[...], normed_ref[:, lb * 512 : (lb + 1) * 512], 1, 0).astype(BF)
        for u in range(4):
            for rb in range(4):
                pack_ref[rb * 24 + lb * 4 + u, :16, :] = g[rb * 16 : (rb + 1) * 16, u * 128 : (u + 1) * 128]
    pack_ref[96:112, :16, :] = icg_ref[...]
    for rb in range(4):
        pack_ref[112 + rb, :16, :] = total[rb * 16 : (rb + 1) * 16]
    pack_ref[116:, :16, :] = jnp.zeros((12, 16, 128), BF)
    for xy in range(16):
        for half in range(2):
            at = pl.ds((xy * 2 + half) * 4, 4)
            rows = slice(half * 24, half * 24 + 24)
            both = keep_ref[xy * 4 : xy * 4 + 4].astype(F32) + other_ref[xy * 4 : xy * 4 + 4].astype(F32)
            pack_ref[at, 16:, :] = both[:, rows, :].astype(BF)
    copy.wait()


def k_hidden(tok_ref, hidden_ref, wt_ref, mod_ref, out_ref):
    gain = 1.0 / D
    h = hidden_ref[...].astype(F32)
    center = h - jnp.sum(h, axis=1, keepdims=True) * gain
    var = jnp.sum(center * center, axis=1, keepdims=True) * gain
    inv = lax.rsqrt(var + 1e-06)
    normed = center * inv
    mod_in = mm(tok_ref[...].T, wt_ref[...], 1, 0)
    ng = mod_in * (1.0 + mod_ref[1:2, :])
    m1 = jnp.sum(ng, axis=1, keepdims=True) * gain
    m2 = jnp.sum(ng * normed, axis=1, keepdims=True) * gain
    out_ref[...] = (inv * (ng - m1 - normed * m2)).astype(BF)


def k_sum(recv_ref, out_hbm, keep_ref, send_hbm, out_ref, send_ref, sems):
    core = lax.axis_index("tm") % 2
    total = jnp.sum(recv_ref[:, :16, :].astype(F32), axis=0).astype(BF)
    out_ref[...] = jnp.broadcast_to(total[None], out_ref.shape)
    copy = pltpu.make_async_copy(out_ref, out_hbm, sems.at[0])
    copy.start()
    sums = [jnp.zeros((24, 128), F32)] * 2
    for d in range(128):
        c = (d // 4) % 2
        sums[c] = sums[c] + recv_ref[d, 16:, :].astype(F32)
    keep_ref[...] = jnp.where(core == 0, sums[0], sums[1])
    send_ref[...] = jnp.where(core == 0, sums[1], sums[0])
    away = pltpu.make_async_copy(send_ref, send_hbm, sems.at[1])
    away.start()
    copy.wait()
    away.wait()


def k_last(all_ref, wt_ref, mod_ref, final_ref, modg_ref, icg_ref, bias_ref):
    tot = [all_ref[112 + rb].astype(F32) for rb in range(4)]
    for lb in range(D // 128):
        at = slice(lb * 128, (lb + 1) * 128)
        scale = 1.0 + mod_ref[1:2, at]
        shift = mod_ref[0:1, at]
        s0 = jnp.zeros((1, 128), F32)
        s1 = jnp.zeros((1, 128), F32)
        for rb in range(4):
            rows = slice(rb * 16, (rb + 1) * 16)
            g = all_ref[rb * 24 + lb].astype(F32)
            w = wt_ref[rows, at].astype(F32)
            final_ref[rows, at] = g * scale + shift * tot[rb]
            s0 = s0 + jnp.sum(w * tot[rb], axis=0, keepdims=True)
            s1 = s1 + jnp.sum(w * g, axis=0, keepdims=True)
        modg_ref[0:1, at] = s0
        modg_ref[1:2, at] = s1
    for rb in range(3):
        for lb in range(4):
            icg_ref[rb * 16 : (rb + 1) * 16, lb * 128 : (lb + 1) * 128] = all_ref[96 + rb * 4 + lb].astype(F32)
    for lb in range(4):
        bias_ref[:, lb * 128 : (lb + 1) * 128] = all_ref[96 + 12 + lb].astype(F32)[0:1]


def k_weight_out(keep_ref, other_ref, wt_ref, mod_ref, out_ref, wt_near_ref, mod_near_ref):
    wt_near_ref[...] = wt_ref[...]
    mod_near_ref[...] = mod_ref[...]
    core = lax.axis_index("tm") % 2
    mine, other = keep_ref[...], other_ref[...]
    halves = [jnp.where(core == 0, mine, other), jnp.where(core == 0, other, mine)]
    for j in range(12):
        rows = halves[j // 6][(j % 6) * 4 : (j % 6) * 4 + 4]
        out_ref[j // 4, :, (j % 4) * 128 : (j % 4 + 1) * 128] = rows


def call(fn, outs, specs, scratch=(), mib=40, est=None, name=None):
    return pl.pallas_call(
        fn,
        out_shape=outs,
        in_specs=specs,
        out_specs=jax.tree.map(lambda _: VMEM, outs),
        scratch_shapes=list(scratch),
        compiler_params=params(mib),
        cost_estimate=est,
        name=name,
    )


def sds(shape, dtype):
    return jax.ShapeDtypeStruct(shape, dtype)


def pinned(*arrays):
    return [pltpu.with_memory_space_constraint(a, pltpu.HBM) for a in arrays]


def shifted(block, distance):
    n = lax.axis_size("tm")
    route = [(i - distance, i) for i in range(n) if 0 <= i - distance < n]
    return lax.ppermute(block, "tm", route)


def swapped(block):
    return lax.ppermute(block, "tm", [(i, i ^ 1) for i in range(lax.axis_size("tm"))])


def exchange(block, axes):
    return lax.all_to_all(block, axes, split_axis=0, concat_axis=0, tiled=True)


def local(latents, hidden, grad_out, conv_in_w, conv_in_b, conv_w, final_w, modulation, clip_start):
    win = conv_in_w.transpose(0, 2, 1)
    wt = final_w.T
    bias = conv_in_b.reshape(1, C)
    lat_prev = shifted(latents, 1)
    unit = 2 * C * C * PX
    grad_sent = grad_out[:2]
    grad_next = shifted(grad_sent, -1)
    acc = call(
        k_back, sds((SLAB, C, PX), F32), [PIN, PIN, VMEM, PIN],
        [
            pltpu.SMEM((FRAMES,), jnp.int32), pltpu.VMEM((TAPS, C, C), BF), pltpu.VMEM((SLAB, C, PX), BF),
            pltpu.SemaphoreType.DMA((3,)),
        ],
        mib=16, est=cost(9 * unit, 8 << 20), name="back",
    )(*pinned(clip_start, conv_w), grad_sent, *pinned(grad_out))
    act01, part, halo, icg_part = call(
        k_first,
        (sds((2, C, PX), BF), sds((SLAB, CL, PX), F32), sds((2, CL, PX), F32), sds((E, C), F32)),
        [SMEM] + [VMEM] * 5,
        [
            pltpu.VMEM((2 * SLAB, CL, PX), BF), pltpu.VMEM((2, E, PX), BF), pltpu.VMEM((E, C), BF),
            pltpu.VMEM((SLAB + 2, CL, PX), F32),
        ],
        mib=16, est=cost(2 * unit, 5 << 20), name="first",
    )(clip_start, lat_prev, latents, win, bias, acc)
    halo_recv = shifted(halo, -1)
    act, slope = call(
        k_rest, (sds((SLAB + 2, C, PX), BF), sds((2, C, PX), F32)), [SMEM] + [VMEM] * 5,
        [pltpu.VMEM((2 * SLAB, CL, PX), BF), pltpu.VMEM((SLAB, E, PX), BF), pltpu.VMEM((E, C), BF)],
        mib=16, est=cost(2 * unit, 8 << 20), name="rest",
    )(clip_start, lat_prev, latents, win, bias, act01)
    keep, send = call(
        k_weight, (sds((32, 2, 48, 128), BF),) * 2, [SMEM] + [VMEM] * 2,
        [pltpu.VMEM((16, 2, 16, TAPS * C), F32)], mib=16, est=cost(12 * unit, 60 << 20), name="weight",
    )(clip_start, grad_out, act)
    piece = sds((CL, PX), BF)
    half = sds((32, 2, 48, 128), BF)
    *tok_parts, icg_blocks, send = pl.pallas_call(
        k_second,
        out_shape=(piece,) * 4 + (sds((16, 16, 128), BF), half),
        in_specs=[SMEM] + [VMEM] * 9 + [HERE],
        out_specs=(VMEM,) * 5 + (HERE,),
        scratch_shapes=[
            pltpu.VMEM((2, C, PX), F32), pltpu.VMEM((2, E, PX), BF), pltpu.VMEM((TAPS * CL, C), BF),
            pltpu.VMEM((SLAB, CL, PX), F32), pltpu.VMEM((E, C), F32), pltpu.VMEM((SLAB * CL, PX), BF),
        ],
        input_output_aliases={10: 5},
        compiler_params=params(16),
        cost_estimate=cost(6 * unit, 8 << 20),
        name="second",
    )(clip_start, grad_next, latents, win, conv_w, acc, slope, part, halo_recv, icg_part, send)
    toks = [tok_parts[0]] + [
        lax.ppermute(tok_parts[k], "seq", [(i, (i + k) % 4) for i in range(4)]) for k in range(1, 4)
    ]
    other = swapped(send)
    normed = call(
        k_prep, sds((NTOK, D), BF), [VMEM, HERE], mib=16, est=cost(10 * NTOK * D, 6 << 20), name="prep"
    )(hidden, icg_blocks)
    pack, tok = pl.pallas_call(
        k_grad,
        out_shape=(sds((128, 40, 128), BF), pltpu.HBM((E, NTOK), BF)),
        in_specs=[VMEM] * 8,
        out_specs=(VMEM, PIN),
        scratch_shapes=[
            pltpu.VMEM((E, NTOK), BF), pltpu.VMEM((4, CL, PX), BF), pltpu.VMEM((E, NTOK), BF),
            pltpu.SemaphoreType.DMA,
        ],
        compiler_params=params(16),
        cost_estimate=cost(2 * NTOK * D * E, 5 << 20),
        name="grad",
    )(*toks, normed, icg_blocks, keep.reshape(64, 48, 128), other.reshape(64, 48, 128))
    recv = exchange(pack, BOTH)
    hidden_grad = pl.pallas_call(
        k_hidden,
        grid=(4,),
        out_shape=sds((NTOK, D), BF),
        in_specs=[
            pl.BlockSpec((E, 128), lambda i: (0, i)),
            pl.BlockSpec((128, D), lambda i: (i, 0)),
            pl.BlockSpec((E, D), lambda i: (0, 0)),
            pl.BlockSpec((2, D), lambda i: (0, 0)),
        ],
        out_specs=pl.BlockSpec((128, D), lambda i: (i, 0)),
        compiler_params=params(16),
        cost_estimate=cost(2 * NTOK * D * E, 6 << 20),
        name="hidden",
    )(tok, hidden, wt, modulation)
    copies, own, away = pl.pallas_call(
        k_sum,
        out_shape=(pltpu.HBM((128, 16, 128), BF), sds((24, 128), F32), pltpu.HBM((24, 128), F32)),
        in_specs=[VMEM],
        out_specs=(PIN, VMEM, PIN),
        scratch_shapes=[
            pltpu.VMEM((128, 16, 128), BF), pltpu.VMEM((24, 128), F32), pltpu.SemaphoreType.DMA((2,)),
        ],
        compiler_params=params(16),
        cost_estimate=cost(1 << 20, 2 << 20),
        name="sum",
    )(recv)
    everything = exchange(copies, BOTH)
    weight_grad, wt_near, mod_near = call(
        k_weight_out, (sds((TAPS, 4, C), F32), sds((E, D), BF), sds((2, D), F32)), [VMEM] * 4,
        mib=16, est=cost(1 << 12, 1 << 16), name="weight_out",
    )(own, swapped(away), wt, modulation)
    final_t, mod_grad, icg, bias_grad = call(
        k_last, (sds((E, D), F32), sds((2, D), F32), sds((TAPS * CL, C), F32), sds((1, C), F32)), [VMEM] * 3,
        mib=16, est=cost(1 << 20, 2 << 20), name="last",
    )(everything, wt_near, mod_near)
    return (
        hidden_grad,
        weight_grad.transpose(1, 0, 2),
        icg.reshape(TAPS, CL, C).transpose(0, 2, 1),
        bias_grad.reshape(C),
        final_t.T,
        mod_grad,
    )


def solution(mesh):
    return jax.shard_map(
        local,
        mesh=mesh,
        in_specs=(
            P("tm", None, "seq"),
            P(("tm", "seq"), None),
            P("tm", None, "seq"),
            P(), P(), P(), P(), P(), P(),
        ),
        out_specs=(P(("tm", "seq"), None), P(("tm", "seq"), None, None), P(), P(), P(), P()),
        check_vma=False,
    )
```

```python
import jax
import jax.numpy as jnp
from jax import lax
from jax.experimental import pallas as pl
from jax.experimental.pallas import tpu as pltpu
from jax.sharding import PartitionSpec as P

BF = jnp.bfloat16
F32 = jnp.float32
VMEM = pl.BlockSpec(memory_space=pltpu.VMEM)
SMEM = pl.BlockSpec(memory_space=pltpu.SMEM)
HERE = pl.BlockSpec(memory_space=pl.ANY)
PIN = pl.BlockSpec(memory_space=pltpu.HBM)
EDGE = 4
TAPS = 3
SLAB = 4
CL = 16
C = 512
PX = 512
D = 3072
E = 64
NTOK = 512
FRAMES = 128
BOTH = ("tm", "seq")


def params(mib):
    return pltpu.CompilerParams(vmem_limit_bytes=mib * 1024 * 1024)


def cost(flops, nbytes, trans=0):
    return pl.CostEstimate(flops=flops, bytes_accessed=nbytes, transcendentals=trans)


def mm(a, b, ca, cb):
    return lax.dot_general(a, b, (((ca,), (cb,)), ((), ())), preferred_element_type=F32)


def clip_rel(clip_ref, first, frame):
    whole = first + frame
    start = clip_ref[jnp.clip(whole, 0, FRAMES - 1)]
    return jnp.where(whole >= FRAMES, frame, start - first)


def source(clip_ref, first, frame, tap):
    return jnp.maximum(frame - tap, clip_rel(clip_ref, first, frame))


def k_prep(hidden_ref, after_ref, normed_ref):
    gain = 1.0 / D

    def rows(i, _):
        at = pl.ds(pl.multiple_of(i * 64, 64), 64)
        h = hidden_ref[at, :].astype(F32)
        center = h - jnp.sum(h, axis=1, keepdims=True) * gain
        var = jnp.sum(center * center, axis=1, keepdims=True) * gain
        normed_ref[at, :] = (center * lax.rsqrt(var + 1e-06)).astype(BF)
        return 0

    lax.fori_loop(0, NTOK // 64, rows, 0)


def only(keep, value):
    return jnp.where(keep, value, jnp.zeros_like(value))


def k_back(clip_hbm, conv_hbm, sent_ref, grad_hbm, acc_ref, clip_ref, conv_ref, grad_ref, sems):
    copies = [
        pltpu.make_async_copy(conv_hbm.at[0], conv_ref.at[0], sems.at[0]),
        pltpu.make_async_copy(clip_hbm, clip_ref, sems.at[1]),
        pltpu.make_async_copy(conv_hbm.at[pl.ds(1, 2)], conv_ref.at[pl.ds(1, 2)], sems.at[2]),
        pltpu.make_async_copy(grad_hbm.at[pl.ds(2, 2)], grad_ref.at[pl.ds(2, 2)], sems.at[3]),
    ]
    for copy in copies:
        copy.start()
    grad_ref[:2] = sent_ref[...]
    first = lax.axis_index("tm") * SLAB
    copies[0].wait()
    for s in range(2):
        acc_ref[s] = mm(conv_ref[0], grad_ref[s], 0, 0)
    for copy in copies[1:]:
        copy.wait()
    start = [clip_rel(clip_ref, first, t) for t in range(SLAB)]
    for s in range(SLAB):
        total = acc_ref[s] if s < 2 else mm(conv_ref[0], grad_ref[s], 0, 0)
        for k in range(1, min(TAPS, SLAB - s)):
            total = total + mm(conv_ref[k], only(start[s + k] <= s, grad_ref[s + k]), 0, 0)
        acc_ref[s] = total

    def opens(s, _):
        @pl.when(clip_rel(clip_ref, first, s) == s)
        def _():
            later = jnp.minimum(s + 1, SLAB - 1)
            keep = (s + 1 < SLAB) & (clip_rel(clip_ref, first, s + 1) <= s)
            acc_ref[s] += (
                mm(conv_ref[1], grad_ref[s], 0, 0)
                + mm(conv_ref[2], grad_ref[s], 0, 0)
                + mm(conv_ref[2], only(keep, grad_ref[later]), 0, 0)
            )

        return 0

    lax.fori_loop(0, SLAB, opens, 0)


def load_taps(clip_ref, first, lat_ref, z_ref, slot, frame, base):
    for k in range(TAPS):
        src = jnp.clip(source(clip_ref, first, frame, k) + base, 0, lat_ref.shape[0] - 1)
        z_ref[slot, k * CL : (k + 1) * CL, :] = lat_ref[src]


def set_weights(win_ref, bias_ref, wcat_ref):
    for k in range(TAPS):
        wcat_ref[k * CL : (k + 1) * CL, :] = win_ref[k]
    bias = bias_ref[...]
    high = bias.astype(BF)
    rest = bias - high.astype(F32)
    mid = rest.astype(BF)
    low = (rest - mid.astype(F32)).astype(BF)
    row = lax.broadcasted_iota(jnp.int32, (CL, C), 0)
    tail = jnp.where(row == 0, high.astype(F32), 0.0)
    tail = jnp.where(row == 1, mid.astype(F32), tail)
    tail = jnp.where(row == 2, low.astype(F32), tail)
    wcat_ref[TAPS * CL :, :] = tail.astype(BF)


def pre_of(clip_ref, first, all_ref, z_ref, wcol, slot, frame):
    load_taps(clip_ref, first, all_ref, z_ref, slot, frame, SLAB)
    z_ref[slot, TAPS * CL :, :] = jnp.ones((CL, PX), BF)
    pre = mm(wcol, z_ref[slot], 1, 0)
    return pre, 0.5 * jnp.tanh(0.5 * pre) + 0.5


def k_first(
    clip_ref, prev_ref, lat_ref, win_ref, bias_ref, acc_ref,
    act_ref, part_ref, halo_ref, icg_ref,
    all_ref, z_ref, wcat_ref, lacc_ref,
):
    first = lax.axis_index("tm") * SLAB
    all_ref[:SLAB] = prev_ref[...]
    all_ref[SLAB:] = lat_ref[...]
    set_weights(win_ref, bias_ref, wcat_ref)
    wcol = wcat_ref[...].T
    lacc_ref[...] = jnp.zeros_like(lacc_ref)
    icg = jnp.zeros((E, C), F32)
    for t in range(2):
        pre, sig = pre_of(clip_ref, first, all_ref, z_ref, wcol, t, t)
        act_ref[t] = (pre * sig).astype(BF)
        gp = (acc_ref[t] * (sig * (1.0 + pre * (1.0 - sig)))).astype(BF)
        back = mm(wcat_ref[...], gp, 1, 0)
        for k in range(TAPS):
            src = source(clip_ref, first, t, k) + 2
            lacc_ref[src] += back[k * CL : (k + 1) * CL]
        icg = icg + mm(z_ref[t], gp, 1, 1)
    halo_ref[...] = lacc_ref[:2]
    part_ref[...] = lacc_ref[2:]
    icg_ref[...] = icg


def k_rest(
    clip_ref, prev_ref, lat_ref, win_ref, bias_ref, act01_ref,
    act_ref, slope_ref, all_ref, z_ref, wcat_ref,
):
    first = lax.axis_index("tm") * SLAB
    all_ref[:SLAB] = prev_ref[...]
    all_ref[SLAB:] = lat_ref[...]
    set_weights(win_ref, bias_ref, wcat_ref)
    wcol = wcat_ref[...].T
    act_ref[2:4] = act01_ref[...]

    def before(j, _):
        pre, sig = pre_of(clip_ref, first, all_ref, z_ref, wcol, j, j - 2)
        act_ref[j] = (pre * sig).astype(BF)
        return 0

    def own(j, _):
        pre, sig = pre_of(clip_ref, first, all_ref, z_ref, wcol, j, j)
        act_ref[j + 2] = (pre * sig).astype(BF)
        slope_ref[j - 2] = sig * (1.0 + pre * (1.0 - sig))
        return 0

    lax.fori_loop(0, 2, before, 0)
    lax.fori_loop(2, SLAB, own, 0)


def k_weight(clip_ref, grad_ref, act_ref, keep_ref, send_ref, acc_ref):
    first = lax.axis_index("tm") * SLAB
    core = lax.axis_index("tm") % 2
    for k in range(TAPS):
        total = None
        for t in range(SLAB):
            src = jnp.maximum(source(clip_ref, first, t, k), -2) + 2
            part = mm(grad_ref[t], act_ref[src], 1, 1)
            total = part if total is None else total + part
        acc_ref[:, :, :, k * C : (k + 1) * C] = total.reshape(16, 2, 16, C)
    upper = lax.broadcasted_iota(jnp.int32, (32, 8, 128), 1) < 4
    for ref, half in ((keep_ref, core), (send_ref, 1 - core)):
        for jj in range(0, TAPS * C // 128, 4):
            even, odd = [], []
            for h in range(2):
                at = (jj + 2 * h) * 128
                a = acc_ref[:, half, :, at : at + 128].reshape(32, 8, 128)
                b = acc_ref[:, half, :, at + 128 : at + 256].reshape(32, 8, 128)
                even.append(jnp.where(upper, a, pltpu.roll(b, 4, 1)))
                odd.append(jnp.where(upper, pltpu.roll(a, 4, 1), b))
            ref[:, 0, jj * 4 : jj * 4 + 16, :] = jnp.concatenate(even, axis=1).astype(BF)
            ref[:, 1, jj * 4 : jj * 4 + 16, :] = jnp.concatenate(odd, axis=1).astype(BF)


def k_second(
    clip_ref, next_ref, lat_ref, win_ref, conv_ref, acc_in_ref, slope_ref, part_ref, halo_ref, icg_in_ref, after_ref,
    tok0_ref, tok1_ref, tok2_ref, tok3_ref, icg_ref, passed_ref, acc_ref, z_ref, wcat_ref, lacc_ref, icg_acc, low_ref,
):
    first = lax.axis_index("tm") * SLAB
    start = [clip_rel(clip_ref, first, SLAB + t) for t in range(2)]
    for k in range(TAPS):
        wcat_ref[k * CL : (k + 1) * CL, :] = win_ref[k]
    acc_ref[0] = acc_in_ref[2] + mm(conv_ref[2], only(start[0] <= 2, next_ref[0]), 0, 0)
    acc_ref[1] = (
        acc_in_ref[3]
        + mm(conv_ref[1], only(start[0] <= 3, next_ref[0]), 0, 0)
        + mm(conv_ref[2], only(start[1] <= 3, next_ref[1]), 0, 0)
    )

    @pl.when((clip_rel(clip_ref, first, 3) == 3) & (start[0] <= 3))
    def _():
        acc_ref[1] += mm(conv_ref[2], next_ref[0], 0, 0)

    lacc_ref[:SLAB] = part_ref[...]
    lacc_ref[2:SLAB] += halo_ref[...]
    icg = icg_in_ref[...]
    for t in range(2):
        gp = (acc_ref[t] * slope_ref[t]).astype(BF)
        load_taps(clip_ref, first, lat_ref, z_ref, t, t + 2, 0)
        z_ref[t, TAPS * CL :, :] = jnp.ones((CL, PX), BF)
        back = mm(wcat_ref[...], gp, 1, 0)
        for k in range(TAPS):
            src = source(clip_ref, first, t + 2, k)
            lacc_ref[src] += back[k * CL : (k + 1) * CL]
        icg = icg + mm(z_ref[t], gp, 1, 1)
    icg_acc[...] = icg
    for f in range(SLAB):
        low_ref[f * CL : (f + 1) * CL, :] = lacc_ref[f].astype(BF)
    r = lax.broadcasted_iota(jnp.int32, (PX, PX), 0)
    c = lax.broadcasted_iota(jnp.int32, (PX, PX), 1)
    pick = (((r & 3) << 7) + (r >> 2) == c).astype(F32).astype(BF)
    low_ref[...] = mm(low_ref[...], pick, 1, 0).astype(BF)
    z = lax.axis_index("seq")
    for k, ref in enumerate((tok0_ref, tok1_ref, tok2_ref, tok3_ref)):
        ref[...] = low_ref[pl.ds(pl.multiple_of(lax.rem(z + k, 4) * CL, CL), CL), :]
    for rb in range(4):
        for lb in range(4):
            icg_ref[rb * 4 + lb] = icg_acc[rb * 16 : (rb + 1) * 16, lb * 128 : (lb + 1) * 128].astype(BF)


def k_grad(
    tok0_ref, tok1_ref, tok2_ref, tok3_ref, normed_ref, icg_ref, keep_ref, other_ref,
    pack_ref, tok_hbm, raw_ref, recv_ref, tok_ref, sem,
):
    z = lax.axis_index("seq")
    for k, ref in enumerate((tok0_ref, tok1_ref, tok2_ref, tok3_ref)):
        recv_ref[lax.rem(z + 4 - k, 4)] = ref[...]
    for s in range(4):
        for q in range(EDGE):
            raw_ref[q * CL : (q + 1) * CL, s * 128 : (s + 1) * 128] = recv_ref[
                s, :, q * 128 : (q + 1) * 128
            ]
    r = lax.broadcasted_iota(jnp.int32, (E, E), 0)
    c = lax.broadcasted_iota(jnp.int32, (E, E), 1)
    order = (((r & 3) << 4) + (r >> 2) == c).astype(F32).astype(BF)
    tok = mm(order, raw_ref[...], 1, 0)
    tok_ref[...] = tok.astype(BF)
    copy = pltpu.make_async_copy(tok_ref, tok_hbm, sem)
    copy.start()
    total = jnp.broadcast_to(jnp.sum(tok, axis=1, keepdims=True), (E, 128)).astype(BF)
    for lb in range(D // 512):
        g = mm(tok_ref[...], normed_ref[:, lb * 512 : (lb + 1) * 512], 1, 0).astype(BF)
        for u in range(4):
            for rb in range(4):
                pack_ref[rb * 24 + lb * 4 + u, :16, :] = g[rb * 16 : (rb + 1) * 16, u * 128 : (u + 1) * 128]
    pack_ref[96:112, :16, :] = icg_ref[...]
    for rb in range(4):
        pack_ref[112 + rb, :16, :] = total[rb * 16 : (rb + 1) * 16]
    pack_ref[116:, :16, :] = jnp.zeros((12, 16, 128), BF)
    for xy in range(16):
        for half in range(2):
            at = pl.ds((xy * 2 + half) * 4, 4)
            rows = slice(half * 24, half * 24 + 24)
            both = keep_ref[xy * 4 : xy * 4 + 4].astype(F32) + other_ref[xy * 4 : xy * 4 + 4].astype(F32)
            pack_ref[at, 16:, :] = both[:, rows, :].astype(BF)
    copy.wait()


def k_hidden(tok_ref, hidden_ref, wt_ref, mod_ref, out_ref):
    gain = 1.0 / D
    h = hidden_ref[...].astype(F32)
    center = h - jnp.sum(h, axis=1, keepdims=True) * gain
    var = jnp.sum(center * center, axis=1, keepdims=True) * gain
    inv = lax.rsqrt(var + 1e-06)
    normed = center * inv
    mod_in = mm(tok_ref[...].T, wt_ref[...], 1, 0)
    ng = mod_in * (1.0 + mod_ref[1:2, :])
    m1 = jnp.sum(ng, axis=1, keepdims=True) * gain
    m2 = jnp.sum(ng * normed, axis=1, keepdims=True) * gain
    out_ref[...] = (inv * (ng - m1 - normed * m2)).astype(BF)


def k_sum(recv_ref, out_hbm, keep_ref, send_hbm, out_ref, send_ref, sems):
    core = lax.axis_index("tm") % 2
    total = jnp.sum(recv_ref[:, :16, :].astype(F32), axis=0).astype(BF)
    out_ref[...] = jnp.broadcast_to(total[None], out_ref.shape)
    copy = pltpu.make_async_copy(out_ref, out_hbm, sems.at[0])
    copy.start()
    sums = [jnp.zeros((24, 128), F32)] * 2
    for d in range(128):
        c = (d // 4) % 2
        sums[c] = sums[c] + recv_ref[d, 16:, :].astype(F32)
    keep_ref[...] = jnp.where(core == 0, sums[0], sums[1])
    send_ref[...] = jnp.where(core == 0, sums[1], sums[0])
    away = pltpu.make_async_copy(send_ref, send_hbm, sems.at[1])
    away.start()
    copy.wait()
    away.wait()


def k_last(all_ref, wt_ref, mod_ref, final_ref, modg_ref, icg_ref, bias_ref):
    tot = [all_ref[112 + rb].astype(F32) for rb in range(4)]
    for lb in range(D // 128):
        at = slice(lb * 128, (lb + 1) * 128)
        scale = 1.0 + mod_ref[1:2, at]
        shift = mod_ref[0:1, at]
        s0 = jnp.zeros((1, 128), F32)
        s1 = jnp.zeros((1, 128), F32)
        for rb in range(4):
            rows = slice(rb * 16, (rb + 1) * 16)
            g = all_ref[rb * 24 + lb].astype(F32)
            w = wt_ref[rows, at].astype(F32)
            final_ref[rows, at] = g * scale + shift * tot[rb]
            s0 = s0 + jnp.sum(w * tot[rb], axis=0, keepdims=True)
            s1 = s1 + jnp.sum(w * g, axis=0, keepdims=True)
        modg_ref[0:1, at] = s0
        modg_ref[1:2, at] = s1
    for rb in range(3):
        for lb in range(4):
            icg_ref[rb * 16 : (rb + 1) * 16, lb * 128 : (lb + 1) * 128] = all_ref[96 + rb * 4 + lb].astype(F32)
    for lb in range(4):
        bias_ref[:, lb * 128 : (lb + 1) * 128] = all_ref[96 + 12 + lb].astype(F32)[0:1]


def k_weight_out(keep_ref, other_ref, wt_ref, mod_ref, out_ref, wt_near_ref, mod_near_ref):
    wt_near_ref[...] = wt_ref[...]
    mod_near_ref[...] = mod_ref[...]
    core = lax.axis_index("tm") % 2
    mine, other = keep_ref[...], other_ref[...]
    halves = [jnp.where(core == 0, mine, other), jnp.where(core == 0, other, mine)]
    for j in range(12):
        rows = halves[j // 6][(j % 6) * 4 : (j % 6) * 4 + 4]
        out_ref[j // 4, :, (j % 4) * 128 : (j % 4 + 1) * 128] = rows


def call(fn, outs, specs, scratch=(), mib=40, est=None, name=None):
    return pl.pallas_call(
        fn,
        out_shape=outs,
        in_specs=specs,
        out_specs=jax.tree.map(lambda _: VMEM, outs),
        scratch_shapes=list(scratch),
        compiler_params=params(mib),
        cost_estimate=est,
        name=name,
    )


def sds(shape, dtype):
    return jax.ShapeDtypeStruct(shape, dtype)


def pinned(*arrays):
    return [pltpu.with_memory_space_constraint(a, pltpu.HBM) for a in arrays]


def shifted(block, distance):
    n = lax.axis_size("tm")
    route = [(i - distance, i) for i in range(n) if 0 <= i - distance < n]
    return lax.ppermute(block, "tm", route)


def swapped(block):
    return lax.ppermute(block, "tm", [(i, i ^ 1) for i in range(lax.axis_size("tm"))])


def exchange(block, axes):
    return lax.all_to_all(block, axes, split_axis=0, concat_axis=0, tiled=True)


def local(latents, hidden, grad_out, conv_in_w, conv_in_b, conv_w, final_w, modulation, clip_start):
    win = conv_in_w.transpose(0, 2, 1)
    wt = final_w.T
    bias = conv_in_b.reshape(1, C)
    lat_prev = shifted(latents, 1)
    unit = 2 * C * C * PX
    grad_sent = grad_out[:2]
    grad_next = shifted(grad_sent, -1)
    acc = call(
        k_back, sds((SLAB, C, PX), F32), [PIN, PIN, VMEM, PIN],
        [
            pltpu.SMEM((FRAMES,), jnp.int32), pltpu.VMEM((TAPS, C, C), BF), pltpu.VMEM((SLAB, C, PX), BF),
            pltpu.SemaphoreType.DMA((4,)),
        ],
        mib=16, est=cost(1 << 10, 1 << 10), name="back",
    )(*pinned(clip_start, conv_w), grad_sent, *pinned(grad_out))
    act01, part, halo, icg_part = call(
        k_first,
        (sds((2, C, PX), BF), sds((SLAB, CL, PX), F32), sds((2, CL, PX), F32), sds((E, C), F32)),
        [SMEM] + [VMEM] * 5,
        [
            pltpu.VMEM((2 * SLAB, CL, PX), BF), pltpu.VMEM((2, E, PX), BF), pltpu.VMEM((E, C), BF),
            pltpu.VMEM((SLAB + 2, CL, PX), F32),
        ],
        mib=16, est=cost(2 * unit, 5 << 20), name="first",
    )(clip_start, lat_prev, latents, win, bias, acc)
    halo_recv = shifted(halo, -1)
    act, slope = call(
        k_rest, (sds((SLAB + 2, C, PX), BF), sds((2, C, PX), F32)), [SMEM] + [VMEM] * 5,
        [pltpu.VMEM((2 * SLAB, CL, PX), BF), pltpu.VMEM((SLAB, E, PX), BF), pltpu.VMEM((E, C), BF)],
        mib=16, est=cost(2 * unit, 8 << 20), name="rest",
    )(clip_start, lat_prev, latents, win, bias, act01)
    keep, send = call(
        k_weight, (sds((32, 2, 48, 128), BF),) * 2, [SMEM] + [VMEM] * 2,
        [pltpu.VMEM((16, 2, 16, TAPS * C), F32)], mib=16, est=cost(50 * unit, 7 << 20), name="weight",
    )(clip_start, grad_out, act)
    piece = sds((CL, PX), BF)
    half = sds((32, 2, 48, 128), BF)
    *tok_parts, icg_blocks, send = pl.pallas_call(
        k_second,
        out_shape=(piece,) * 4 + (sds((16, 16, 128), BF), half),
        in_specs=[SMEM] + [VMEM] * 9 + [HERE],
        out_specs=(VMEM,) * 5 + (HERE,),
        scratch_shapes=[
            pltpu.VMEM((2, C, PX), F32), pltpu.VMEM((2, E, PX), BF), pltpu.VMEM((TAPS * CL, C), BF),
            pltpu.VMEM((SLAB, CL, PX), F32), pltpu.VMEM((E, C), F32), pltpu.VMEM((SLAB * CL, PX), BF),
        ],
        input_output_aliases={10: 5},
        compiler_params=params(16),
        cost_estimate=cost(6 * unit, 8 << 20),
        name="second",
    )(clip_start, grad_next, latents, win, conv_w, acc, slope, part, halo_recv, icg_part, send)
    toks = [tok_parts[0]] + [
        lax.ppermute(tok_parts[k], "seq", [(i, (i + k) % 4) for i in range(4)]) for k in range(1, 4)
    ]
    other = swapped(send)
    normed = call(
        k_prep, sds((NTOK, D), BF), [VMEM, HERE], mib=16, est=cost(10 * NTOK * D, 6 << 20), name="prep"
    )(hidden, icg_blocks)
    pack, tok = pl.pallas_call(
        k_grad,
        out_shape=(sds((128, 40, 128), BF), pltpu.HBM((E, NTOK), BF)),
        in_specs=[VMEM] * 8,
        out_specs=(VMEM, PIN),
        scratch_shapes=[
            pltpu.VMEM((E, NTOK), BF), pltpu.VMEM((4, CL, PX), BF), pltpu.VMEM((E, NTOK), BF),
            pltpu.SemaphoreType.DMA,
        ],
        compiler_params=params(16),
        cost_estimate=cost(2 * NTOK * D * E, 5 << 20),
        name="grad",
    )(*toks, normed, icg_blocks, keep.reshape(64, 48, 128), other.reshape(64, 48, 128))
    recv = exchange(pack, BOTH)
    hidden_grad = pl.pallas_call(
        k_hidden,
        grid=(4,),
        out_shape=sds((NTOK, D), BF),
        in_specs=[
            pl.BlockSpec((E, 128), lambda i: (0, i)),
            pl.BlockSpec((128, D), lambda i: (i, 0)),
            pl.BlockSpec((E, D), lambda i: (0, 0)),
            pl.BlockSpec((2, D), lambda i: (0, 0)),
        ],
        out_specs=pl.BlockSpec((128, D), lambda i: (i, 0)),
        compiler_params=params(16),
        cost_estimate=cost(2 * NTOK * D * E, 6 << 20),
        name="hidden",
    )(tok, hidden, wt, modulation)
    copies, own, away = pl.pallas_call(
        k_sum,
        out_shape=(pltpu.HBM((128, 16, 128), BF), sds((24, 128), F32), pltpu.HBM((24, 128), F32)),
        in_specs=[VMEM],
        out_specs=(PIN, VMEM, PIN),
        scratch_shapes=[
            pltpu.VMEM((128, 16, 128), BF), pltpu.VMEM((24, 128), F32), pltpu.SemaphoreType.DMA((2,)),
        ],
        compiler_params=params(16),
        cost_estimate=cost(1 << 20, 2 << 20),
        name="sum",
    )(recv)
    everything = exchange(copies, BOTH)
    weight_grad, wt_near, mod_near = call(
        k_weight_out, (sds((TAPS, 4, C), F32), sds((E, D), BF), sds((2, D), F32)), [VMEM] * 4,
        mib=16, est=cost(1 << 12, 1 << 16), name="weight_out",
    )(own, swapped(away), wt, modulation)
    final_t, mod_grad, icg, bias_grad = call(
        k_last, (sds((E, D), F32), sds((2, D), F32), sds((TAPS * CL, C), F32), sds((1, C), F32)), [VMEM] * 3,
        mib=16, est=cost(1 << 20, 2 << 20), name="last",
    )(everything, wt_near, mod_near)
    return (
        hidden_grad,
        weight_grad.transpose(1, 0, 2),
        icg.reshape(TAPS, CL, C).transpose(0, 2, 1),
        bias_grad.reshape(C),
        final_t.T,
        mod_grad,
    )


def solution(mesh):
    return jax.shard_map(
        local,
        mesh=mesh,
        in_specs=(
            P("tm", None, "seq"),
            P(("tm", "seq"), None),
            P("tm", None, "seq"),
            P(), P(), P(), P(), P(), P(),
        ),
        out_specs=(P(("tm", "seq"), None), P(("tm", "seq"), None, None), P(), P(), P(), P()),
        check_vma=False,
    )
```

```python
import jax
import jax.numpy as jnp
from jax import lax
from jax.experimental import pallas as pl
from jax.experimental.pallas import tpu as pltpu
from jax.sharding import PartitionSpec as P

BF = jnp.bfloat16
F32 = jnp.float32
VMEM = pl.BlockSpec(memory_space=pltpu.VMEM)
SMEM = pl.BlockSpec(memory_space=pltpu.SMEM)
HERE = pl.BlockSpec(memory_space=pl.ANY)
PIN = pl.BlockSpec(memory_space=pltpu.HBM)
EDGE = 4
TAPS = 3
SLAB = 4
CL = 16
C = 512
PX = 512
D = 3072
E = 64
NTOK = 512
FRAMES = 128
BOTH = ("tm", "seq")


def params(mib):
    return pltpu.CompilerParams(vmem_limit_bytes=mib * 1024 * 1024)


def cost(flops, nbytes, trans=0):
    return pl.CostEstimate(flops=flops, bytes_accessed=nbytes, transcendentals=trans)


def mm(a, b, ca, cb):
    return lax.dot_general(a, b, (((ca,), (cb,)), ((), ())), preferred_element_type=F32)


def clip_rel(clip_ref, first, frame):
    whole = first + frame
    start = clip_ref[jnp.clip(whole, 0, FRAMES - 1)]
    return jnp.where(whole >= FRAMES, frame, start - first)


def source(clip_ref, first, frame, tap):
    return jnp.maximum(frame - tap, clip_rel(clip_ref, first, frame))


def k_prep(hidden_ref, after_ref, normed_ref):
    gain = 1.0 / D

    def rows(i, _):
        at = pl.ds(pl.multiple_of(i * 64, 64), 64)
        h = hidden_ref[at, :].astype(F32)
        center = h - jnp.sum(h, axis=1, keepdims=True) * gain
        var = jnp.sum(center * center, axis=1, keepdims=True) * gain
        normed_ref[at, :] = (center * lax.rsqrt(var + 1e-06)).astype(BF)
        return 0

    lax.fori_loop(0, NTOK // 64, rows, 0)


def only(keep, value):
    return jnp.where(keep, value, jnp.zeros_like(value))


def k_back(clip_hbm, conv_hbm, sent_ref, grad_hbm, acc_ref, clip_ref, conv_ref, grad_ref, sems):
    copies = [
        pltpu.make_async_copy(conv_hbm.at[0], conv_ref.at[0], sems.at[0]),
        pltpu.make_async_copy(clip_hbm, clip_ref, sems.at[1]),
        pltpu.make_async_copy(conv_hbm.at[pl.ds(1, 2)], conv_ref.at[pl.ds(1, 2)], sems.at[2]),
        pltpu.make_async_copy(grad_hbm.at[pl.ds(2, 2)], grad_ref.at[pl.ds(2, 2)], sems.at[3]),
    ]
    for copy in copies:
        copy.start()
    grad_ref[:2] = sent_ref[...]
    first = lax.axis_index("tm") * SLAB
    copies[0].wait()
    for s in range(2):
        acc_ref[s] = mm(conv_ref[0], grad_ref[s], 0, 0)
    for copy in copies[1:]:
        copy.wait()
    start = [clip_rel(clip_ref, first, t) for t in range(SLAB)]
    for s in range(SLAB):
        total = acc_ref[s] if s < 2 else mm(conv_ref[0], grad_ref[s], 0, 0)
        for k in range(1, min(TAPS, SLAB - s)):
            total = total + mm(conv_ref[k], only(start[s + k] <= s, grad_ref[s + k]), 0, 0)
        acc_ref[s] = total

    def opens(s, _):
        @pl.when(clip_rel(clip_ref, first, s) == s)
        def _():
            later = jnp.minimum(s + 1, SLAB - 1)
            keep = (s + 1 < SLAB) & (clip_rel(clip_ref, first, s + 1) <= s)
            acc_ref[s] += (
                mm(conv_ref[1], grad_ref[s], 0, 0)
                + mm(conv_ref[2], grad_ref[s], 0, 0)
                + mm(conv_ref[2], only(keep, grad_ref[later]), 0, 0)
            )

        return 0

    lax.fori_loop(0, SLAB, opens, 0)


def load_taps(clip_ref, first, lat_ref, z_ref, slot, frame, base):
    for k in range(TAPS):
        src = jnp.clip(source(clip_ref, first, frame, k) + base, 0, lat_ref.shape[0] - 1)
        z_ref[slot, k * CL : (k + 1) * CL, :] = lat_ref[src]


def set_weights(win_ref, bias_ref, wcat_ref):
    for k in range(TAPS):
        wcat_ref[k * CL : (k + 1) * CL, :] = win_ref[k]
    bias = bias_ref[...]
    high = bias.astype(BF)
    rest = bias - high.astype(F32)
    mid = rest.astype(BF)
    low = (rest - mid.astype(F32)).astype(BF)
    row = lax.broadcasted_iota(jnp.int32, (CL, C), 0)
    tail = jnp.where(row == 0, high.astype(F32), 0.0)
    tail = jnp.where(row == 1, mid.astype(F32), tail)
    tail = jnp.where(row == 2, low.astype(F32), tail)
    wcat_ref[TAPS * CL :, :] = tail.astype(BF)


def half_of(clip_ref, first, all_ref, z_ref, wcol, slot, frame):
    load_taps(clip_ref, first, all_ref, z_ref, slot, frame, SLAB)
    z_ref[slot, TAPS * CL :, :] = jnp.ones((CL, PX), BF)
    h = mm(wcol, z_ref[slot], 1, 0)
    return h, jnp.tanh(h) + 1.0


def slope_of(act, twice):
    sig = 0.5 * twice
    return sig + act * (1.0 - sig)


def k_first(
    clip_ref, prev_ref, lat_ref, win_ref, bias_ref, acc_ref,
    act_ref, part_ref, halo_ref, icg_ref, wcol_ref,
    all_ref, z_ref, wcat_ref, lacc_ref,
):
    first = lax.axis_index("tm") * SLAB
    all_ref[:SLAB] = prev_ref[...]
    all_ref[SLAB:] = lat_ref[...]
    set_weights(win_ref, bias_ref, wcat_ref)
    wcol = (wcat_ref[...].astype(F32) * 0.5).astype(BF).T
    wcol_ref[...] = wcol
    lacc_ref[...] = jnp.zeros_like(lacc_ref)
    icg = jnp.zeros((E, C), F32)
    for t in range(2):
        h, twice = half_of(clip_ref, first, all_ref, z_ref, wcol, t, t)
        act = h * twice
        act_ref[t] = act.astype(BF)
        gp = (acc_ref[t] * slope_of(act, twice)).astype(BF)
        back = mm(wcat_ref[...], gp, 1, 0)
        for k in range(TAPS):
            src = source(clip_ref, first, t, k) + 2
            lacc_ref[src] += back[k * CL : (k + 1) * CL]
        icg = icg + mm(z_ref[t], gp, 1, 1)
    halo_ref[...] = lacc_ref[:2]
    part_ref[...] = lacc_ref[2:]
    icg_ref[...] = icg


def k_rest(clip_ref, prev_ref, lat_ref, wcol_ref, act01_ref, act_ref, slope_ref, all_ref, z_ref):
    first = lax.axis_index("tm") * SLAB
    all_ref[:SLAB] = prev_ref[...]
    all_ref[SLAB:] = lat_ref[...]
    wcol = wcol_ref[...]
    act_ref[2:4] = act01_ref[...]
    for j in range(2):
        h, twice = half_of(clip_ref, first, all_ref, z_ref, wcol, j, j - 2)
        act_ref[j] = (h * twice).astype(BF)
    for j in range(2, SLAB):
        h, twice = half_of(clip_ref, first, all_ref, z_ref, wcol, j, j)
        act = h * twice
        act_ref[j + 2] = act.astype(BF)
        slope_ref[j - 2] = slope_of(act, twice)


def k_weight(clip_ref, grad_ref, act_ref, keep_ref, send_ref, acc_ref):
    first = lax.axis_index("tm") * SLAB
    core = lax.axis_index("tm") % 2
    for k in range(TAPS):
        total = None
        for t in range(SLAB):
            src = jnp.maximum(source(clip_ref, first, t, k), -2) + 2
            part = mm(grad_ref[t], act_ref[src], 1, 1)
            total = part if total is None else total + part
        acc_ref[:, :, :, k * C : (k + 1) * C] = total.reshape(16, 2, 16, C)
    upper = lax.broadcasted_iota(jnp.int32, (32, 8, 128), 1) < 4
    for ref, half in ((keep_ref, core), (send_ref, 1 - core)):
        for jj in range(0, TAPS * C // 128, 4):
            even, odd = [], []
            for h in range(2):
                at = (jj + 2 * h) * 128
                a = acc_ref[:, half, :, at : at + 128].reshape(32, 8, 128)
                b = acc_ref[:, half, :, at + 128 : at + 256].reshape(32, 8, 128)
                even.append(jnp.where(upper, a, pltpu.roll(b, 4, 1)))
                odd.append(jnp.where(upper, pltpu.roll(a, 4, 1), b))
            ref[:, 0, jj * 4 : jj * 4 + 16, :] = jnp.concatenate(even, axis=1).astype(BF)
            ref[:, 1, jj * 4 : jj * 4 + 16, :] = jnp.concatenate(odd, axis=1).astype(BF)


def k_second(
    clip_ref, next_ref, lat_ref, win_ref, conv_ref, acc_in_ref, slope_ref, part_ref, halo_ref, icg_in_ref, after_ref,
    tok0_ref, tok1_ref, tok2_ref, tok3_ref, icg_ref, passed_ref, acc_ref, z_ref, wcat_ref, lacc_ref, icg_acc, low_ref,
):
    first = lax.axis_index("tm") * SLAB
    start = [clip_rel(clip_ref, first, SLAB + t) for t in range(2)]
    for k in range(TAPS):
        wcat_ref[k * CL : (k + 1) * CL, :] = win_ref[k]
    acc_ref[0] = acc_in_ref[2] + mm(conv_ref[2], only(start[0] <= 2, next_ref[0]), 0, 0)
    acc_ref[1] = (
        acc_in_ref[3]
        + mm(conv_ref[1], only(start[0] <= 3, next_ref[0]), 0, 0)
        + mm(conv_ref[2], only(start[1] <= 3, next_ref[1]), 0, 0)
    )

    @pl.when((clip_rel(clip_ref, first, 3) == 3) & (start[0] <= 3))
    def _():
        acc_ref[1] += mm(conv_ref[2], next_ref[0], 0, 0)

    lacc_ref[:SLAB] = part_ref[...]
    lacc_ref[2:SLAB] += halo_ref[...]
    icg = icg_in_ref[...]
    for t in range(2):
        gp = (acc_ref[t] * slope_ref[t]).astype(BF)
        load_taps(clip_ref, first, lat_ref, z_ref, t, t + 2, 0)
        z_ref[t, TAPS * CL :, :] = jnp.ones((CL, PX), BF)
        back = mm(wcat_ref[...], gp, 1, 0)
        for k in range(TAPS):
            src = source(clip_ref, first, t + 2, k)
            lacc_ref[src] += back[k * CL : (k + 1) * CL]
        icg = icg + mm(z_ref[t], gp, 1, 1)
    icg_acc[...] = icg
    for f in range(SLAB):
        low_ref[f * CL : (f + 1) * CL, :] = lacc_ref[f].astype(BF)
    r = lax.broadcasted_iota(jnp.int32, (PX, 1), 0)
    c = lax.broadcasted_iota(jnp.int32, (PX, PX), 1)
    pick = (((r & 3) << 7) + (r >> 2) == c).astype(F32).astype(BF)
    low_ref[...] = mm(low_ref[...], pick, 1, 0).astype(BF)
    z = lax.axis_index("seq")
    for k, ref in enumerate((tok0_ref, tok1_ref, tok2_ref, tok3_ref)):
        ref[...] = low_ref[pl.ds(pl.multiple_of(lax.rem(z + k, 4) * CL, CL), CL), :]
    for rb in range(4):
        for lb in range(4):
            icg_ref[rb * 4 + lb] = icg_acc[rb * 16 : (rb + 1) * 16, lb * 128 : (lb + 1) * 128].astype(BF)


def k_grad(
    tok0_ref, tok1_ref, tok2_ref, tok3_ref, normed_ref, icg_ref, keep_ref, other_ref,
    pack_ref, tok_hbm, raw_ref, recv_ref, tok_ref, sem,
):
    z = lax.axis_index("seq")
    for k, ref in enumerate((tok0_ref, tok1_ref, tok2_ref, tok3_ref)):
        recv_ref[lax.rem(z + 4 - k, 4)] = ref[...]
    for s in range(4):
        for q in range(EDGE):
            raw_ref[q * CL : (q + 1) * CL, s * 128 : (s + 1) * 128] = recv_ref[
                s, :, q * 128 : (q + 1) * 128
            ]
    r = lax.broadcasted_iota(jnp.int32, (E, E), 0)
    c = lax.broadcasted_iota(jnp.int32, (E, E), 1)
    order = (((r & 3) << 4) + (r >> 2) == c).astype(F32).astype(BF)
    tok = mm(order, raw_ref[...], 1, 0)
    tok_ref[...] = tok.astype(BF)
    copy = pltpu.make_async_copy(tok_ref, tok_hbm, sem)
    copy.start()
    total = jnp.broadcast_to(jnp.sum(tok, axis=1, keepdims=True), (E, 128)).astype(BF)
    for lb in range(D // 512):
        g = mm(tok_ref[...], normed_ref[:, lb * 512 : (lb + 1) * 512], 1, 0).astype(BF)
        for u in range(4):
            for rb in range(4):
                pack_ref[rb * 24 + lb * 4 + u, :16, :] = g[rb * 16 : (rb + 1) * 16, u * 128 : (u + 1) * 128]
    pack_ref[96:112, :16, :] = icg_ref[...]
    for rb in range(4):
        pack_ref[112 + rb, :16, :] = total[rb * 16 : (rb + 1) * 16]
    pack_ref[116:, :16, :] = jnp.zeros((12, 16, 128), BF)
    for xy in range(16):
        for half in range(2):
            at = pl.ds((xy * 2 + half) * 4, 4)
            rows = slice(half * 24, half * 24 + 24)
            both = keep_ref[xy * 4 : xy * 4 + 4].astype(F32) + other_ref[xy * 4 : xy * 4 + 4].astype(F32)
            pack_ref[at, 16:, :] = both[:, rows, :].astype(BF)
    copy.wait()


def k_hidden(tok_ref, hidden_ref, wt_ref, mod_ref, out_ref):
    gain = 1.0 / D
    h = hidden_ref[...].astype(F32)
    center = h - jnp.sum(h, axis=1, keepdims=True) * gain
    var = jnp.sum(center * center, axis=1, keepdims=True) * gain
    inv = lax.rsqrt(var + 1e-06)
    normed = center * inv
    mod_in = mm(tok_ref[...].T, wt_ref[...], 1, 0)
    ng = mod_in * (1.0 + mod_ref[1:2, :])
    m1 = jnp.sum(ng, axis=1, keepdims=True) * gain
    m2 = jnp.sum(ng * normed, axis=1, keepdims=True) * gain
    out_ref[...] = (inv * (ng - m1 - normed * m2)).astype(BF)


def k_sum(recv_ref, out_hbm, keep_ref, send_hbm, out_ref, send_ref, sems):
    core = lax.axis_index("tm") % 2
    total = jnp.sum(recv_ref[:, :16, :].astype(F32), axis=0).astype(BF)
    out_ref[...] = jnp.broadcast_to(total[None], out_ref.shape)
    copy = pltpu.make_async_copy(out_ref, out_hbm, sems.at[0])
    copy.start()
    sums = [jnp.zeros((24, 128), F32)] * 2
    for d in range(128):
        c = (d // 4) % 2
        sums[c] = sums[c] + recv_ref[d, 16:, :].astype(F32)
    keep_ref[...] = jnp.where(core == 0, sums[0], sums[1])
    send_ref[...] = jnp.where(core == 0, sums[1], sums[0])
    away = pltpu.make_async_copy(send_ref, send_hbm, sems.at[1])
    away.start()
    copy.wait()
    away.wait()


def k_last(all_ref, wt_ref, mod_ref, final_ref, modg_ref, icg_ref, bias_ref):
    tot = [all_ref[112 + rb].astype(F32) for rb in range(4)]
    for lb in range(D // 128):
        at = slice(lb * 128, (lb + 1) * 128)
        scale = 1.0 + mod_ref[1:2, at]
        shift = mod_ref[0:1, at]
        s0 = jnp.zeros((1, 128), F32)
        s1 = jnp.zeros((1, 128), F32)
        for rb in range(4):
            rows = slice(rb * 16, (rb + 1) * 16)
            g = all_ref[rb * 24 + lb].astype(F32)
            w = wt_ref[rows, at].astype(F32)
            final_ref[rows, at] = g * scale + shift * tot[rb]
            s0 = s0 + jnp.sum(w * tot[rb], axis=0, keepdims=True)
            s1 = s1 + jnp.sum(w * g, axis=0, keepdims=True)
        modg_ref[0:1, at] = s0
        modg_ref[1:2, at] = s1
    for rb in range(3):
        for lb in range(4):
            icg_ref[rb * 16 : (rb + 1) * 16, lb * 128 : (lb + 1) * 128] = all_ref[96 + rb * 4 + lb].astype(F32)
    for lb in range(4):
        bias_ref[:, lb * 128 : (lb + 1) * 128] = all_ref[96 + 12 + lb].astype(F32)[0:1]


def k_weight_out(keep_ref, other_ref, wt_ref, mod_ref, out_ref, wt_near_ref, mod_near_ref):
    wt_near_ref[...] = wt_ref[...]
    mod_near_ref[...] = mod_ref[...]
    core = lax.axis_index("tm") % 2
    mine, other = keep_ref[...], other_ref[...]
    halves = [jnp.where(core == 0, mine, other), jnp.where(core == 0, other, mine)]
    for j in range(12):
        rows = halves[j // 6][(j % 6) * 4 : (j % 6) * 4 + 4]
        out_ref[j // 4, :, (j % 4) * 128 : (j % 4 + 1) * 128] = rows


def call(fn, outs, specs, scratch=(), mib=40, est=None, name=None):
    return pl.pallas_call(
        fn,
        out_shape=outs,
        in_specs=specs,
        out_specs=jax.tree.map(lambda _: VMEM, outs),
        scratch_shapes=list(scratch),
        compiler_params=params(mib),
        cost_estimate=est,
        name=name,
    )


def sds(shape, dtype):
    return jax.ShapeDtypeStruct(shape, dtype)


def pinned(*arrays):
    return [pltpu.with_memory_space_constraint(a, pltpu.HBM) for a in arrays]


def shifted(block, distance):
    n = lax.axis_size("tm")
    route = [(i - distance, i) for i in range(n) if 0 <= i - distance < n]
    return lax.ppermute(block, "tm", route)


def swapped(block):
    return lax.ppermute(block, "tm", [(i, i ^ 1) for i in range(lax.axis_size("tm"))])


def exchange(block, axes):
    return lax.all_to_all(block, axes, split_axis=0, concat_axis=0, tiled=True)


def local(latents, hidden, grad_out, conv_in_w, conv_in_b, conv_w, final_w, modulation, clip_start):
    win = conv_in_w.transpose(0, 2, 1)
    wt = final_w.T
    bias = conv_in_b.reshape(1, C)
    lat_prev = shifted(latents, 1)
    unit = 2 * C * C * PX
    grad_sent = grad_out[:2]
    grad_next = shifted(grad_sent, -1)
    acc = call(
        k_back, sds((SLAB, C, PX), F32), [PIN, PIN, VMEM, PIN],
        [
            pltpu.SMEM((FRAMES,), jnp.int32), pltpu.VMEM((TAPS, C, C), BF), pltpu.VMEM((SLAB, C, PX), BF),
            pltpu.SemaphoreType.DMA((4,)),
        ],
        mib=16, est=cost(1 << 10, 1 << 10), name="back",
    )(*pinned(clip_start, conv_w), grad_sent, *pinned(grad_out))
    act01, part, halo, icg_part, wcol = call(
        k_first,
        (
            sds((2, C, PX), BF), sds((SLAB, CL, PX), F32), sds((2, CL, PX), F32), sds((E, C), F32), sds((C, E), BF),
        ),
        [SMEM] + [VMEM] * 5,
        [
            pltpu.VMEM((2 * SLAB, CL, PX), BF), pltpu.VMEM((2, E, PX), BF), pltpu.VMEM((E, C), BF),
            pltpu.VMEM((SLAB + 2, CL, PX), F32),
        ],
        mib=16, est=cost(2 * unit, 5 << 20), name="first",
    )(clip_start, lat_prev, latents, win, bias, acc)
    halo_recv = shifted(halo, -1)
    act, slope = call(
        k_rest, (sds((SLAB + 2, C, PX), BF), sds((2, C, PX), F32)), [SMEM] + [VMEM] * 4,
        [pltpu.VMEM((2 * SLAB, CL, PX), BF), pltpu.VMEM((SLAB, E, PX), BF)],
        mib=16, est=cost(2 * unit, 8 << 20), name="rest",
    )(clip_start, lat_prev, latents, wcol, act01)
    keep, send = call(
        k_weight, (sds((32, 2, 48, 128), BF),) * 2, [SMEM] + [VMEM] * 2,
        [pltpu.VMEM((16, 2, 16, TAPS * C), F32)], mib=16, est=cost(50 * unit, 7 << 20), name="weight",
    )(clip_start, grad_out, act)
    piece = sds((CL, PX), BF)
    half = sds((32, 2, 48, 128), BF)
    *tok_parts, icg_blocks, send = pl.pallas_call(
        k_second,
        out_shape=(piece,) * 4 + (sds((16, 16, 128), BF), half),
        in_specs=[SMEM] + [VMEM] * 9 + [HERE],
        out_specs=(VMEM,) * 5 + (HERE,),
        scratch_shapes=[
            pltpu.VMEM((2, C, PX), F32), pltpu.VMEM((2, E, PX), BF), pltpu.VMEM((TAPS * CL, C), BF),
            pltpu.VMEM((SLAB, CL, PX), F32), pltpu.VMEM((E, C), F32), pltpu.VMEM((SLAB * CL, PX), BF),
        ],
        input_output_aliases={10: 5},
        compiler_params=params(16),
        cost_estimate=cost(6 * unit, 8 << 20),
        name="second",
    )(clip_start, grad_next, latents, win, conv_w, acc, slope, part, halo_recv, icg_part, send)
    toks = [tok_parts[0]] + [
        lax.ppermute(tok_parts[k], "seq", [(i, (i + k) % 4) for i in range(4)]) for k in range(1, 4)
    ]
    other = swapped(send)
    normed = call(
        k_prep, sds((NTOK, D), BF), [VMEM, HERE], mib=16, est=cost(10 * NTOK * D, 6 << 20), name="prep"
    )(hidden, icg_blocks)
    pack, tok = pl.pallas_call(
        k_grad,
        out_shape=(sds((128, 40, 128), BF), pltpu.HBM((E, NTOK), BF)),
        in_specs=[VMEM] * 8,
        out_specs=(VMEM, PIN),
        scratch_shapes=[
            pltpu.VMEM((E, NTOK), BF), pltpu.VMEM((4, CL, PX), BF), pltpu.VMEM((E, NTOK), BF),
            pltpu.SemaphoreType.DMA,
        ],
        compiler_params=params(16),
        cost_estimate=cost(2 * NTOK * D * E, 5 << 20),
        name="grad",
    )(*toks, normed, icg_blocks, keep.reshape(64, 48, 128), other.reshape(64, 48, 128))
    recv = exchange(pack, BOTH)
    hidden_grad = pl.pallas_call(
        k_hidden,
        grid=(4,),
        out_shape=sds((NTOK, D), BF),
        in_specs=[
            pl.BlockSpec((E, 128), lambda i: (0, i)),
            pl.BlockSpec((128, D), lambda i: (i, 0)),
            pl.BlockSpec((E, D), lambda i: (0, 0)),
            pl.BlockSpec((2, D), lambda i: (0, 0)),
        ],
        out_specs=pl.BlockSpec((128, D), lambda i: (i, 0)),
        compiler_params=params(16),
        cost_estimate=cost(2 * NTOK * D * E, 6 << 20),
        name="hidden",
    )(tok, hidden, wt, modulation)
    copies, own, away = pl.pallas_call(
        k_sum,
        out_shape=(pltpu.HBM((128, 16, 128), BF), sds((24, 128), F32), pltpu.HBM((24, 128), F32)),
        in_specs=[VMEM],
        out_specs=(PIN, VMEM, PIN),
        scratch_shapes=[
            pltpu.VMEM((128, 16, 128), BF), pltpu.VMEM((24, 128), F32), pltpu.SemaphoreType.DMA((2,)),
        ],
        compiler_params=params(16),
        cost_estimate=cost(1 << 20, 2 << 20),
        name="sum",
    )(recv)
    everything = exchange(copies, BOTH)
    weight_grad, wt_near, mod_near = call(
        k_weight_out, (sds((TAPS, 4, C), F32), sds((E, D), BF), sds((2, D), F32)), [VMEM] * 4,
        mib=16, est=cost(1 << 12, 1 << 16), name="weight_out",
    )(own, swapped(away), wt, modulation)
    final_t, mod_grad, icg, bias_grad = call(
        k_last, (sds((E, D), F32), sds((2, D), F32), sds((TAPS * CL, C), F32), sds((1, C), F32)), [VMEM] * 3,
        mib=16, est=cost(1 << 20, 2 << 20), name="last",
    )(everything, wt_near, mod_near)
    return (
        hidden_grad,
        weight_grad.transpose(1, 0, 2),
        icg.reshape(TAPS, CL, C).transpose(0, 2, 1),
        bias_grad.reshape(C),
        final_t.T,
        mod_grad,
    )


def solution(mesh):
    return jax.shard_map(
        local,
        mesh=mesh,
        in_specs=(
            P("tm", None, "seq"),
            P(("tm", "seq"), None),
            P("tm", None, "seq"),
            P(), P(), P(), P(), P(), P(),
        ),
        out_specs=(P(("tm", "seq"), None), P(("tm", "seq"), None, None), P(), P(), P(), P()),
        check_vma=False,
    )
```

```python
import jax
import jax.numpy as jnp
from jax import lax
from jax.experimental import pallas as pl
from jax.experimental.pallas import tpu as pltpu
from jax.sharding import PartitionSpec as P

BF = jnp.bfloat16
F32 = jnp.float32
VMEM = pl.BlockSpec(memory_space=pltpu.VMEM)
SMEM = pl.BlockSpec(memory_space=pltpu.SMEM)
HERE = pl.BlockSpec(memory_space=pl.ANY)
PIN = pl.BlockSpec(memory_space=pltpu.HBM)
EDGE = 4
TAPS = 3
SLAB = 4
CL = 16
C = 512
PX = 512
D = 3072
E = 64
NTOK = 512
FRAMES = 128
BOTH = ("tm", "seq")


def params(mib):
    return pltpu.CompilerParams(vmem_limit_bytes=mib * 1024 * 1024)


def cost(flops, nbytes, trans=0):
    return pl.CostEstimate(flops=flops, bytes_accessed=nbytes, transcendentals=trans)


def mm(a, b, ca, cb):
    return lax.dot_general(a, b, (((ca,), (cb,)), ((), ())), preferred_element_type=F32)


def clip_rel(clip_ref, first, frame):
    whole = first + frame
    start = clip_ref[jnp.clip(whole, 0, FRAMES - 1)]
    return jnp.where(whole >= FRAMES, frame, start - first)


def source(clip_ref, first, frame, tap):
    return jnp.maximum(frame - tap, clip_rel(clip_ref, first, frame))


def k_prep(hidden_ref, after_ref, normed_ref):
    gain = 1.0 / D

    def rows(i, _):
        at = pl.ds(pl.multiple_of(i * 64, 64), 64)
        h = hidden_ref[at, :].astype(F32)
        center = h - jnp.sum(h, axis=1, keepdims=True) * gain
        var = jnp.sum(center * center, axis=1, keepdims=True) * gain
        normed_ref[at, :] = (center * lax.rsqrt(var + 1e-06)).astype(BF)
        return 0

    lax.fori_loop(0, NTOK // 64, rows, 0)


def only(keep, value):
    return jnp.where(keep, value, jnp.zeros_like(value))


def k_back(clip_hbm, conv_hbm, sent_ref, grad_hbm, acc_ref, clip_ref, conv_ref, grad_ref, sems):
    copies = [
        pltpu.make_async_copy(conv_hbm.at[0], conv_ref.at[0], sems.at[0]),
        pltpu.make_async_copy(clip_hbm, clip_ref, sems.at[1]),
        pltpu.make_async_copy(conv_hbm.at[pl.ds(1, 2)], conv_ref.at[pl.ds(1, 2)], sems.at[2]),
        pltpu.make_async_copy(grad_hbm.at[pl.ds(2, 2)], grad_ref.at[pl.ds(2, 2)], sems.at[3]),
    ]
    for copy in copies:
        copy.start()
    grad_ref[:2] = sent_ref[...]
    first = lax.axis_index("tm") * SLAB
    copies[0].wait()
    for s in range(2):
        acc_ref[s] = mm(conv_ref[0], grad_ref[s], 0, 0)
    for copy in copies[1:]:
        copy.wait()
    start = [clip_rel(clip_ref, first, t) for t in range(SLAB)]
    for s in range(SLAB):
        total = acc_ref[s] if s < 2 else mm(conv_ref[0], grad_ref[s], 0, 0)
        for k in range(1, min(TAPS, SLAB - s)):
            total = total + mm(conv_ref[k], only(start[s + k] <= s, grad_ref[s + k]), 0, 0)
        acc_ref[s] = total

    def opens(s, _):
        @pl.when(clip_rel(clip_ref, first, s) == s)
        def _():
            later = jnp.minimum(s + 1, SLAB - 1)
            keep = (s + 1 < SLAB) & (clip_rel(clip_ref, first, s + 1) <= s)
            acc_ref[s] += (
                mm(conv_ref[1], grad_ref[s], 0, 0)
                + mm(conv_ref[2], grad_ref[s], 0, 0)
                + mm(conv_ref[2], only(keep, grad_ref[later]), 0, 0)
            )

        return 0

    lax.fori_loop(0, SLAB, opens, 0)


def load_taps(clip_ref, first, lat_ref, z_ref, slot, frame, base):
    for k in range(TAPS):
        src = jnp.clip(source(clip_ref, first, frame, k) + base, 0, lat_ref.shape[0] - 1)
        z_ref[slot, k * CL : (k + 1) * CL, :] = lat_ref[src]


def set_weights(win_ref, bias_ref, wcat_ref):
    for k in range(TAPS):
        wcat_ref[k * CL : (k + 1) * CL, :] = win_ref[k]
    bias = bias_ref[...]
    high = bias.astype(BF)
    rest = bias - high.astype(F32)
    mid = rest.astype(BF)
    low = (rest - mid.astype(F32)).astype(BF)
    row = lax.broadcasted_iota(jnp.int32, (CL, C), 0)
    tail = jnp.where(row == 0, high.astype(F32), 0.0)
    tail = jnp.where(row == 1, mid.astype(F32), tail)
    tail = jnp.where(row == 2, low.astype(F32), tail)
    wcat_ref[TAPS * CL :, :] = tail.astype(BF)


def half_of(clip_ref, first, all_ref, z_ref, wcol, slot, frame):
    load_taps(clip_ref, first, all_ref, z_ref, slot, frame, SLAB)
    z_ref[slot, TAPS * CL :, :] = jnp.ones((CL, PX), BF)
    h = mm(wcol, z_ref[slot], 1, 0)
    return h, jnp.tanh(h) + 1.0


def slope_of(act, twice):
    sig = 0.5 * twice
    return sig + act * (1.0 - sig)


def k_first(
    clip_ref, prev_ref, lat_ref, win_ref, bias_ref, acc_ref,
    act_ref, part_ref, halo_ref, icg_ref, wcol_ref,
    all_ref, z_ref, wcat_ref, lacc_ref,
):
    first = lax.axis_index("tm") * SLAB
    all_ref[:SLAB] = prev_ref[...]
    all_ref[SLAB:] = lat_ref[...]
    set_weights(win_ref, bias_ref, wcat_ref)
    wcol = (wcat_ref[...].astype(F32) * 0.5).astype(BF).T
    wcol_ref[...] = wcol
    lacc_ref[...] = jnp.zeros_like(lacc_ref)
    icg = jnp.zeros((E, C), F32)
    for t in range(2):
        h, twice = half_of(clip_ref, first, all_ref, z_ref, wcol, t, t)
        act = h * twice
        act_ref[t] = act.astype(BF)
        gp = (acc_ref[t] * slope_of(act, twice)).astype(BF)
        back = mm(wcat_ref[...], gp, 1, 0)
        for k in range(TAPS):
            src = source(clip_ref, first, t, k) + 2
            lacc_ref[src] += back[k * CL : (k + 1) * CL]
        icg = icg + mm(z_ref[t], gp, 1, 1)
    halo_ref[...] = lacc_ref[:2]
    part_ref[...] = lacc_ref[2:]
    icg_ref[...] = icg


def k_rest(clip_ref, prev_ref, lat_ref, wcol_ref, act01_ref, act_ref, slope_ref, all_ref, z_ref):
    first = lax.axis_index("tm") * SLAB
    all_ref[:SLAB] = prev_ref[...]
    all_ref[SLAB:] = lat_ref[...]
    wcol = wcol_ref[...]
    act_ref[2:4] = act01_ref[...]
    for j in range(2):
        h, twice = half_of(clip_ref, first, all_ref, z_ref, wcol, j, j - 2)
        act_ref[j] = (h * twice).astype(BF)
    for j in range(2, SLAB):
        h, twice = half_of(clip_ref, first, all_ref, z_ref, wcol, j, j)
        act = h * twice
        act_ref[j + 2] = act.astype(BF)
        slope_ref[j - 2] = slope_of(act, twice)


def k_weight(clip_ref, grad_ref, act_ref, keep_ref, send_ref, acc_ref):
    first = lax.axis_index("tm") * SLAB
    core = lax.axis_index("tm") % 2
    for k in range(TAPS):
        total = None
        for t in range(SLAB):
            src = jnp.maximum(source(clip_ref, first, t, k), -2) + 2
            part = mm(grad_ref[t], act_ref[src], 1, 1)
            total = part if total is None else total + part
        acc_ref[:, :, :, k * C : (k + 1) * C] = total.reshape(16, 2, 16, C)
    upper = lax.broadcasted_iota(jnp.int32, (32, 8, 128), 1) < 4
    for ref, half in ((keep_ref, core), (send_ref, 1 - core)):
        for jj in range(0, TAPS * C // 128, 4):
            even, odd = [], []
            for h in range(2):
                at = (jj + 2 * h) * 128
                a = acc_ref[:, half, :, at : at + 128].reshape(32, 8, 128)
                b = acc_ref[:, half, :, at + 128 : at + 256].reshape(32, 8, 128)
                even.append(jnp.where(upper, a, pltpu.roll(b, 4, 1)))
                odd.append(jnp.where(upper, pltpu.roll(a, 4, 1), b))
            ref[:, 0, jj * 4 : jj * 4 + 16, :] = jnp.concatenate(even, axis=1).astype(BF)
            ref[:, 1, jj * 4 : jj * 4 + 16, :] = jnp.concatenate(odd, axis=1).astype(BF)


def k_second(
    clip_ref, next_ref, lat_ref, win_ref, conv_ref, acc_in_ref, slope_ref, part_ref, halo_ref, icg_in_ref, after_ref,
    tok0_ref, tok1_ref, tok2_ref, tok3_ref, icg_ref, passed_ref, acc_ref, z_ref, wcat_ref, lacc_ref, icg_acc, low_ref,
):
    first = lax.axis_index("tm") * SLAB
    start = [clip_rel(clip_ref, first, SLAB + t) for t in range(2)]
    for k in range(TAPS):
        wcat_ref[k * CL : (k + 1) * CL, :] = win_ref[k]
    acc_ref[0] = acc_in_ref[2] + mm(conv_ref[2], only(start[0] <= 2, next_ref[0]), 0, 0)
    acc_ref[1] = (
        acc_in_ref[3]
        + mm(conv_ref[1], only(start[0] <= 3, next_ref[0]), 0, 0)
        + mm(conv_ref[2], only(start[1] <= 3, next_ref[1]), 0, 0)
    )

    @pl.when((clip_rel(clip_ref, first, 3) == 3) & (start[0] <= 3))
    def _():
        acc_ref[1] += mm(conv_ref[2], next_ref[0], 0, 0)

    lacc_ref[:SLAB] = part_ref[...]
    lacc_ref[2:SLAB] += halo_ref[...]
    icg = icg_in_ref[...]
    for t in range(2):
        gp = (acc_ref[t] * slope_ref[t]).astype(BF)
        load_taps(clip_ref, first, lat_ref, z_ref, t, t + 2, 0)
        z_ref[t, TAPS * CL :, :] = jnp.ones((CL, PX), BF)
        back = mm(wcat_ref[...], gp, 1, 0)
        for k in range(TAPS):
            src = source(clip_ref, first, t + 2, k)
            lacc_ref[src] += back[k * CL : (k + 1) * CL]
        icg = icg + mm(z_ref[t], gp, 1, 1)
    icg_acc[...] = icg
    for f in range(SLAB):
        low_ref[f * CL : (f + 1) * CL, :] = lacc_ref[f].astype(BF)
    r = lax.broadcasted_iota(jnp.int32, (PX, 1), 0)
    c = lax.broadcasted_iota(jnp.int32, (PX, PX), 1)
    pick = (((r & 3) << 7) + (r >> 2) == c).astype(F32).astype(BF)
    low_ref[...] = mm(low_ref[...], pick, 1, 0).astype(BF)
    z = lax.axis_index("seq")
    for k, ref in enumerate((tok0_ref, tok1_ref, tok2_ref, tok3_ref)):
        ref[...] = low_ref[pl.ds(pl.multiple_of(lax.rem(z + k, 4) * CL, CL), CL), :]
    for rb in range(4):
        for lb in range(4):
            icg_ref[rb * 4 + lb] = icg_acc[rb * 16 : (rb + 1) * 16, lb * 128 : (lb + 1) * 128].astype(BF)


def k_grad(
    tok0_ref, tok1_ref, tok2_ref, tok3_ref, normed_ref, icg_ref, keep_ref, other_ref,
    pack_ref, tok_hbm, raw_ref, recv_ref, tok_ref, sem,
):
    z = lax.axis_index("seq")
    for k, ref in enumerate((tok0_ref, tok1_ref, tok2_ref, tok3_ref)):
        recv_ref[lax.rem(z + 4 - k, 4)] = ref[...]
    for s in range(4):
        for q in range(EDGE):
            raw_ref[q * CL : (q + 1) * CL, s * 128 : (s + 1) * 128] = recv_ref[
                s, :, q * 128 : (q + 1) * 128
            ]
    r = lax.broadcasted_iota(jnp.int32, (E, E), 0)
    c = lax.broadcasted_iota(jnp.int32, (E, E), 1)
    order = (((r & 3) << 4) + (r >> 2) == c).astype(F32).astype(BF)
    tok = mm(order, raw_ref[...], 1, 0)
    tok_ref[...] = tok.astype(BF)
    copy = pltpu.make_async_copy(tok_ref, tok_hbm, sem)
    copy.start()
    total = jnp.broadcast_to(jnp.sum(tok, axis=1, keepdims=True), (E, 128)).astype(BF)
    for lb in range(D // 512):
        g = mm(tok_ref[...], normed_ref[:, lb * 512 : (lb + 1) * 512], 1, 0).astype(BF)
        for u in range(4):
            for rb in range(4):
                pack_ref[rb * 24 + lb * 4 + u, :16, :] = g[rb * 16 : (rb + 1) * 16, u * 128 : (u + 1) * 128]
    pack_ref[96:112, :16, :] = icg_ref[...]
    for rb in range(4):
        pack_ref[112 + rb, :16, :] = total[rb * 16 : (rb + 1) * 16]
    pack_ref[116:, :16, :] = jnp.zeros((12, 16, 128), BF)
    for xy in range(16):
        for half in range(2):
            at = pl.ds((xy * 2 + half) * 4, 4)
            rows = slice(half * 24, half * 24 + 24)
            both = keep_ref[xy * 4 : xy * 4 + 4].astype(F32) + other_ref[xy * 4 : xy * 4 + 4].astype(F32)
            pack_ref[at, 16:, :] = both[:, rows, :].astype(BF)
    copy.wait()


def k_hidden(tok_ref, hidden_ref, wt_ref, mod_ref, out_ref):
    gain = 1.0 / D
    h = hidden_ref[...].astype(F32)
    center = h - jnp.sum(h, axis=1, keepdims=True) * gain
    var = jnp.sum(center * center, axis=1, keepdims=True) * gain
    inv = lax.rsqrt(var + 1e-06)
    normed = center * inv
    mod_in = mm(tok_ref[...].T, wt_ref[...], 1, 0)
    ng = mod_in * (1.0 + mod_ref[1:2, :])
    m1 = jnp.sum(ng, axis=1, keepdims=True) * gain
    m2 = jnp.sum(ng * normed, axis=1, keepdims=True) * gain
    out_ref[...] = (inv * (ng - m1 - normed * m2)).astype(BF)


def k_sum(recv_ref, out_hbm, keep_ref, send_hbm, out_ref, send_ref, sems):
    core = lax.axis_index("tm") % 2
    total = jnp.sum(recv_ref[:, :16, :].astype(F32), axis=0).astype(BF)
    out_ref[...] = jnp.broadcast_to(total[None], out_ref.shape)
    copy = pltpu.make_async_copy(out_ref, out_hbm, sems.at[0])
    copy.start()
    sums = [jnp.zeros((24, 128), F32)] * 2
    for d in range(128):
        c = (d // 4) % 2
        sums[c] = sums[c] + recv_ref[d, 16:, :].astype(F32)
    keep_ref[...] = jnp.where(core == 0, sums[0], sums[1])
    send_ref[...] = jnp.where(core == 0, sums[1], sums[0])
    away = pltpu.make_async_copy(send_ref, send_hbm, sems.at[1])
    away.start()
    copy.wait()
    away.wait()


def k_last(all_ref, wt_ref, mod_ref, final_ref, modg_ref, icg_ref, bias_ref):
    tot = [all_ref[112 + rb].astype(F32) for rb in range(4)]
    for lb in range(D // 128):
        at = slice(lb * 128, (lb + 1) * 128)
        scale = 1.0 + mod_ref[1:2, at]
        shift = mod_ref[0:1, at]
        s0 = jnp.zeros((1, 128), F32)
        s1 = jnp.zeros((1, 128), F32)
        for rb in range(4):
            rows = slice(rb * 16, (rb + 1) * 16)
            g = all_ref[rb * 24 + lb].astype(F32)
            w = wt_ref[rows, at].astype(F32)
            final_ref[rows, at] = g * scale + shift * tot[rb]
            s0 = s0 + jnp.sum(w * tot[rb], axis=0, keepdims=True)
            s1 = s1 + jnp.sum(w * g, axis=0, keepdims=True)
        modg_ref[0:1, at] = s0
        modg_ref[1:2, at] = s1
    for rb in range(3):
        for lb in range(4):
            icg_ref[rb * 16 : (rb + 1) * 16, lb * 128 : (lb + 1) * 128] = all_ref[96 + rb * 4 + lb].astype(F32)
    for lb in range(4):
        bias_ref[:, lb * 128 : (lb + 1) * 128] = all_ref[96 + 12 + lb].astype(F32)[0:1]


def k_weight_out(keep_ref, other_ref, wt_ref, mod_ref, out_ref, wt_near_ref, mod_near_ref):
    wt_near_ref[...] = wt_ref[...]
    mod_near_ref[...] = mod_ref[...]
    core = lax.axis_index("tm") % 2
    mine, other = keep_ref[...], other_ref[...]
    halves = [jnp.where(core == 0, mine, other), jnp.where(core == 0, other, mine)]
    for j in range(12):
        rows = halves[j // 6][(j % 6) * 4 : (j % 6) * 4 + 4]
        out_ref[j // 4, :, (j % 4) * 128 : (j % 4 + 1) * 128] = rows


def call(fn, outs, specs, scratch=(), mib=40, est=None, name=None):
    return pl.pallas_call(
        fn,
        out_shape=outs,
        in_specs=specs,
        out_specs=jax.tree.map(lambda _: VMEM, outs),
        scratch_shapes=list(scratch),
        compiler_params=params(mib),
        cost_estimate=est,
        name=name,
    )


def sds(shape, dtype):
    return jax.ShapeDtypeStruct(shape, dtype)


def pinned(*arrays):
    return [pltpu.with_memory_space_constraint(a, pltpu.HBM) for a in arrays]


def shifted(block, distance):
    n = lax.axis_size("tm")
    route = [(i - distance, i) for i in range(n) if 0 <= i - distance < n]
    return lax.ppermute(block, "tm", route)


def swapped(block):
    return lax.ppermute(block, "tm", [(i, i ^ 1) for i in range(lax.axis_size("tm"))])


def exchange(block, axes):
    return lax.all_to_all(block, axes, split_axis=0, concat_axis=0, tiled=True)


def local(latents, hidden, grad_out, conv_in_w, conv_in_b, conv_w, final_w, modulation, clip_start):
    win = conv_in_w.transpose(0, 2, 1)
    wt = final_w.T
    bias = conv_in_b.reshape(1, C)
    lat_prev = shifted(latents, 1)
    unit = 2 * C * C * PX
    grad_sent = grad_out[:2]
    grad_next = shifted(grad_sent, -1)
    acc = call(
        k_back, sds((SLAB, C, PX), F32), [PIN, PIN, VMEM, PIN],
        [
            pltpu.SMEM((FRAMES,), jnp.int32), pltpu.VMEM((TAPS, C, C), BF), pltpu.VMEM((SLAB, C, PX), BF),
            pltpu.SemaphoreType.DMA((4,)),
        ],
        mib=16, est=cost(1 << 10, 1 << 10), name="back",
    )(*pinned(clip_start, conv_w), grad_sent, *pinned(grad_out))
    act01, part, halo, icg_part, wcol = call(
        k_first,
        (
            sds((2, C, PX), BF), sds((SLAB, CL, PX), F32), sds((2, CL, PX), F32), sds((E, C), F32), sds((C, E), BF),
        ),
        [SMEM] + [VMEM] * 5,
        [
            pltpu.VMEM((2 * SLAB, CL, PX), BF), pltpu.VMEM((2, E, PX), BF), pltpu.VMEM((E, C), BF),
            pltpu.VMEM((SLAB + 2, CL, PX), F32),
        ],
        mib=16, est=cost(2 * unit, 5 << 20), name="first",
    )(clip_start, lat_prev, latents, win, bias, acc)
    halo_recv = shifted(halo, -1)
    act, slope = call(
        k_rest, (sds((SLAB + 2, C, PX), BF), sds((2, C, PX), F32)), [SMEM] + [VMEM] * 4,
        [pltpu.VMEM((2 * SLAB, CL, PX), BF), pltpu.VMEM((SLAB, E, PX), BF)],
        mib=16, est=cost(2 * unit, 8 << 20), name="rest",
    )(clip_start, lat_prev, latents, wcol, act01)
    keep, send = call(
        k_weight, (sds((32, 2, 48, 128), BF),) * 2, [SMEM] + [VMEM] * 2,
        [pltpu.VMEM((16, 2, 16, TAPS * C), F32)], mib=16, est=cost(50 * unit, 7 << 20), name="weight",
    )(clip_start, grad_out, act)
    piece = sds((CL, PX), BF)
    half = sds((32, 2, 48, 128), BF)
    *tok_parts, icg_blocks, send = pl.pallas_call(
        k_second,
        out_shape=(piece,) * 4 + (sds((16, 16, 128), BF), half),
        in_specs=[SMEM] + [VMEM] * 9 + [HERE],
        out_specs=(VMEM,) * 5 + (HERE,),
        scratch_shapes=[
            pltpu.VMEM((2, C, PX), F32), pltpu.VMEM((2, E, PX), BF), pltpu.VMEM((TAPS * CL, C), BF),
            pltpu.VMEM((SLAB, CL, PX), F32), pltpu.VMEM((E, C), F32), pltpu.VMEM((SLAB * CL, PX), BF),
        ],
        input_output_aliases={10: 5},
        compiler_params=params(16),
        cost_estimate=cost(6 * unit, 8 << 20),
        name="second",
    )(clip_start, grad_next, latents, win, conv_w, acc, slope, part, halo_recv, icg_part, send)
    toks = [tok_parts[0]] + [
        lax.ppermute(tok_parts[k], "seq", [(i, (i + k) % 4) for i in range(4)]) for k in range(1, 4)
    ]
    other = swapped(send)
    normed = call(
        k_prep, sds((NTOK, D), BF), [VMEM, HERE], mib=16, est=cost(10 * NTOK * D, 6 << 20), name="prep"
    )(hidden, icg_blocks)
    pack, tok = pl.pallas_call(
        k_grad,
        out_shape=(sds((128, 40, 128), BF), pltpu.HBM((E, NTOK), BF)),
        in_specs=[VMEM] * 8,
        out_specs=(VMEM, PIN),
        scratch_shapes=[
            pltpu.VMEM((E, NTOK), BF), pltpu.VMEM((4, CL, PX), BF), pltpu.VMEM((E, NTOK), BF),
            pltpu.SemaphoreType.DMA,
        ],
        compiler_params=params(16),
        cost_estimate=cost(2 * NTOK * D * E, 5 << 20),
        name="grad",
    )(*toks, normed, icg_blocks, keep.reshape(64, 48, 128), other.reshape(64, 48, 128))
    recv = exchange(pack, BOTH)
    hidden_grad = pl.pallas_call(
        k_hidden,
        grid=(4,),
        out_shape=sds((NTOK, D), BF),
        in_specs=[
            pl.BlockSpec((E, 128), lambda i: (0, i)),
            pl.BlockSpec((128, D), lambda i: (i, 0)),
            pl.BlockSpec((E, D), lambda i: (0, 0)),
            pl.BlockSpec((2, D), lambda i: (0, 0)),
        ],
        out_specs=pl.BlockSpec((128, D), lambda i: (i, 0)),
        compiler_params=params(16),
        cost_estimate=cost(2 * NTOK * D * E, 6 << 20),
        name="hidden",
    )(*pinned(tok, hidden, wt, modulation))
    copies, own, away = pl.pallas_call(
        k_sum,
        out_shape=(pltpu.HBM((128, 16, 128), BF), sds((24, 128), F32), pltpu.HBM((24, 128), F32)),
        in_specs=[VMEM],
        out_specs=(PIN, VMEM, PIN),
        scratch_shapes=[
            pltpu.VMEM((128, 16, 128), BF), pltpu.VMEM((24, 128), F32), pltpu.SemaphoreType.DMA((2,)),
        ],
        compiler_params=params(16),
        cost_estimate=cost(1 << 20, 2 << 20),
        name="sum",
    )(recv)
    everything = exchange(copies, BOTH)
    weight_grad, wt_near, mod_near = call(
        k_weight_out, (sds((TAPS, 4, C), F32), sds((E, D), BF), sds((2, D), F32)), [VMEM] * 4,
        mib=16, est=cost(1 << 12, 1 << 16), name="weight_out",
    )(own, swapped(away), wt, modulation)
    final_t, mod_grad, icg, bias_grad = call(
        k_last, (sds((E, D), F32), sds((2, D), F32), sds((TAPS * CL, C), F32), sds((1, C), F32)), [VMEM] * 3,
        mib=16, est=cost(1 << 20, 2 << 20), name="last",
    )(everything, wt_near, mod_near)
    return (
        hidden_grad,
        weight_grad.transpose(1, 0, 2),
        icg.reshape(TAPS, CL, C).transpose(0, 2, 1),
        bias_grad.reshape(C),
        final_t.T,
        mod_grad,
    )


def solution(mesh):
    return jax.shard_map(
        local,
        mesh=mesh,
        in_specs=(
            P("tm", None, "seq"),
            P(("tm", "seq"), None),
            P("tm", None, "seq"),
            P(), P(), P(), P(), P(), P(),
        ),
        out_specs=(P(("tm", "seq"), None), P(("tm", "seq"), None, None), P(), P(), P(), P()),
        check_vma=False,
    )
```

```python
import jax
import jax.numpy as jnp
from jax import lax
from jax.experimental import pallas as pl
from jax.experimental.pallas import tpu as pltpu
from jax.sharding import PartitionSpec as P

BF = jnp.bfloat16
F32 = jnp.float32
VMEM = pl.BlockSpec(memory_space=pltpu.VMEM)
SMEM = pl.BlockSpec(memory_space=pltpu.SMEM)
HERE = pl.BlockSpec(memory_space=pl.ANY)
PIN = pl.BlockSpec(memory_space=pltpu.HBM)
EDGE = 4
TAPS = 3
SLAB = 4
CL = 16
C = 512
PX = 512
D = 3072
E = 64
NTOK = 512
FRAMES = 128
BOTH = ("tm", "seq")


def params(mib):
    return pltpu.CompilerParams(vmem_limit_bytes=mib * 1024 * 1024)


def cost(flops, nbytes, trans=0):
    return pl.CostEstimate(flops=flops, bytes_accessed=nbytes, transcendentals=trans)


def mm(a, b, ca, cb):
    return lax.dot_general(a, b, (((ca,), (cb,)), ((), ())), preferred_element_type=F32)


def clip_rel(clip_ref, first, frame):
    whole = first + frame
    start = clip_ref[jnp.clip(whole, 0, FRAMES - 1)]
    return jnp.where(whole >= FRAMES, frame, start - first)


def source(clip_ref, first, frame, tap):
    return jnp.maximum(frame - tap, clip_rel(clip_ref, first, frame))


def k_prep(hidden_ref, after_ref, normed_ref):
    gain = 1.0 / D

    def rows(i, _):
        at = pl.ds(pl.multiple_of(i * 64, 64), 64)
        h = hidden_ref[at, :].astype(F32)
        center = h - jnp.sum(h, axis=1, keepdims=True) * gain
        var = jnp.sum(center * center, axis=1, keepdims=True) * gain
        normed_ref[at, :] = (center * lax.rsqrt(var + 1e-06)).astype(BF)
        return 0

    lax.fori_loop(0, NTOK // 64, rows, 0)


def only(keep, value):
    return jnp.where(keep, value, jnp.zeros_like(value))


def k_back(clip_hbm, conv_hbm, sent_ref, grad_hbm, acc_ref, clip_ref, conv_ref, grad_ref, sems):
    copies = [
        pltpu.make_async_copy(conv_hbm.at[0], conv_ref.at[0], sems.at[0]),
        pltpu.make_async_copy(clip_hbm, clip_ref, sems.at[1]),
        pltpu.make_async_copy(conv_hbm.at[pl.ds(1, 2)], conv_ref.at[pl.ds(1, 2)], sems.at[2]),
        pltpu.make_async_copy(grad_hbm.at[pl.ds(2, 2)], grad_ref.at[pl.ds(2, 2)], sems.at[3]),
    ]
    for copy in copies:
        copy.start()
    grad_ref[:2] = sent_ref[...]
    first = lax.axis_index("tm") * SLAB
    copies[0].wait()
    for s in range(2):
        acc_ref[s] = mm(conv_ref[0], grad_ref[s], 0, 0)
    for copy in copies[1:]:
        copy.wait()
    start = [clip_rel(clip_ref, first, t) for t in range(SLAB)]
    for s in range(SLAB):
        total = acc_ref[s] if s < 2 else mm(conv_ref[0], grad_ref[s], 0, 0)
        for k in range(1, min(TAPS, SLAB - s)):
            total = total + mm(conv_ref[k], only(start[s + k] <= s, grad_ref[s + k]), 0, 0)
        acc_ref[s] = total

    def opens(s, _):
        @pl.when(clip_rel(clip_ref, first, s) == s)
        def _():
            later = jnp.minimum(s + 1, SLAB - 1)
            keep = (s + 1 < SLAB) & (clip_rel(clip_ref, first, s + 1) <= s)
            acc_ref[s] += (
                mm(conv_ref[1], grad_ref[s], 0, 0)
                + mm(conv_ref[2], grad_ref[s], 0, 0)
                + mm(conv_ref[2], only(keep, grad_ref[later]), 0, 0)
            )

        return 0

    lax.fori_loop(0, SLAB, opens, 0)


def load_taps(clip_ref, first, lat_ref, z_ref, slot, frame, base):
    for k in range(TAPS):
        src = jnp.clip(source(clip_ref, first, frame, k) + base, 0, lat_ref.shape[0] - 1)
        z_ref[slot, k * CL : (k + 1) * CL, :] = lat_ref[src]


def set_weights(win_ref, bias_ref, wcat_ref):
    for k in range(TAPS):
        wcat_ref[k * CL : (k + 1) * CL, :] = win_ref[k]
    bias = bias_ref[...]
    high = bias.astype(BF)
    rest = bias - high.astype(F32)
    mid = rest.astype(BF)
    low = (rest - mid.astype(F32)).astype(BF)
    row = lax.broadcasted_iota(jnp.int32, (CL, C), 0)
    tail = jnp.where(row == 0, high.astype(F32), 0.0)
    tail = jnp.where(row == 1, mid.astype(F32), tail)
    tail = jnp.where(row == 2, low.astype(F32), tail)
    wcat_ref[TAPS * CL :, :] = tail.astype(BF)


def half_of(clip_ref, first, all_ref, z_ref, wcol, slot, frame):
    load_taps(clip_ref, first, all_ref, z_ref, slot, frame, SLAB)
    z_ref[slot, TAPS * CL :, :] = jnp.ones((CL, PX), BF)
    h = mm(wcol, z_ref[slot], 1, 0)
    return h, jnp.tanh(h) + 1.0


def slope_of(act, twice):
    sig = 0.5 * twice
    return sig + act * (1.0 - sig)


def k_first(
    clip_ref, prev_ref, lat_ref, win_ref, bias_ref, acc_ref,
    act_ref, part_ref, halo_ref, icg_ref, wcol_ref,
    all_ref, z_ref, wcat_ref, lacc_ref,
):
    first = lax.axis_index("tm") * SLAB
    all_ref[:SLAB] = prev_ref[...]
    all_ref[SLAB:] = lat_ref[...]
    set_weights(win_ref, bias_ref, wcat_ref)
    wcol = (wcat_ref[...].astype(F32) * 0.5).astype(BF).T
    wcol_ref[...] = wcol
    lacc_ref[...] = jnp.zeros_like(lacc_ref)
    icg = jnp.zeros((E, C), F32)
    for t in range(2):
        h, twice = half_of(clip_ref, first, all_ref, z_ref, wcol, t, t)
        act = h * twice
        act_ref[t] = act.astype(BF)
        gp = (acc_ref[t] * slope_of(act, twice)).astype(BF)
        back = mm(wcat_ref[...], gp, 1, 0)
        for k in range(TAPS):
            src = source(clip_ref, first, t, k) + 2
            lacc_ref[src] += back[k * CL : (k + 1) * CL]
        icg = icg + mm(z_ref[t], gp, 1, 1)
    halo_ref[...] = lacc_ref[:2].astype(BF)
    part_ref[...] = lacc_ref[2:]
    icg_ref[...] = icg


def k_rest(clip_ref, prev_ref, lat_ref, wcol_ref, act01_ref, act_ref, slope_ref, all_ref, z_ref):
    first = lax.axis_index("tm") * SLAB
    all_ref[:SLAB] = prev_ref[...]
    all_ref[SLAB:] = lat_ref[...]
    wcol = wcol_ref[...]
    act_ref[2:4] = act01_ref[...]
    for j in range(2):
        h, twice = half_of(clip_ref, first, all_ref, z_ref, wcol, j, j - 2)
        act_ref[j] = (h * twice).astype(BF)
    for j in range(2, SLAB):
        h, twice = half_of(clip_ref, first, all_ref, z_ref, wcol, j, j)
        act = h * twice
        act_ref[j + 2] = act.astype(BF)
        slope_ref[j - 2] = slope_of(act, twice)


def k_weight(clip_ref, grad_ref, act_ref, keep_ref, send_ref, acc_ref):
    first = lax.axis_index("tm") * SLAB
    core = lax.axis_index("tm") % 2
    for k in range(TAPS):
        total = None
        for t in range(SLAB):
            src = jnp.maximum(source(clip_ref, first, t, k), -2) + 2
            part = mm(grad_ref[t], act_ref[src], 1, 1)
            total = part if total is None else total + part
        acc_ref[:, :, :, k * C : (k + 1) * C] = total.reshape(16, 2, 16, C)
    upper = lax.broadcasted_iota(jnp.int32, (32, 8, 128), 1) < 4
    for ref, half in ((keep_ref, core), (send_ref, 1 - core)):
        for jj in range(0, TAPS * C // 128, 4):
            even, odd = [], []
            for h in range(2):
                at = (jj + 2 * h) * 128
                a = acc_ref[:, half, :, at : at + 128].reshape(32, 8, 128)
                b = acc_ref[:, half, :, at + 128 : at + 256].reshape(32, 8, 128)
                even.append(jnp.where(upper, a, pltpu.roll(b, 4, 1)))
                odd.append(jnp.where(upper, pltpu.roll(a, 4, 1), b))
            ref[:, 0, jj * 4 : jj * 4 + 16, :] = jnp.concatenate(even, axis=1).astype(BF)
            ref[:, 1, jj * 4 : jj * 4 + 16, :] = jnp.concatenate(odd, axis=1).astype(BF)


def k_second(
    clip_ref, next_ref, lat_ref, win_ref, conv_ref, acc_in_ref, slope_ref, part_ref, halo_ref, icg_in_ref, after_ref,
    tok0_ref, tok1_ref, tok2_ref, tok3_ref, icg_ref, passed_ref, acc_ref, z_ref, wcat_ref, lacc_ref, icg_acc, low_ref,
):
    first = lax.axis_index("tm") * SLAB
    start = [clip_rel(clip_ref, first, SLAB + t) for t in range(2)]
    for k in range(TAPS):
        wcat_ref[k * CL : (k + 1) * CL, :] = win_ref[k]
    acc_ref[0] = acc_in_ref[2] + mm(conv_ref[2], only(start[0] <= 2, next_ref[0]), 0, 0)
    acc_ref[1] = (
        acc_in_ref[3]
        + mm(conv_ref[1], only(start[0] <= 3, next_ref[0]), 0, 0)
        + mm(conv_ref[2], only(start[1] <= 3, next_ref[1]), 0, 0)
    )

    @pl.when((clip_rel(clip_ref, first, 3) == 3) & (start[0] <= 3))
    def _():
        acc_ref[1] += mm(conv_ref[2], next_ref[0], 0, 0)

    lacc_ref[:SLAB] = part_ref[...]
    lacc_ref[2:SLAB] += halo_ref[...].astype(F32)
    icg = icg_in_ref[...]
    for t in range(2):
        gp = (acc_ref[t] * slope_ref[t]).astype(BF)
        load_taps(clip_ref, first, lat_ref, z_ref, t, t + 2, 0)
        z_ref[t, TAPS * CL :, :] = jnp.ones((CL, PX), BF)
        back = mm(wcat_ref[...], gp, 1, 0)
        for k in range(TAPS):
            src = source(clip_ref, first, t + 2, k)
            lacc_ref[src] += back[k * CL : (k + 1) * CL]
        icg = icg + mm(z_ref[t], gp, 1, 1)
    icg_acc[...] = icg
    for f in range(SLAB):
        low_ref[f * CL : (f + 1) * CL, :] = lacc_ref[f].astype(BF)
    r = lax.broadcasted_iota(jnp.int32, (PX, 1), 0)
    c = lax.broadcasted_iota(jnp.int32, (PX, PX), 1)
    pick = (((r & 3) << 7) + (r >> 2) == c).astype(F32).astype(BF)
    low_ref[...] = mm(low_ref[...], pick, 1, 0).astype(BF)
    z = lax.axis_index("seq")
    for k, ref in enumerate((tok0_ref, tok1_ref, tok2_ref, tok3_ref)):
        ref[...] = low_ref[pl.ds(pl.multiple_of(lax.rem(z + k, 4) * CL, CL), CL), :]
    for rb in range(4):
        for lb in range(4):
            icg_ref[rb * 4 + lb] = icg_acc[rb * 16 : (rb + 1) * 16, lb * 128 : (lb + 1) * 128].astype(BF)


def k_grad(
    tok0_ref, tok1_ref, tok2_ref, tok3_ref, normed_ref, icg_ref, keep_ref, other_ref,
    pack_ref, tok_hbm, raw_ref, recv_ref, tok_ref, sem,
):
    z = lax.axis_index("seq")
    for k, ref in enumerate((tok0_ref, tok1_ref, tok2_ref, tok3_ref)):
        recv_ref[lax.rem(z + 4 - k, 4)] = ref[...]
    for s in range(4):
        for q in range(EDGE):
            raw_ref[q * CL : (q + 1) * CL, s * 128 : (s + 1) * 128] = recv_ref[
                s, :, q * 128 : (q + 1) * 128
            ]
    r = lax.broadcasted_iota(jnp.int32, (E, E), 0)
    c = lax.broadcasted_iota(jnp.int32, (E, E), 1)
    order = (((r & 3) << 4) + (r >> 2) == c).astype(F32).astype(BF)
    tok = mm(order, raw_ref[...], 1, 0)
    tok_ref[...] = tok.astype(BF)
    copy = pltpu.make_async_copy(tok_ref, tok_hbm, sem)
    copy.start()
    total = jnp.broadcast_to(jnp.sum(tok, axis=1, keepdims=True), (E, 128)).astype(BF)
    for lb in range(D // 512):
        g = mm(tok_ref[...], normed_ref[:, lb * 512 : (lb + 1) * 512], 1, 0).astype(BF)
        for u in range(4):
            for rb in range(4):
                pack_ref[rb * 24 + lb * 4 + u, :16, :] = g[rb * 16 : (rb + 1) * 16, u * 128 : (u + 1) * 128]
    pack_ref[96:112, :16, :] = icg_ref[...]
    for rb in range(4):
        pack_ref[112 + rb, :16, :] = total[rb * 16 : (rb + 1) * 16]
    pack_ref[116:, :16, :] = jnp.zeros((12, 16, 128), BF)
    for xy in range(16):
        for half in range(2):
            at = pl.ds((xy * 2 + half) * 4, 4)
            rows = slice(half * 24, half * 24 + 24)
            both = keep_ref[xy * 4 : xy * 4 + 4].astype(F32) + other_ref[xy * 4 : xy * 4 + 4].astype(F32)
            pack_ref[at, 16:, :] = both[:, rows, :].astype(BF)
    copy.wait()


def k_hidden(tok_ref, hidden_ref, wt_ref, mod_ref, out_ref):
    gain = 1.0 / D
    h = hidden_ref[...].astype(F32)
    center = h - jnp.sum(h, axis=1, keepdims=True) * gain
    var = jnp.sum(center * center, axis=1, keepdims=True) * gain
    inv = lax.rsqrt(var + 1e-06)
    normed = center * inv
    mod_in = mm(tok_ref[...].T, wt_ref[...], 1, 0)
    ng = mod_in * (1.0 + mod_ref[1:2, :])
    m1 = jnp.sum(ng, axis=1, keepdims=True) * gain
    m2 = jnp.sum(ng * normed, axis=1, keepdims=True) * gain
    out_ref[...] = (inv * (ng - m1 - normed * m2)).astype(BF)


def k_sum(recv_ref, out_hbm, keep_ref, send_hbm, out_ref, send_ref, sems):
    core = lax.axis_index("tm") % 2
    total = jnp.sum(recv_ref[:, :16, :].astype(F32), axis=0).astype(BF)
    out_ref[...] = jnp.broadcast_to(total[None], out_ref.shape)
    copy = pltpu.make_async_copy(out_ref, out_hbm, sems.at[0])
    copy.start()
    sums = [jnp.zeros((24, 128), F32)] * 2
    for d in range(128):
        c = (d // 4) % 2
        sums[c] = sums[c] + recv_ref[d, 16:, :].astype(F32)
    keep_ref[...] = jnp.where(core == 0, sums[0], sums[1])
    send_ref[...] = jnp.where(core == 0, sums[1], sums[0])
    away = pltpu.make_async_copy(send_ref, send_hbm, sems.at[1])
    away.start()
    copy.wait()
    away.wait()


def k_last(all_ref, wt_ref, mod_ref, final_ref, modg_ref, icg_ref, bias_ref):
    tot = [all_ref[112 + rb].astype(F32) for rb in range(4)]
    for lb in range(D // 128):
        at = slice(lb * 128, (lb + 1) * 128)
        scale = 1.0 + mod_ref[1:2, at]
        shift = mod_ref[0:1, at]
        s0 = jnp.zeros((1, 128), F32)
        s1 = jnp.zeros((1, 128), F32)
        for rb in range(4):
            rows = slice(rb * 16, (rb + 1) * 16)
            g = all_ref[rb * 24 + lb].astype(F32)
            w = wt_ref[rows, at].astype(F32)
            final_ref[rows, at] = g * scale + shift * tot[rb]
            s0 = s0 + jnp.sum(w * tot[rb], axis=0, keepdims=True)
            s1 = s1 + jnp.sum(w * g, axis=0, keepdims=True)
        modg_ref[0:1, at] = s0
        modg_ref[1:2, at] = s1
    for rb in range(3):
        for lb in range(4):
            icg_ref[rb * 16 : (rb + 1) * 16, lb * 128 : (lb + 1) * 128] = all_ref[96 + rb * 4 + lb].astype(F32)
    for lb in range(4):
        bias_ref[:, lb * 128 : (lb + 1) * 128] = all_ref[96 + 12 + lb].astype(F32)[0:1]


def k_weight_out(keep_ref, other_ref, wt_ref, mod_ref, out_ref, wt_near_ref, mod_near_ref):
    wt_near_ref[...] = wt_ref[...]
    mod_near_ref[...] = mod_ref[...]
    core = lax.axis_index("tm") % 2
    mine, other = keep_ref[...], other_ref[...]
    halves = [jnp.where(core == 0, mine, other), jnp.where(core == 0, other, mine)]
    for j in range(12):
        rows = halves[j // 6][(j % 6) * 4 : (j % 6) * 4 + 4]
        out_ref[j // 4, :, (j % 4) * 128 : (j % 4 + 1) * 128] = rows


def call(fn, outs, specs, scratch=(), mib=40, est=None, name=None):
    return pl.pallas_call(
        fn,
        out_shape=outs,
        in_specs=specs,
        out_specs=jax.tree.map(lambda _: VMEM, outs),
        scratch_shapes=list(scratch),
        compiler_params=params(mib),
        cost_estimate=est,
        name=name,
    )


def sds(shape, dtype):
    return jax.ShapeDtypeStruct(shape, dtype)


def pinned(*arrays):
    return [pltpu.with_memory_space_constraint(a, pltpu.HBM) for a in arrays]


def shifted(block, distance):
    n = lax.axis_size("tm")
    route = [(i - distance, i) for i in range(n) if 0 <= i - distance < n]
    return lax.ppermute(block, "tm", route)


def swapped(block):
    return lax.ppermute(block, "tm", [(i, i ^ 1) for i in range(lax.axis_size("tm"))])


def exchange(block, axes):
    return lax.all_to_all(block, axes, split_axis=0, concat_axis=0, tiled=True)


def local(latents, hidden, grad_out, conv_in_w, conv_in_b, conv_w, final_w, modulation, clip_start):
    win = conv_in_w.transpose(0, 2, 1)
    wt = final_w.T
    bias = conv_in_b.reshape(1, C)
    lat_prev = shifted(latents, 1)
    unit = 2 * C * C * PX
    grad_sent = grad_out[:2]
    grad_next = shifted(grad_sent, -1)
    acc = call(
        k_back, sds((SLAB, C, PX), F32), [PIN, PIN, VMEM, PIN],
        [
            pltpu.SMEM((FRAMES,), jnp.int32), pltpu.VMEM((TAPS, C, C), BF), pltpu.VMEM((SLAB, C, PX), BF),
            pltpu.SemaphoreType.DMA((4,)),
        ],
        mib=16, est=cost(1 << 10, 1 << 10), name="back",
    )(*pinned(clip_start, conv_w), grad_sent, *pinned(grad_out))
    act01, part, halo, icg_part, wcol = call(
        k_first,
        (
            sds((2, C, PX), BF), sds((SLAB, CL, PX), F32), sds((2, CL, PX), BF), sds((E, C), F32), sds((C, E), BF),
        ),
        [SMEM] + [VMEM] * 5,
        [
            pltpu.VMEM((2 * SLAB, CL, PX), BF), pltpu.VMEM((2, E, PX), BF), pltpu.VMEM((E, C), BF),
            pltpu.VMEM((SLAB + 2, CL, PX), F32),
        ],
        mib=16, est=cost(2 * unit, 5 << 20), name="first",
    )(clip_start, lat_prev, latents, win, bias, acc)
    halo_recv = shifted(halo, -1)
    act, slope = call(
        k_rest, (sds((SLAB + 2, C, PX), BF), sds((2, C, PX), F32)), [SMEM] + [VMEM] * 4,
        [pltpu.VMEM((2 * SLAB, CL, PX), BF), pltpu.VMEM((SLAB, E, PX), BF)],
        mib=16, est=cost(2 * unit, 8 << 20), name="rest",
    )(clip_start, lat_prev, latents, wcol, act01)
    keep, send = call(
        k_weight, (sds((32, 2, 48, 128), BF),) * 2, [SMEM] + [VMEM] * 2,
        [pltpu.VMEM((16, 2, 16, TAPS * C), F32)], mib=16, est=cost(50 * unit, 7 << 20), name="weight",
    )(clip_start, grad_out, act)
    piece = sds((CL, PX), BF)
    half = sds((32, 2, 48, 128), BF)
    *tok_parts, icg_blocks, send = pl.pallas_call(
        k_second,
        out_shape=(piece,) * 4 + (sds((16, 16, 128), BF), half),
        in_specs=[SMEM] + [VMEM] * 9 + [HERE],
        out_specs=(VMEM,) * 5 + (HERE,),
        scratch_shapes=[
            pltpu.VMEM((2, C, PX), F32), pltpu.VMEM((2, E, PX), BF), pltpu.VMEM((TAPS * CL, C), BF),
            pltpu.VMEM((SLAB, CL, PX), F32), pltpu.VMEM((E, C), F32), pltpu.VMEM((SLAB * CL, PX), BF),
        ],
        input_output_aliases={10: 5},
        compiler_params=params(16),
        cost_estimate=cost(6 * unit, 8 << 20),
        name="second",
    )(clip_start, grad_next, latents, win, conv_w, acc, slope, part, halo_recv, icg_part, send)
    toks = [tok_parts[0]] + [
        lax.ppermute(tok_parts[k], "seq", [(i, (i + k) % 4) for i in range(4)]) for k in range(1, 4)
    ]
    other = swapped(send)
    normed = call(
        k_prep, sds((NTOK, D), BF), [VMEM, HERE], mib=16, est=cost(10 * NTOK * D, 6 << 20), name="prep"
    )(hidden, icg_blocks)
    pack, tok = pl.pallas_call(
        k_grad,
        out_shape=(sds((128, 40, 128), BF), pltpu.HBM((E, NTOK), BF)),
        in_specs=[VMEM] * 8,
        out_specs=(VMEM, PIN),
        scratch_shapes=[
            pltpu.VMEM((E, NTOK), BF), pltpu.VMEM((4, CL, PX), BF), pltpu.VMEM((E, NTOK), BF),
            pltpu.SemaphoreType.DMA,
        ],
        compiler_params=params(16),
        cost_estimate=cost(2 * NTOK * D * E, 5 << 20),
        name="grad",
    )(*toks, normed, icg_blocks, keep.reshape(64, 48, 128), other.reshape(64, 48, 128))
    recv = exchange(pack, BOTH)
    hidden_grad = pl.pallas_call(
        k_hidden,
        grid=(4,),
        out_shape=sds((NTOK, D), BF),
        in_specs=[
            pl.BlockSpec((E, 128), lambda i: (0, i)),
            pl.BlockSpec((128, D), lambda i: (i, 0)),
            pl.BlockSpec((E, D), lambda i: (0, 0)),
            pl.BlockSpec((2, D), lambda i: (0, 0)),
        ],
        out_specs=pl.BlockSpec((128, D), lambda i: (i, 0)),
        compiler_params=params(16),
        cost_estimate=cost(2 * NTOK * D * E, 6 << 20),
        name="hidden",
    )(*pinned(tok, hidden, wt, modulation))
    copies, own, away = pl.pallas_call(
        k_sum,
        out_shape=(pltpu.HBM((128, 16, 128), BF), sds((24, 128), F32), pltpu.HBM((24, 128), F32)),
        in_specs=[VMEM],
        out_specs=(PIN, VMEM, PIN),
        scratch_shapes=[
            pltpu.VMEM((128, 16, 128), BF), pltpu.VMEM((24, 128), F32), pltpu.SemaphoreType.DMA((2,)),
        ],
        compiler_params=params(16),
        cost_estimate=cost(1 << 20, 2 << 20),
        name="sum",
    )(recv)
    everything = exchange(copies, BOTH)
    weight_grad, wt_near, mod_near = call(
        k_weight_out, (sds((TAPS, 4, C), F32), sds((E, D), BF), sds((2, D), F32)), [VMEM] * 4,
        mib=16, est=cost(1 << 12, 1 << 16), name="weight_out",
    )(own, swapped(away), wt, modulation)
    final_t, mod_grad, icg, bias_grad = call(
        k_last, (sds((E, D), F32), sds((2, D), F32), sds((TAPS * CL, C), F32), sds((1, C), F32)), [VMEM] * 3,
        mib=16, est=cost(1 << 20, 2 << 20), name="last",
    )(everything, wt_near, mod_near)
    return (
        hidden_grad,
        weight_grad.transpose(1, 0, 2),
        icg.reshape(TAPS, CL, C).transpose(0, 2, 1),
        bias_grad.reshape(C),
        final_t.T,
        mod_grad,
    )


def solution(mesh):
    return jax.shard_map(
        local,
        mesh=mesh,
        in_specs=(
            P("tm", None, "seq"),
            P(("tm", "seq"), None),
            P("tm", None, "seq"),
            P(), P(), P(), P(), P(), P(),
        ),
        out_specs=(P(("tm", "seq"), None), P(("tm", "seq"), None, None), P(), P(), P(), P()),
        check_vma=False,
    )
```

```python
import jax
import jax.numpy as jnp
from jax import lax
from jax.experimental import pallas as pl
from jax.experimental.pallas import tpu as pltpu
from jax.sharding import PartitionSpec as P

BF = jnp.bfloat16
F32 = jnp.float32
VMEM = pl.BlockSpec(memory_space=pltpu.VMEM)
SMEM = pl.BlockSpec(memory_space=pltpu.SMEM)
HERE = pl.BlockSpec(memory_space=pl.ANY)
PIN = pl.BlockSpec(memory_space=pltpu.HBM)
EDGE = 4
TAPS = 3
SLAB = 4
CL = 16
C = 512
PX = 512
D = 3072
E = 64
NTOK = 512
FRAMES = 128
BOTH = ("tm", "seq")


def params(mib):
    return pltpu.CompilerParams(vmem_limit_bytes=mib * 1024 * 1024)


def cost(flops, nbytes, trans=0):
    return pl.CostEstimate(flops=flops, bytes_accessed=nbytes, transcendentals=trans)


def mm(a, b, ca, cb):
    return lax.dot_general(a, b, (((ca,), (cb,)), ((), ())), preferred_element_type=F32)


def clip_rel(clip_ref, first, frame):
    whole = first + frame
    start = clip_ref[jnp.clip(whole, 0, FRAMES - 1)]
    return jnp.where(whole >= FRAMES, frame, start - first)


def source(clip_ref, first, frame, tap):
    return jnp.maximum(frame - tap, clip_rel(clip_ref, first, frame))


def k_prep(hidden_ref, after_ref, normed_ref):
    gain = 1.0 / D

    def rows(i, _):
        at = pl.ds(pl.multiple_of(i * 64, 64), 64)
        h = hidden_ref[at, :].astype(F32)
        center = h - jnp.sum(h, axis=1, keepdims=True) * gain
        var = jnp.sum(center * center, axis=1, keepdims=True) * gain
        normed_ref[at, :] = (center * lax.rsqrt(var + 1e-06)).astype(BF)
        return 0

    lax.fori_loop(0, NTOK // 64, rows, 0)


def only(keep, value):
    return jnp.where(keep, value, jnp.zeros_like(value))


def k_back(clip_hbm, conv_hbm, sent_ref, grad_hbm, acc_ref, clip_ref, conv_ref, grad_ref, sems):
    copies = [
        pltpu.make_async_copy(conv_hbm.at[0], conv_ref.at[0], sems.at[0]),
        pltpu.make_async_copy(clip_hbm, clip_ref, sems.at[1]),
        pltpu.make_async_copy(conv_hbm.at[pl.ds(1, 2)], conv_ref.at[pl.ds(1, 2)], sems.at[2]),
        pltpu.make_async_copy(grad_hbm.at[pl.ds(2, 2)], grad_ref.at[pl.ds(2, 2)], sems.at[3]),
    ]
    for copy in copies:
        copy.start()
    grad_ref[:2] = sent_ref[...]
    first = lax.axis_index("tm") * SLAB
    copies[0].wait()
    for s in range(2):
        acc_ref[s] = mm(conv_ref[0], grad_ref[s], 0, 0)
    for copy in copies[1:]:
        copy.wait()
    start = [clip_rel(clip_ref, first, t) for t in range(SLAB)]
    for s in range(SLAB):
        total = acc_ref[s] if s < 2 else mm(conv_ref[0], grad_ref[s], 0, 0)
        for k in range(1, min(TAPS, SLAB - s)):
            total = total + mm(conv_ref[k], only(start[s + k] <= s, grad_ref[s + k]), 0, 0)
        acc_ref[s] = total

    def opens(s, _):
        @pl.when(clip_rel(clip_ref, first, s) == s)
        def _():
            later = jnp.minimum(s + 1, SLAB - 1)
            keep = (s + 1 < SLAB) & (clip_rel(clip_ref, first, s + 1) <= s)
            acc_ref[s] += (
                mm(conv_ref[1], grad_ref[s], 0, 0)
                + mm(conv_ref[2], grad_ref[s], 0, 0)
                + mm(conv_ref[2], only(keep, grad_ref[later]), 0, 0)
            )

        return 0

    lax.fori_loop(0, SLAB, opens, 0)


def load_taps(clip_ref, first, lat_ref, z_ref, slot, frame, base):
    for k in range(TAPS):
        src = jnp.clip(source(clip_ref, first, frame, k) + base, 0, lat_ref.shape[0] - 1)
        z_ref[slot, k * CL : (k + 1) * CL, :] = lat_ref[src]


def set_weights(win_ref, bias_ref, wcat_ref):
    for k in range(TAPS):
        wcat_ref[k * CL : (k + 1) * CL, :] = win_ref[k]
    bias = bias_ref[...]
    high = bias.astype(BF)
    rest = bias - high.astype(F32)
    mid = rest.astype(BF)
    low = (rest - mid.astype(F32)).astype(BF)
    row = lax.broadcasted_iota(jnp.int32, (CL, C), 0)
    tail = jnp.where(row == 0, high.astype(F32), 0.0)
    tail = jnp.where(row == 1, mid.astype(F32), tail)
    tail = jnp.where(row == 2, low.astype(F32), tail)
    wcat_ref[TAPS * CL :, :] = tail.astype(BF)


def half_of(clip_ref, first, all_ref, z_ref, wcol, slot, frame):
    load_taps(clip_ref, first, all_ref, z_ref, slot, frame, SLAB)
    z_ref[slot, TAPS * CL :, :] = jnp.ones((CL, PX), BF)
    h = mm(wcol, z_ref[slot], 1, 0)
    return h, jnp.tanh(h) + 1.0


def slope_of(act, twice):
    sig = 0.5 * twice
    return sig + act * (1.0 - sig)


def k_first(
    clip_ref, prev_ref, lat_ref, win_ref, bias_ref, acc_ref,
    act_ref, part_ref, halo_ref, icg_ref, wcol_ref,
    all_ref, z_ref, wcat_ref, lacc_ref,
):
    first = lax.axis_index("tm") * SLAB
    all_ref[:SLAB] = prev_ref[...]
    all_ref[SLAB:] = lat_ref[...]
    set_weights(win_ref, bias_ref, wcat_ref)
    wcol = (wcat_ref[...].astype(F32) * 0.5).astype(BF).T
    wcol_ref[...] = wcol
    lacc_ref[...] = jnp.zeros_like(lacc_ref)
    icg = jnp.zeros((E, C), F32)
    for t in range(2):
        h, twice = half_of(clip_ref, first, all_ref, z_ref, wcol, t, t)
        act = h * twice
        act_ref[t] = act.astype(BF)
        gp = (acc_ref[t] * slope_of(act, twice)).astype(BF)
        back = mm(wcat_ref[...], gp, 1, 0)
        for k in range(TAPS):
            src = source(clip_ref, first, t, k) + 2
            lacc_ref[src] += back[k * CL : (k + 1) * CL]
        icg = icg + mm(z_ref[t], gp, 1, 1)
    halo_ref[...] = lacc_ref[:2].astype(BF)
    part_ref[...] = lacc_ref[2:]
    icg_ref[...] = icg


def k_rest(clip_ref, prev_ref, lat_ref, wcol_ref, act01_ref, act_ref, slope_ref, all_ref, z_ref):
    first = lax.axis_index("tm") * SLAB
    all_ref[:SLAB] = prev_ref[...]
    all_ref[SLAB:] = lat_ref[...]
    wcol = wcol_ref[...]
    act_ref[2:4] = act01_ref[...]
    for j in range(2):
        h, twice = half_of(clip_ref, first, all_ref, z_ref, wcol, j, j - 2)
        act_ref[j] = (h * twice).astype(BF)
    for j in range(2, SLAB):
        h, twice = half_of(clip_ref, first, all_ref, z_ref, wcol, j, j)
        act = h * twice
        act_ref[j + 2] = act.astype(BF)
        slope_ref[j - 2] = slope_of(act, twice)


def k_weight(clip_ref, grad_ref, act_ref, keep_ref, send_ref, acc_ref):
    first = lax.axis_index("tm") * SLAB
    core = lax.axis_index("tm") % 2
    for k in range(TAPS):
        total = None
        for t in range(SLAB):
            src = jnp.maximum(source(clip_ref, first, t, k), -2) + 2
            part = mm(grad_ref[t], act_ref[src], 1, 1)
            total = part if total is None else total + part
        acc_ref[:, :, :, k * C : (k + 1) * C] = total.reshape(16, 2, 16, C)
    upper = lax.broadcasted_iota(jnp.int32, (32, 8, 128), 1) < 4
    for ref, half in ((keep_ref, core), (send_ref, 1 - core)):
        for jj in range(0, TAPS * C // 128, 4):
            even, odd = [], []
            for h in range(2):
                at = (jj + 2 * h) * 128
                a = acc_ref[:, half, :, at : at + 128].reshape(32, 8, 128)
                b = acc_ref[:, half, :, at + 128 : at + 256].reshape(32, 8, 128)
                even.append(jnp.where(upper, a, pltpu.roll(b, 4, 1)))
                odd.append(jnp.where(upper, pltpu.roll(a, 4, 1), b))
            ref[:, 0, jj * 4 : jj * 4 + 16, :] = jnp.concatenate(even, axis=1).astype(BF)
            ref[:, 1, jj * 4 : jj * 4 + 16, :] = jnp.concatenate(odd, axis=1).astype(BF)


def k_second(
    clip_ref, next_ref, lat_ref, win_ref, conv_ref, acc_in_ref, slope_ref, part_ref, halo_ref, icg_in_ref, after_ref,
    tok0_ref, tok1_ref, tok2_ref, tok3_ref, icg_ref, passed_ref, acc_ref, z_ref, wcat_ref, lacc_ref, icg_acc, low_ref,
):
    first = lax.axis_index("tm") * SLAB
    start = [clip_rel(clip_ref, first, SLAB + t) for t in range(2)]
    for k in range(TAPS):
        wcat_ref[k * CL : (k + 1) * CL, :] = win_ref[k]
    acc_ref[0] = acc_in_ref[2] + mm(conv_ref[2], only(start[0] <= 2, next_ref[0]), 0, 0)
    acc_ref[1] = (
        acc_in_ref[3]
        + mm(conv_ref[1], only(start[0] <= 3, next_ref[0]), 0, 0)
        + mm(conv_ref[2], only(start[1] <= 3, next_ref[1]), 0, 0)
    )

    @pl.when((clip_rel(clip_ref, first, 3) == 3) & (start[0] <= 3))
    def _():
        acc_ref[1] += mm(conv_ref[2], next_ref[0], 0, 0)

    lacc_ref[:SLAB] = part_ref[...]
    lacc_ref[2:SLAB] += halo_ref[...].astype(F32)
    icg = icg_in_ref[...]
    for t in range(2):
        gp = (acc_ref[t] * slope_ref[t]).astype(BF)
        load_taps(clip_ref, first, lat_ref, z_ref, t, t + 2, 0)
        z_ref[t, TAPS * CL :, :] = jnp.ones((CL, PX), BF)
        back = mm(wcat_ref[...], gp, 1, 0)
        for k in range(TAPS):
            src = source(clip_ref, first, t + 2, k)
            lacc_ref[src] += back[k * CL : (k + 1) * CL]
        icg = icg + mm(z_ref[t], gp, 1, 1)
    icg_acc[...] = icg
    for f in range(SLAB):
        low_ref[f * CL : (f + 1) * CL, :] = lacc_ref[f].astype(BF)
    r = lax.broadcasted_iota(jnp.int32, (PX, 1), 0)
    c = lax.broadcasted_iota(jnp.int32, (PX, PX), 1)
    pick = (((r & 3) << 7) + (r >> 2) == c).astype(F32).astype(BF)
    low_ref[...] = mm(low_ref[...], pick, 1, 0).astype(BF)
    z = lax.axis_index("seq")
    for k, ref in enumerate((tok0_ref, tok1_ref, tok2_ref, tok3_ref)):
        ref[...] = low_ref[pl.ds(pl.multiple_of(lax.rem(z + k, 4) * CL, CL), CL), :]
    for rb in range(4):
        for lb in range(4):
            icg_ref[rb * 4 + lb] = icg_acc[rb * 16 : (rb + 1) * 16, lb * 128 : (lb + 1) * 128].astype(BF)


def k_grad(
    tok0_ref, tok1_ref, tok2_ref, tok3_ref, normed_ref, icg_ref, keep_ref, other_ref,
    pack_ref, tok_hbm, raw_ref, recv_ref, tok_ref, sem,
):
    z = lax.axis_index("seq")
    for k, ref in enumerate((tok0_ref, tok1_ref, tok2_ref, tok3_ref)):
        recv_ref[lax.rem(z + 4 - k, 4)] = ref[...]
    for s in range(4):
        for q in range(EDGE):
            raw_ref[q * CL : (q + 1) * CL, s * 128 : (s + 1) * 128] = recv_ref[
                s, :, q * 128 : (q + 1) * 128
            ]
    r = lax.broadcasted_iota(jnp.int32, (E, E), 0)
    c = lax.broadcasted_iota(jnp.int32, (E, E), 1)
    order = (((r & 3) << 4) + (r >> 2) == c).astype(F32).astype(BF)
    tok = mm(order, raw_ref[...], 1, 0)
    tok_ref[...] = tok.astype(BF)
    copy = pltpu.make_async_copy(tok_ref, tok_hbm, sem)
    copy.start()
    total = jnp.broadcast_to(jnp.sum(tok, axis=1, keepdims=True), (E, 128)).astype(BF)
    for lb in range(D // 512):
        g = mm(tok_ref[...], normed_ref[:, lb * 512 : (lb + 1) * 512], 1, 0).astype(BF)
        for u in range(4):
            for rb in range(4):
                pack_ref[rb * 24 + lb * 4 + u, :16, :] = g[rb * 16 : (rb + 1) * 16, u * 128 : (u + 1) * 128]
    pack_ref[96:112, :16, :] = icg_ref[...]
    for rb in range(4):
        pack_ref[112 + rb, :16, :] = total[rb * 16 : (rb + 1) * 16]
    pack_ref[116:, :16, :] = jnp.zeros((12, 16, 128), BF)
    for xy in range(16):
        for half in range(2):
            at = pl.ds((xy * 2 + half) * 4, 4)
            rows = slice(half * 24, half * 24 + 24)
            both = keep_ref[xy * 4 : xy * 4 + 4].astype(F32) + other_ref[xy * 4 : xy * 4 + 4].astype(F32)
            pack_ref[at, 16:, :] = both[:, rows, :].astype(BF)
    copy.wait()


def k_hidden(tok_ref, hidden_ref, wt_ref, mod_ref, out_ref):
    gain = 1.0 / D
    h = hidden_ref[...].astype(F32)
    center = h - jnp.sum(h, axis=1, keepdims=True) * gain
    var = jnp.sum(center * center, axis=1, keepdims=True) * gain
    inv = lax.rsqrt(var + 1e-06)
    normed = center * inv
    mod_in = mm(tok_ref[...].T, wt_ref[...], 1, 0)
    ng = mod_in * (1.0 + mod_ref[1:2, :])
    m1 = jnp.sum(ng, axis=1, keepdims=True) * gain
    m2 = jnp.sum(ng * normed, axis=1, keepdims=True) * gain
    out_ref[...] = (inv * (ng - m1 - normed * m2)).astype(BF)


def k_sum(recv_ref, out_hbm, keep_ref, send_hbm, out_ref, send_ref, sems):
    core = lax.axis_index("tm") % 2
    total = jnp.sum(recv_ref[:, :16, :].astype(F32), axis=0).astype(BF)
    out_ref[...] = jnp.broadcast_to(total[None], out_ref.shape)
    copy = pltpu.make_async_copy(out_ref, out_hbm, sems.at[0])
    copy.start()
    sums = [jnp.zeros((24, 128), F32)] * 2
    for d in range(128):
        c = (d // 4) % 2
        sums[c] = sums[c] + recv_ref[d, 16:, :].astype(F32)
    keep_ref[...] = jnp.where(core == 0, sums[0], sums[1])
    send_ref[...] = jnp.where(core == 0, sums[1], sums[0])
    away = pltpu.make_async_copy(send_ref, send_hbm, sems.at[1])
    away.start()
    copy.wait()
    away.wait()


def k_last(all_ref, wt_ref, mod_ref, final_ref, modg_ref, icg_ref, bias_ref):
    tot = [all_ref[112 + rb].astype(F32) for rb in range(4)]
    for lb in range(D // 128):
        at = slice(lb * 128, (lb + 1) * 128)
        scale = 1.0 + mod_ref[1:2, at]
        shift = mod_ref[0:1, at]
        s0 = jnp.zeros((1, 128), F32)
        s1 = jnp.zeros((1, 128), F32)
        for rb in range(4):
            rows = slice(rb * 16, (rb + 1) * 16)
            g = all_ref[rb * 24 + lb].astype(F32)
            w = wt_ref[rows, at].astype(F32)
            final_ref[rows, at] = g * scale + shift * tot[rb]
            s0 = s0 + jnp.sum(w * tot[rb], axis=0, keepdims=True)
            s1 = s1 + jnp.sum(w * g, axis=0, keepdims=True)
        modg_ref[0:1, at] = s0
        modg_ref[1:2, at] = s1
    for rb in range(3):
        for lb in range(4):
            icg_ref[rb * 16 : (rb + 1) * 16, lb * 128 : (lb + 1) * 128] = all_ref[96 + rb * 4 + lb].astype(F32)
    for lb in range(4):
        bias_ref[:, lb * 128 : (lb + 1) * 128] = all_ref[96 + 12 + lb].astype(F32)[0:1]


def k_weight_out(keep_ref, other_ref, wt_ref, mod_ref, out_ref, wt_near_ref, mod_near_ref):
    wt_near_ref[...] = wt_ref[...]
    mod_near_ref[...] = mod_ref[...]
    core = lax.axis_index("tm") % 2
    mine, other = keep_ref[...], other_ref[...]
    halves = [jnp.where(core == 0, mine, other), jnp.where(core == 0, other, mine)]
    for j in range(12):
        rows = halves[j // 6][(j % 6) * 4 : (j % 6) * 4 + 4]
        out_ref[j // 4, :, (j % 4) * 128 : (j % 4 + 1) * 128] = rows


def call(fn, outs, specs, scratch=(), mib=40, est=None, name=None):
    return pl.pallas_call(
        fn,
        out_shape=outs,
        in_specs=specs,
        out_specs=jax.tree.map(lambda _: VMEM, outs),
        scratch_shapes=list(scratch),
        compiler_params=params(mib),
        cost_estimate=est,
        name=name,
    )


def sds(shape, dtype):
    return jax.ShapeDtypeStruct(shape, dtype)


def pinned(*arrays):
    return [pltpu.with_memory_space_constraint(a, pltpu.HBM) for a in arrays]


def shifted(block, distance):
    n = lax.axis_size("tm")
    route = [(i - distance, i) for i in range(n) if 0 <= i - distance < n]
    return lax.ppermute(block, "tm", route)


def swapped(block):
    return lax.ppermute(block, "tm", [(i, i ^ 1) for i in range(lax.axis_size("tm"))])


def exchange(block, axes):
    return lax.all_to_all(block, axes, split_axis=0, concat_axis=0, tiled=True)


def local(latents, hidden, grad_out, conv_in_w, conv_in_b, conv_w, final_w, modulation, clip_start):
    win = conv_in_w.transpose(0, 2, 1)
    wt = final_w.T
    bias = conv_in_b.reshape(1, C)
    lat_prev = shifted(latents, 1)
    unit = 2 * C * C * PX
    grad_sent = grad_out[:2]
    grad_next = shifted(grad_sent, -1)
    acc = call(
        k_back, sds((SLAB, C, PX), F32), [PIN, PIN, VMEM, PIN],
        [
            pltpu.SMEM((FRAMES,), jnp.int32), pltpu.VMEM((TAPS, C, C), BF), pltpu.VMEM((SLAB, C, PX), BF),
            pltpu.SemaphoreType.DMA((4,)),
        ],
        mib=16, est=cost(1 << 10, 1 << 10), name="back",
    )(*pinned(clip_start, conv_w), grad_sent, *pinned(grad_out))
    act01, part, halo, icg_part, wcol = call(
        k_first,
        (
            sds((2, C, PX), BF), sds((SLAB, CL, PX), F32), sds((2, CL, PX), BF), sds((E, C), F32), sds((C, E), BF),
        ),
        [SMEM] + [VMEM] * 5,
        [
            pltpu.VMEM((2 * SLAB, CL, PX), BF), pltpu.VMEM((2, E, PX), BF), pltpu.VMEM((E, C), BF),
            pltpu.VMEM((SLAB + 2, CL, PX), F32),
        ],
        mib=16, est=cost(2 * unit, 5 << 20), name="first",
    )(clip_start, lat_prev, latents, win, bias, acc)
    halo_recv = shifted(halo, -1)
    act, slope = call(
        k_rest, (sds((SLAB + 2, C, PX), BF), sds((2, C, PX), F32)), [SMEM] + [VMEM] * 4,
        [pltpu.VMEM((2 * SLAB, CL, PX), BF), pltpu.VMEM((SLAB, E, PX), BF)],
        mib=16, est=cost(2 * unit, 8 << 20), name="rest",
    )(clip_start, lat_prev, latents, wcol, act01)
    keep, send = call(
        k_weight, (sds((32, 2, 48, 128), BF),) * 2, [SMEM] + [VMEM] * 2,
        [pltpu.VMEM((16, 2, 16, TAPS * C), F32)], mib=16, est=cost(50 * unit, 7 << 20), name="weight",
    )(clip_start, grad_out, act)
    piece = sds((CL, PX), BF)
    half = sds((32, 2, 48, 128), BF)
    *tok_parts, icg_blocks, send = pl.pallas_call(
        k_second,
        out_shape=(piece,) * 4 + (sds((16, 16, 128), BF), half),
        in_specs=[SMEM] + [VMEM] * 9 + [HERE],
        out_specs=(VMEM,) * 5 + (HERE,),
        scratch_shapes=[
            pltpu.VMEM((2, C, PX), F32), pltpu.VMEM((2, E, PX), BF), pltpu.VMEM((TAPS * CL, C), BF),
            pltpu.VMEM((SLAB, CL, PX), F32), pltpu.VMEM((E, C), F32), pltpu.VMEM((SLAB * CL, PX), BF),
        ],
        input_output_aliases={10: 5},
        compiler_params=params(16),
        cost_estimate=cost(6 * unit, 8 << 20),
        name="second",
    )(clip_start, grad_next, latents, win, conv_w, acc, slope, part, halo_recv, icg_part, send)
    toks = [tok_parts[0]] + [
        lax.ppermute(tok_parts[k], "seq", [(i, (i + k) % 4) for i in range(4)]) for k in range(1, 4)
    ]
    other = swapped(send)
    normed = call(
        k_prep, sds((NTOK, D), BF), [VMEM, HERE], mib=16, est=cost(50 * unit, 6 << 20), name="prep"
    )(hidden, icg_blocks)
    pack, tok = pl.pallas_call(
        k_grad,
        out_shape=(sds((128, 40, 128), BF), pltpu.HBM((E, NTOK), BF)),
        in_specs=[VMEM] * 8,
        out_specs=(VMEM, PIN),
        scratch_shapes=[
            pltpu.VMEM((E, NTOK), BF), pltpu.VMEM((4, CL, PX), BF), pltpu.VMEM((E, NTOK), BF),
            pltpu.SemaphoreType.DMA,
        ],
        compiler_params=params(16),
        cost_estimate=cost(2 * NTOK * D * E, 5 << 20),
        name="grad",
    )(*toks, normed, icg_blocks, keep.reshape(64, 48, 128), other.reshape(64, 48, 128))
    recv = exchange(pack, BOTH)
    hidden_grad = pl.pallas_call(
        k_hidden,
        grid=(4,),
        out_shape=sds((NTOK, D), BF),
        in_specs=[
            pl.BlockSpec((E, 128), lambda i: (0, i)),
            pl.BlockSpec((128, D), lambda i: (i, 0)),
            pl.BlockSpec((E, D), lambda i: (0, 0)),
            pl.BlockSpec((2, D), lambda i: (0, 0)),
        ],
        out_specs=pl.BlockSpec((128, D), lambda i: (i, 0)),
        compiler_params=params(16),
        cost_estimate=cost(2 * NTOK * D * E, 6 << 20),
        name="hidden",
    )(*pinned(tok, hidden, wt, modulation))
    copies, own, away = pl.pallas_call(
        k_sum,
        out_shape=(pltpu.HBM((128, 16, 128), BF), sds((24, 128), F32), pltpu.HBM((24, 128), F32)),
        in_specs=[VMEM],
        out_specs=(PIN, VMEM, PIN),
        scratch_shapes=[
            pltpu.VMEM((128, 16, 128), BF), pltpu.VMEM((24, 128), F32), pltpu.SemaphoreType.DMA((2,)),
        ],
        compiler_params=params(16),
        cost_estimate=cost(1 << 20, 2 << 20),
        name="sum",
    )(recv)
    everything = exchange(copies, BOTH)
    weight_grad, wt_near, mod_near = call(
        k_weight_out, (sds((TAPS, 4, C), F32), sds((E, D), BF), sds((2, D), F32)), [VMEM] * 4,
        mib=16, est=cost(1 << 12, 1 << 16), name="weight_out",
    )(own, swapped(away), wt, modulation)
    final_t, mod_grad, icg, bias_grad = call(
        k_last, (sds((E, D), F32), sds((2, D), F32), sds((TAPS * CL, C), F32), sds((1, C), F32)), [VMEM] * 3,
        mib=16, est=cost(1 << 20, 2 << 20), name="last",
    )(everything, wt_near, mod_near)
    return (
        hidden_grad,
        weight_grad.transpose(1, 0, 2),
        icg.reshape(TAPS, CL, C).transpose(0, 2, 1),
        bias_grad.reshape(C),
        final_t.T,
        mod_grad,
    )


def solution(mesh):
    return jax.shard_map(
        local,
        mesh=mesh,
        in_specs=(
            P("tm", None, "seq"),
            P(("tm", "seq"), None),
            P("tm", None, "seq"),
            P(), P(), P(), P(), P(), P(),
        ),
        out_specs=(P(("tm", "seq"), None), P(("tm", "seq"), None, None), P(), P(), P(), P()),
        check_vma=False,
    )
```
